32 devices in a mesh: dim: 16 (over z, y, core), row: 2 (over x).
Axes of the slice: x: 2, y: 2, z: 4, core: 2. Of those that a mesh axis runs over, the one named last changes fastest.
Arguments:
- vectors: bfloat16 [3328, 4096], P('row', 'dim'), may hold values from -6 to 6
- blocks: float32 [5, 4096, 128], P(None, 'dim'), may hold values from -0.5 to 0.5
- angles: float32 [5, 4096], P(None, 'dim'), may hold values from -3.140625 to 3.140625
- codes: int32 [3328, 4096], P('row', 'dim'), may hold values from 0 to 15
- scale_index: int32 [3328], P('row'), may hold values from 0 to 15
- scale_table: float32 [16], replicated, may hold values from 0.05 to 0.3
- block_state: float32 [5, 4096, 128], P(None, 'dim'), may hold values from 0.1 to 2
- angle_state: float32 [5, 4096], P(None, 'dim'), may hold values from 0.1 to 2
Outputs:
- step_blocks: float32 [5, 4096, 128], P(None, 'dim')
- new_block_state: float32 [5, 4096, 128], P(None, 'dim')
- step_angles: float32 [5, 4096], P(None, 'dim')
- new_angle_state: float32 [5, 4096], P(None, 'dim')
The draws below stay inside these ranges and needn't reach their ends.
All inputs are finite; a program needn't handle non-finite values.
Results may differ from the reference program's by a relative error of at most 0.015.
The reference program's roundings to bfloat16 on the way count: a program that leaves them out, or rounds other values in their place, can miss the bound.
Values may be sent and summed in bfloat16 or wider, within the bound.
No kernel may reach another device: no remote copies, remote signals or barrier semaphores. Data moves between devices by JAX's collectives and lax.ppermute only.
A program may use at most 128 MiB of HBM per device.

```python
import math
import jax
import jax.numpy as jnp
from jax import lax

D = 4096
BLOCK = 128
S = 5
LEVELS = 16
ROWS_DEV = 1664
ROWS = 3328
N_ROW = 2


def with_ends(entries, key, least, largest):
    index_at = [jax.random.randint(jax.random.fold_in(key, axis), (), 0, length) for axis, length in enumerate(entries.shape)]
    longest = entries.shape.index(max(entries.shape))
    next_to = index_at[:longest] + [(index_at[longest] + 1) % entries.shape[longest]] + index_at[longest + 1:]
    return entries.at[tuple(index_at)].set(least).at[tuple(next_to)].set(largest)


def block_levels(rng, shape, shards, smallest, top_value):
    level = 1.0
    for dim, shards_of in shards:
        heights = jax.random.uniform(jax.random.fold_in(jax.random.fold_in(rng, 6), dim), (shards_of,), jnp.float32, smallest / len(shards), top_value / len(shards))
        level = level * jnp.repeat(jnp.exp(heights), shape[dim] // shards_of).reshape((-1,) + (1,) * (len(shape) - 1 - dim))
    return level


def gaussian(own_key, shape, width, reach, cuts=(), kind=jnp.bfloat16):
    values = jax.random.normal(own_key, shape, jnp.float32) * width
    if len(cuts) > 0:
        values = block_levels(own_key, shape, cuts, -0.22, 0.18) * values
    return jnp.clip(values, min=-reach, max=reach).astype(kind)


def setup_inputs(seed: int = 0) -> dict:
    key_list = jax.random.split(jax.random.key(seed), 9)
    vectors = gaussian(key_list[0], (ROWS, D), 1.0, 6.0, ((0, 2), (1, 16)))
    blocks = gaussian(key_list[1], (S, D, BLOCK), BLOCK ** -0.5, 0.5, ((1, 16),), jnp.float32)
    angles = jnp.clip(jax.random.uniform(key_list[2], (S, D), jnp.float32, -3.140625, 3.140625), -3.140625, 3.140625)
    codes = with_ends(jax.random.randint(key_list[3], (ROWS, D), 0, 16), jax.random.fold_in(key_list[3], 1), 0, 15).astype(jnp.int32)
    scale_index = with_ends(jax.random.randint(key_list[4], (ROWS,), 0, LEVELS), jax.random.fold_in(key_list[4], 1), 0, LEVELS - 1).astype(jnp.int32)
    scale_table = jnp.clip(jnp.exp(jax.random.uniform(key_list[5], (LEVELS,), jnp.float32, math.log(0.05), math.log(0.3))), 0.05, 0.3)
    block_state = jnp.clip(jnp.exp(math.log(2.0) - 2.9957323 * jax.random.uniform(key_list[6], (S, D, BLOCK), jnp.float32) ** block_levels(key_list[6], (S, D, BLOCK), ((1, 16),), -0.2, 0.2)), 0.1, 2.0)
    angle_state = jnp.clip(jnp.exp(math.log(2.0) - 2.9957323 * jax.random.uniform(key_list[7], (S, D), jnp.float32) ** block_levels(key_list[7], (S, D), ((1, 16),), -0.2, 0.2)), 0.1, 2.0)
    return {"vectors": vectors, "blocks": blocks, "angles": angles, "codes": codes, "scale_index": scale_index, "scale_table": scale_table, "block_state": block_state, "angle_state": angle_state}


def swap_halves(tensor, section):
    layout = tensor.shape
    stride = 2 ** section
    number = layout[-2]
    parted = tensor.reshape(layout[:-2] + (number // (2 * stride), 2, stride, layout[-1]))
    return jnp.flip(parted, axis=-3).reshape(layout)

def reference(vectors, blocks, angles, codes, scale_index, scale_table, block_state, angle_state):
    block_count = D // BLOCK
    weights = blocks.astype(jnp.bfloat16).reshape(S, block_count, BLOCK, BLOCK)
    thetas = angles.reshape(S, block_count, BLOCK)
    cosines = jnp.cos(thetas)
    sines = jnp.sin(thetas)
    block_ids = jnp.arange(block_count, dtype=jnp.int32)
    all_signs = [jnp.where(block_ids // 2 ** section % 2 == 0, 1.0, -1.0).astype(jnp.float32)[:, None] for section in range(S)]

    def group(carry, inputs):
        rows_x, rows_codes, rows_index = inputs
        current = rows_x.reshape(ROWS_DEV, block_count, BLOCK)
        saved = []
        for section in range(S):
            mixed = jnp.einsum('rnb,nbc->rnc', current.astype(jnp.float32), weights[section].astype(jnp.float32)).astype(jnp.bfloat16)
            partner = swap_halves(mixed, section)
            result = (cosines[section] * mixed.astype(jnp.float32) + all_signs[section] * sines[section] * partner.astype(jnp.float32)).astype(jnp.bfloat16)
            saved.append((current, mixed, partner))
            current = result
        factor = scale_table[rows_index]
        recon = factor[:, None] * (rows_codes.astype(jnp.float32) - 7.5)
        cotangent = ((current.reshape(ROWS_DEV, D).astype(jnp.float32) - recon) / math.sqrt(ROWS)).astype(jnp.bfloat16).reshape(ROWS_DEV, block_count, BLOCK)
        block_grads = [None] * S
        angle_grads = [None] * S
        for section in reversed(range(S)):
            source, mixed, partner = saved[section]
            signs = all_signs[section]
            upstream = cotangent.astype(jnp.float32)
            angle_grads[section] = lax.optimization_barrier(jnp.sum(upstream * (-sines[section] * mixed.astype(jnp.float32) + signs * cosines[section] * partner.astype(jnp.float32)), axis=0))
            outgoing = (signs * sines[section] * upstream).astype(jnp.bfloat16)
            incoming = swap_halves(outgoing, section)
            direction = (cosines[section] * upstream + incoming.astype(jnp.float32)).astype(jnp.bfloat16)
            block_grads[section] = jnp.einsum('rnb,rnc->nbc', source.astype(jnp.float32), direction.astype(jnp.float32))
            if section > 0:
                cotangent = jnp.einsum('rnc,nbc->rnb', direction.astype(jnp.float32), weights[section].astype(jnp.float32)).astype(jnp.bfloat16)
        return ((carry[0] + jnp.stack(block_grads), carry[1] + jnp.stack(angle_grads)), None)
    start = (jnp.zeros((S, block_count, BLOCK, BLOCK), jnp.float32), jnp.zeros((S, block_count, BLOCK), jnp.float32))
    sliced = (vectors.reshape(N_ROW, ROWS_DEV, D), codes.reshape(N_ROW, ROWS_DEV, D), scale_index.reshape(N_ROW, ROWS_DEV))
    totals, _ = lax.scan(group, start, sliced)
    grad_blocks = totals[0].reshape(S, D, BLOCK)
    grad_angles = totals[1].reshape(S, D)
    new_block_state = 0.9 * block_state + 0.1 * grad_blocks * grad_blocks
    step_blocks = grad_blocks / jnp.sqrt(new_block_state)
    new_angle_state = 0.9 * angle_state + 0.1 * grad_angles * grad_angles
    step_angles = grad_angles / jnp.sqrt(new_angle_state)
    return (step_blocks, new_block_state, step_angles, new_angle_state)
```

```python
import math

import jax
import jax.numpy as jnp
from jax import lax
from jax.experimental import pallas as pl
from jax.experimental.pallas import tpu as pltpu
from jax.sharding import PartitionSpec as P

BLOCK = 128
GROUP = 4
EXTRA = 8
TRIG = 16
BF = jnp.bfloat16
F32 = jnp.float32


def swapped(value, axis, mask):
    pairs = [(source, source ^ mask) for source in range(lax.axis_size(axis))]
    return lax.ppermute(value, axis, pairs)


def dot(a, b):
    return lax.dot_general(a, b, (((1,), (0,)), ((), ())), preferred_element_type=F32)


def dot_t(a, b):
    return lax.dot_general(a, b, (((1,), (1,)), ((), ())), preferred_element_type=F32)


def t_dot(a, b):
    return lax.dot_general(a, b, (((0,), (0,)), ((), ())), preferred_element_type=F32)


def tile_of(rows):
    best = 16
    for size in range(16, 257, 16):
        if rows % size == 0:
            best = size
    return best


def call(body, outs, args, specs=None, scratch=(), flops=0):
    whole = [pl.BlockSpec(a.shape, lambda i, n=a.ndim: (0,) * n) for a in args]
    for at, spec in (specs or {}).items():
        whole[at] = spec
    moved = sum(math.prod(a.shape) * a.dtype.itemsize for a in args) + sum(
        math.prod(o.shape) * o.dtype.itemsize for o in outs
    )
    return list(pl.pallas_call(
        body,
        grid=(1,),
        in_specs=whole,
        out_specs=[pl.BlockSpec(o.shape, lambda i, n=len(o.shape): (0,) * n) for o in outs],
        out_shape=outs,
        scratch_shapes=list(scratch),
        compiler_params=pltpu.CompilerParams(vmem_limit_bytes=40 * 2**20),
        cost_estimate=pl.CostEstimate(flops=flops, bytes_accessed=moved, transcendentals=0),
    )(*args))


def shape(dims, dtype=BF):
    return jax.ShapeDtypeStruct(dims, dtype)


SMEM = pl.BlockSpec(memory_space=pltpu.SMEM)


def split3(x):
    hi = x.astype(BF)
    rest = x - hi.astype(F32)
    mid = rest.astype(BF)
    low = (rest - mid.astype(F32)).astype(BF)
    return [hi, mid, low]


def section_spec(s, width, columns):
    return pl.BlockSpec((1, width, columns), lambda i: (s, 0, 0))


def local(vectors, blocks, angles, codes, scale_index, scale_table, block_state, angle_state):
    rows, width = vectors.shape
    sections = blocks.shape[0]
    nb = width // BLOCK
    local_bits = nb.bit_length() - 1
    shift = sections - 2 - local_bits
    quarter = rows // GROUP
    nrow = lax.axis_size("row")
    inv = 1.0 / math.sqrt(rows * nrow)
    tile = tile_of(quarter)
    device = lax.axis_index("dim")
    place = ((device >> shift) % GROUP).astype(jnp.int32)
    place_arr = place.reshape(1)
    last, third = sections - 1, sections - 2

    ids = device * nb + jnp.arange(width, dtype=jnp.int32) // BLOCK
    bits = (ids[None, :] >> jnp.arange(sections, dtype=jnp.int32)[:, None]) & 1
    signs = jnp.where(bits == 0, 1.0, -1.0).astype(F32)
    trig = jnp.concatenate([jnp.cos(angles), signs * jnp.sin(angles)], axis=0)

    def col(c):
        return slice(c * BLOCK, (c + 1) * BLOCK)

    def cs(ref, s, c):
        return ref[s : s + 1, col(c)], ref[sections + s : sections + s + 1, col(c)]

    def first_body(u_ref, w_ref, trig_ref, *outs):
        saved, sent = outs[:-1], outs[-1]
        weights = [
            [w_ref[s, col(c), :].astype(BF) for c in range(nb)] for s in range(local_bits + 1)
        ]
        for r in range(0, rows, tile):
            at = pl.ds(r, tile)
            u = [u_ref[at, col(c)] for c in range(nb)]
            for s in range(local_bits):
                v = [dot(u[c], weights[s][c]).astype(BF) for c in range(nb)]
                for c in range(nb):
                    saved[2 * s][at, col(c)] = v[c]
                for c in range(nb):
                    co, si = cs(trig_ref, s, c)
                    u[c] = (co * v[c].astype(F32) + si * v[c ^ (1 << s)].astype(F32)).astype(BF)
                    saved[2 * s + 1][at, col(c)] = u[c]
            for c in range(nb):
                sent[at, col(c)] = dot(u[c], weights[local_bits][c]).astype(BF)

    firsts = call(
        first_body,
        [shape((rows, width))] * (2 * local_bits + 1),
        [vectors, blocks, trig],
        flops=rows * width * BLOCK * 4,
    )
    v0s, u0s = firsts[:-1:2], [vectors] + list(firsts[1:-1:2])
    v_first = firsts[-1]

    def pack_body(place_ref, index_ref, table_ref, codes_ref, w_ref, trig_ref, *outs):
        z = place_ref[0]
        w = w_ref[0].astype(BF)
        lines = []
        for s in (third, last):
            lines += split3(trig_ref[s : s + 1, :]) + split3(
                trig_ref[sections + s : sections + s + 1, :]
            )
        lines.append(jnp.zeros((TRIG - len(lines), width), BF))
        for m in range(GROUP):
            q = jnp.bitwise_xor(z, m)
            start = pl.multiple_of(q * quarter, 16)
            for r in range(0, quarter, tile):
                outs[m][r : r + tile, :] = (
                    codes_ref[pl.ds(start + r, tile), :].astype(F32).astype(BF)
                )
            for c in range(nb):
                outs[m][quarter : quarter + BLOCK, col(c)] = w[col(c), :]
            outs[m][quarter + BLOCK :, :] = jnp.concatenate(
                [x.astype(F32) for x in lines], axis=0
            ).astype(BF)
        levels = table_ref.shape[0]
        index = index_ref[pl.ds(z, 1), :]
        onehot = jnp.where(
            lax.broadcasted_iota(jnp.int32, (levels, quarter), 0) == index, 1.0, 0.0
        ).astype(BF)
        total = jnp.zeros((quarter, BLOCK), F32)
        for part in split3(jnp.broadcast_to(table_ref[...], (levels, BLOCK))):
            total = total + t_dot(onehot, part)
        outs[GROUP][...] = total

    packed = call(
        pack_body,
        [shape((quarter + BLOCK + TRIG, width))] * GROUP + [shape((quarter, BLOCK), F32)],
        [
            place_arr,
            scale_index.reshape(GROUP, quarter),
            scale_table.reshape(-1, 1),
            codes,
            blocks,
            trig,
        ],
        specs={0: SMEM, 4: section_spec(last, width, BLOCK)},
        flops=quarter * BLOCK * 100,
    )
    factor = packed[GROUP]
    packs = [packed[0]] + [swapped(packed[m], "dim", m << shift) for m in range(1, GROUP)]

    chunks = list(range(nb))

    def column(c):
        return pl.BlockSpec((rows, BLOCK), lambda i: (0, c))

    def wspec(s, c):
        return pl.BlockSpec((1, BLOCK, BLOCK), lambda i: (s, c, 0))

    product = rows * BLOCK * BLOCK * 2
    other_first = swapped(v_first, "dim", 1)
    saves = {c: {} for c in chunks}

    def middle(c, s, v, other, wide, quarters):
        def body(place_ref, v_ref, o_ref, w_ref, trig_ref, u_out, *outs):
            co, si = cs(trig_ref, s, c)
            w = w_ref[0].astype(BF)
            z = place_ref[0]

            def step(rd, write):
                u = (co * v_ref[rd, :].astype(F32) + si * o_ref[rd, :].astype(F32)).astype(BF)
                u_out[rd, :] = u
                write(dot(u, w).astype(BF))

            if not quarters:
                for r in range(0, rows, tile):

                    def write(x, r=r):
                        outs[0][r : r + tile, :] = x

                    step(pl.ds(r, tile), write)
            else:
                for m in range(GROUP):
                    start = pl.multiple_of(jnp.bitwise_xor(z, m) * quarter, 16)
                    for r in range(0, quarter, tile):

                        def write(x, r=r, m=m):
                            outs[m][r : r + tile, :] = x

                        step(pl.ds(start + r, tile), write)

        outs = [shape((rows, BLOCK))]
        outs += [shape((quarter, BLOCK))] * GROUP if quarters else [shape((rows, BLOCK))]
        specs = {0: SMEM, 3: wspec(s + 1, c)}
        if wide:
            specs.update({1: column(c), 2: column(c)})
        return call(
            body, outs, [place_arr, v, other, blocks, trig], specs=specs, flops=product
        )

    middles = list(range(local_bits, third))
    state = {c: (v_first, other_first) for c in chunks}
    for s in middles:
        for c in chunks:
            v, other = state[c]
            out = middle(c, s, v, other, s == local_bits, s + 1 == third)
            saves[c][s] = (v, other, out[0])
            if s + 1 < third:
                state[c] = (out[1], swapped(out[1], "dim", 1 << (s + 1 - local_bits)))
            else:
                state[c] = [out[1]] + [
                    swapped(out[1 + m], "dim", m << shift) for m in range(1, GROUP)
                ]

    def group_stage(c):
        def body(*refs):
            a_refs, p_refs = refs[:GROUP], refs[GROUP : 2 * GROUP]
            f_ref = refs[2 * GROUP]
            outs, grad = refs[2 * GROUP + 1 : 3 * GROUP + 1], refs[3 * GROUP + 1]
            coef, w = [], []
            for m in range(GROUP):
                t = p_refs[m][quarter + BLOCK :, :].astype(F32)
                coef.append([t[3 * k : 3 * k + 1] + t[3 * k + 1 : 3 * k + 2] + t[3 * k + 2 : 3 * k + 3] for k in range(4)])
                w.append(p_refs[m][quarter : quarter + BLOCK, :])
            gw = [jnp.zeros((BLOCK, BLOCK), F32)] * GROUP
            ga = [[jnp.zeros((1, BLOCK), F32)] * GROUP for _ in range(2)]
            every = range(GROUP)
            for r in range(0, quarter, tile):
                at = pl.ds(r, tile)
                a = [a_refs[m][at, :].astype(F32) for m in every]
                u = [(coef[m][0] * a[m] + coef[m][1] * a[m ^ 1]).astype(BF) for m in every]
                v = [dot(u[m], w[m]).astype(BF).astype(F32) for m in every]
                f = f_ref[at, :]
                g = []
                for m in every:
                    end = (coef[m][2] * v[m] + coef[m][3] * v[m ^ 2]).astype(BF).astype(F32)
                    recon = f * (p_refs[m][at, :].astype(F32) - 7.5)
                    g.append(((end - recon) * inv).astype(BF).astype(F32))
                for m in every:
                    ga[0][m] = ga[0][m] + jnp.sum(
                        g[m] * (coef[m][2] * v[m ^ 2] - coef[m][3] * v[m]), axis=0, keepdims=True
                    )
                q = [(coef[m][3] * g[m]).astype(BF).astype(F32) for m in every]
                dv = [(coef[m][2] * g[m] + q[m ^ 2]).astype(BF) for m in every]
                g = []
                for m in every:
                    gw[m] = gw[m] + t_dot(u[m], dv[m])
                    g.append(dot_t(dv[m], w[m]).astype(BF).astype(F32))
                for m in every:
                    ga[1][m] = ga[1][m] + jnp.sum(
                        g[m] * (coef[m][0] * a[m ^ 1] - coef[m][1] * a[m]), axis=0, keepdims=True
                    )
                q = [(coef[m][1] * g[m]).astype(BF).astype(F32) for m in every]
                for m in every:
                    outs[m][at, :] = (coef[m][0] * g[m] + q[m ^ 1]).astype(BF)
            for m in every:
                grad[m, :BLOCK, :] = gw[m]
                grad[m, BLOCK:, :] = jnp.concatenate(
                    [ga[0][m], ga[1][m], jnp.zeros((EXTRA - 2, BLOCK), F32)], axis=0
                )

        high = quarter + BLOCK + TRIG
        specs = {
            GROUP + m: pl.BlockSpec((high, BLOCK), lambda i: (0, c)) for m in range(GROUP)
        }
        return call(
            body,
            [shape((quarter, BLOCK))] * GROUP + [shape((GROUP, BLOCK + EXTRA, BLOCK), F32)],
            state[c] + packs + [factor],
            specs=specs,
            flops=3 * product,
        )

    back, partial = {}, {}
    for c in chunks:
        out = group_stage(c)
        partial[c] = out[GROUP]
        back[c] = [out[0]] + [swapped(out[m], "dim", m << shift) for m in range(1, GROUP)]

    def write_grad(out, gw, ga):
        out[:BLOCK, :] = gw
        out[BLOCK:, :] = jnp.concatenate([ga, jnp.zeros((EXTRA - 1, BLOCK), F32)], axis=0)

    grad_shape = shape((BLOCK + EXTRA, BLOCK), F32)

    def back_quarters(c, s):
        v, other, u = saves[c][s - 1]
        wide = s - 1 == local_bits

        def body(place_ref, *refs):
            d_refs = refs[:GROUP]
            u_ref, v_ref, o_ref, w_ref, trig_ref, g_out, q_out, grad = refs[GROUP:]
            w = w_ref[0].astype(BF)
            co, si = cs(trig_ref, s - 1, c)
            z = place_ref[0]
            gw = jnp.zeros((BLOCK, BLOCK), F32)
            ga = jnp.zeros((1, BLOCK), F32)
            for m in range(GROUP):
                start = pl.multiple_of(jnp.bitwise_xor(z, m) * quarter, 16)
                for r in range(0, quarter, tile):
                    d = d_refs[m][r : r + tile, :]
                    at = pl.ds(start + r, tile)
                    gw = gw + t_dot(u_ref[at, :], d)
                    g16 = dot_t(d, w).astype(BF)
                    g = g16.astype(F32)
                    g_out[at, :] = g16
                    ga = ga + jnp.sum(
                        g * (co * o_ref[at, :].astype(F32) - si * v_ref[at, :].astype(F32)),
                        axis=0,
                        keepdims=True,
                    )
                    q_out[at, :] = (si * g).astype(BF)
            write_grad(grad, gw, ga)

        specs = {0: SMEM, GROUP + 4: wspec(s, c)}
        if wide:
            specs.update({GROUP + 2: column(c), GROUP + 3: column(c)})
        return call(
            body,
            [shape((rows, BLOCK)), shape((rows, BLOCK)), grad_shape],
            [place_arr] + back[c] + [u, v, other, blocks, trig],
            specs=specs,
            flops=2 * product,
        )

    def back_middle(c, s, g, incoming):
        v, other, u = saves[c][s - 1]
        wide = s - 1 == local_bits

        def body(g_ref, i_ref, u_ref, v_ref, o_ref, w_ref, trig_ref, g_out, q_out, grad):
            w = w_ref[0].astype(BF)
            here = cs(trig_ref, s, c)[0]
            co, si = cs(trig_ref, s - 1, c)
            gw = jnp.zeros((BLOCK, BLOCK), F32)
            ga = jnp.zeros((1, BLOCK), F32)
            for r in range(0, rows, tile):
                at = pl.ds(r, tile)
                d = (here * g_ref[at, :].astype(F32) + i_ref[at, :].astype(F32)).astype(BF)
                gw = gw + t_dot(u_ref[at, :], d)
                g16 = dot_t(d, w).astype(BF)
                gf = g16.astype(F32)
                g_out[at, :] = g16
                ga = ga + jnp.sum(
                    gf * (co * o_ref[at, :].astype(F32) - si * v_ref[at, :].astype(F32)),
                    axis=0,
                    keepdims=True,
                )
                q_out[at, :] = (si * gf).astype(BF)
            write_grad(grad, gw, ga)

        specs = {5: wspec(s, c)}
        if wide:
            specs.update({3: column(c), 4: column(c)})
        return call(
            body,
            [shape((rows, BLOCK)), shape((rows, BLOCK)), grad_shape],
            [g, incoming, u, v, other, blocks, trig],
            specs=specs,
            flops=2 * product,
        )

    grads = {c: {} for c in chunks}
    flow = {}
    for c in chunks:
        g, q, grads[c][third] = back_quarters(c, third)
        flow[c] = (g, swapped(q, "dim", 1 << (third - 1 - local_bits)))
    for s in reversed(middles[1:]):
        for c in chunks:
            g, q, grads[c][s] = back_middle(c, s, *flow[c])
            flow[c] = (g, swapped(q, "dim", 1 << (s - 1 - local_bits)))

    low = local_bits + 1

    def end_body(*refs):
        g_refs, i_refs = refs[:nb], refs[nb : 2 * nb]
        u_refs = refs[2 * nb : 2 * nb + low]
        v_refs = refs[2 * nb + low : 2 * nb + low + local_bits]
        w_ref, trig_ref, grad = refs[2 * nb + low + local_bits :]
        gw = [[jnp.zeros((BLOCK, BLOCK), F32)] * nb for _ in range(low)]
        ga = [[jnp.zeros((1, BLOCK), F32)] * nb for _ in range(low)]
        w = [[w_ref[s, col(c), :].astype(BF) for c in range(nb)] for s in range(low)]
        for r in range(0, rows, tile):
            at = pl.ds(r, tile)
            d = []
            for c in range(nb):
                here = cs(trig_ref, local_bits, c)[0]
                d.append(
                    (here * g_refs[c][at, :].astype(F32) + i_refs[c][at, :].astype(F32)).astype(BF)
                )
            for s in reversed(range(low)):
                for c in range(nb):
                    gw[s][c] = gw[s][c] + t_dot(u_refs[s][at, col(c)], d[c])
                if s == 0:
                    break
                g = [dot_t(d[c], w[s][c]).astype(BF).astype(F32) for c in range(nb)]
                t = s - 1
                v = [v_refs[t][at, col(c)].astype(F32) for c in range(nb)]
                q = []
                for c in range(nb):
                    co, si = cs(trig_ref, t, c)
                    ga[t][c] = ga[t][c] + jnp.sum(
                        g[c] * (co * v[c ^ (1 << t)] - si * v[c]), axis=0, keepdims=True
                    )
                    q.append((si * g[c]).astype(BF).astype(F32))
                d = [
                    (cs(trig_ref, t, c)[0] * g[c] + q[c ^ (1 << t)]).astype(BF) for c in range(nb)
                ]
        for s in range(low):
            for c in range(nb):
                write_grad(grad.at[s * nb + c], gw[s][c], ga[s][c])

    (ends,) = call(
        end_body,
        [shape((low * nb, BLOCK + EXTRA, BLOCK), F32)],
        [flow[c][0] for c in chunks]
        + [flow[c][1] for c in chunks]
        + u0s
        + v0s
        + [blocks, trig],
        flops=6 * product,
    )

    stacked = jnp.stack([partial[c] for c in chunks], axis=1)
    arrived = [swapped(stacked[m], "dim", m << shift) for m in range(1, GROUP)]
    high = sections - low
    uppers = [(s, c) for s in range(low, third + 1) for c in chunks]

    def upper_body(*refs):
        own, others, rest, out = refs[0], refs[1:GROUP], refs[GROUP:-1], refs[-1]
        for k in range(len(uppers)):
            out[k] = rest[k][...]
        for c in range(nb):
            total = own[0, c]
            for other in others:
                total = total + other[c]
            out[len(uppers) + c] = total

    (upper,) = call(
        upper_body,
        [shape((high * nb, BLOCK + EXTRA, BLOCK), F32)],
        [stacked] + arrived + [grads[c][s] for s, c in uppers],
    )
    if nrow == 2:
        pairs = [(ends, swapped(ends, "row", 1)), (upper, swapped(upper, "row", 1))]
    else:
        pairs = [lax.psum(ends, "row"), lax.psum(upper, "row")]
        pairs = [(p, jnp.zeros_like(p)) for p in pairs]

    def final_body(e0, e1, p0, p1, bs_ref, as_ref, sign_ref, step, new, step_a, new_a):
        def get(s, c):
            k = s * nb + c
            if s < low:
                return e0[k] + e1[k]
            k -= low * nb
            return p0[k] + p1[k]

        for c in range(nb):
            angle = [None] * sections
            for s in range(sections):
                total = get(s, c)
                g = total[:BLOCK, :]
                state_new = 0.9 * bs_ref[s, col(c), :] + 0.1 * g * g
                new[s, col(c), :] = state_new
                step[s, col(c), :] = g * lax.rsqrt(state_new)
                if s == last:
                    angle[last] = total[BLOCK : BLOCK + 1, :]
                    angle[third] = total[BLOCK + 1 : BLOCK + 2, :]
                elif s >= low:
                    angle[s - 1] = total[BLOCK : BLOCK + 1, :]
                elif s < local_bits:
                    angle[s] = total[BLOCK : BLOCK + 1, :]
            g = jnp.concatenate(angle, axis=0) * sign_ref[:, col(c)]
            state_new = 0.9 * as_ref[:, col(c)] + 0.1 * g * g
            new_a[:, col(c)] = state_new
            step_a[:, col(c)] = g * lax.rsqrt(state_new)

    step, new, step_a, new_a = call(
        final_body,
        [shape(block_state.shape, F32)] * 2 + [shape(angle_state.shape, F32)] * 2,
        [*pairs[0], *pairs[1], block_state, angle_state, signs],
    )
    return step, new, step_a, new_a


def solution(mesh):
    in_specs = (
        P("row", "dim"),
        P(None, "dim", None),
        P(None, "dim"),
        P("row", "dim"),
        P("row"),
        P(),
        P(None, "dim", None),
        P(None, "dim"),
    )
    out_specs = (P(None, "dim", None), P(None, "dim", None), P(None, "dim"), P(None, "dim"))
    return jax.shard_map(local, mesh=mesh, in_specs=in_specs, out_specs=out_specs, check_vma=False)
```

```python
import math

import jax
import jax.numpy as jnp
from jax import lax
from jax.experimental import pallas as pl
from jax.experimental.pallas import tpu as pltpu
from jax.sharding import PartitionSpec as P

BLOCK = 128
GROUP = 4
EXTRA = 16
TRIG = 16
OPEN_LIMIT = 60
BF = jnp.bfloat16
F32 = jnp.float32


def swapped(value, axis, mask):
    pairs = [(source, source ^ mask) for source in range(lax.axis_size(axis))]
    return lax.ppermute(value, axis, pairs)


def dot(a, b):
    return lax.dot_general(a, b, (((1,), (0,)), ((), ())), preferred_element_type=F32)


def dot_t(a, b):
    return lax.dot_general(a, b, (((1,), (1,)), ((), ())), preferred_element_type=F32)


def t_dot(a, b):
    return lax.dot_general(a, b, (((0,), (0,)), ((), ())), preferred_element_type=F32)


def tile_of(rows):
    best = 16
    for size in range(16, 257, 16):
        if rows % size == 0:
            best = size
    return best


def call(name, body, outs, args, specs=None, scratch=(), flops=0, out_specs=None, limit=16):
    whole = [pl.BlockSpec(a.shape, lambda i, n=a.ndim: (0,) * n) for a in args]
    for at, spec in (specs or {}).items():
        whole[at] = spec
    moved = sum(math.prod(a.shape) * a.dtype.itemsize for a in args) + sum(
        math.prod(o.shape) * o.dtype.itemsize for o in outs
    )
    return list(
        pl.pallas_call(
            body,
            grid=(1,),
            in_specs=whole,
            out_specs=out_specs
            or [pl.BlockSpec(o.shape, lambda i, n=len(o.shape): (0,) * n) for o in outs],
            out_shape=outs,
            scratch_shapes=list(scratch),
            compiler_params=pltpu.CompilerParams(vmem_limit_bytes=limit * 2**20),
            cost_estimate=pl.CostEstimate(flops=flops*100, bytes_accessed=moved*20, transcendentals=0),
            name=name,
        )(*args)
    )


def shape(dims, dtype=BF):
    return jax.ShapeDtypeStruct(dims, dtype)


SMEM = pl.BlockSpec(memory_space=pltpu.SMEM)
HBM = pl.BlockSpec(memory_space=pltpu.HBM)


def split3(x):
    hi = x.astype(BF)
    rest = x - hi.astype(F32)
    mid = rest.astype(BF)
    low = (rest - mid.astype(F32)).astype(BF)
    return [hi, mid, low]


def stack_lines(lines, height):
    lines = [x.astype(F32) for x in lines]
    lines.append(jnp.zeros((height - len(lines), lines[0].shape[1]), F32))
    return jnp.concatenate(lines, axis=0)


def pack_grad(matrix, lines):
    parts = []
    for line in lines:
        parts += split3(line)[:2]
    return matrix.astype(BF), stack_lines(parts, EXTRA).astype(BF)


def unpack_line(tile, k):
    return tile[2 * k : 2 * k + 1] + tile[2 * k + 1 : 2 * k + 2]


def local(vectors, blocks, angles, codes, scale_index, scale_table, block_state, angle_state):
    rows, width = vectors.shape
    sections = blocks.shape[0]
    nb = width // BLOCK
    chunks = list(range(nb))
    local_bits = nb.bit_length() - 1
    shift = sections - 2 - local_bits
    quarter = rows // GROUP
    nrow = lax.axis_size("row")
    inv = 1.0 / math.sqrt(rows * nrow)
    tile = tile_of(quarter)
    device = lax.axis_index("dim")
    place_arr = ((device >> shift) & (GROUP - 1)).astype(jnp.int32).reshape(1)
    last, third = sections - 1, sections - 2
    product = rows * BLOCK * BLOCK * 2
    grad_rows = BLOCK + EXTRA

    ids = device * nb + jnp.arange(width, dtype=jnp.int32) // BLOCK
    bits = (ids[None, :] >> jnp.arange(sections, dtype=jnp.int32)[:, None]) & 1
    signs = jnp.where(bits == 0, 1.0, -1.0).astype(F32)

    def col(c):
        return slice(c * BLOCK, (c + 1) * BLOCK)

    def cs(ref, s, c):
        return ref[s : s + 1, col(c)], ref[sections + s : sections + s + 1, col(c)]

    def quarter_at(z, m):
        return pl.multiple_of(jnp.bitwise_xor(z, m) * quarter, 16)

    order = [2, 3, 1, 0]
    early = local_bits + 1
    high = quarter + BLOCK + TRIG

    def forward(u, weights, trig_ref):
        steps = []
        for s in range(local_bits):
            v = [dot(u[c], weights[s][c]).astype(BF) for c in chunks]
            steps.append((u, v))
            turned = []
            for c in chunks:
                co, si = cs(trig_ref, s, c)
                turned.append(
                    (co * v[c].astype(F32) + si * v[c ^ (1 << s)].astype(F32)).astype(BF)
                )
            u = turned
        return steps, u

    def open_body(place_ref, u_hbm, w_hbm, codes_hbm, angle_ref, sign_ref, *rest):
        p_hbm, v_hbm, wb_hbm, trig_out = rest[:GROUP], *rest[GROUP : GROUP + 3]
        u_held, w_held, c_held, p_held, v_held, wb_held = rest[GROUP + 3 : GROUP + 9]
        u_sems, w_sems, c_sems, p_sems, v_sems, wb_sem = rest[GROUP + 9 :]
        z = place_ref[0]

        def part(m):
            return pl.ds(m * quarter, quarter)

        w_in = [
            pltpu.make_async_copy(w_hbm.at[s], w_held.at[s], w_sems.at[s]) for s in range(sections)
        ]
        u_in = [
            pltpu.make_async_copy(u_hbm.at[part(m)], u_held.at[part(m)], u_sems.at[m])
            for m in range(GROUP)
        ]
        c_in = [
            pltpu.make_async_copy(
                codes_hbm.at[pl.ds(quarter_at(z, m), quarter)], c_held.at[m], c_sems.at[m]
            )
            for m in range(GROUP)
        ]
        p_out = [pltpu.make_async_copy(p_held.at[m], p_hbm[m], p_sems.at[m]) for m in range(GROUP)]
        v_out = [
            pltpu.make_async_copy(v_held.at[part(m)], v_hbm.at[part(m)], v_sems.at[m])
            for m in range(GROUP)
        ]
        wb_out = pltpu.make_async_copy(wb_held, wb_hbm, wb_sem)
        for copy in w_in[:early] + u_in + w_in[early:]:
            copy.start()
        for m in order:
            c_in[m].start()
        angle = angle_ref[...]
        co, si = jnp.cos(angle), sign_ref[...] * jnp.sin(angle)
        trig_out[...] = jnp.concatenate([co, si], axis=0)
        for s in range(early):
            w_in[s].wait()
            wb_held[s] = w_held[s].astype(BF)
        weights = [[wb_held[s, col(c), :] for c in chunks] for s in range(early)]
        for m in range(GROUP):
            u_in[m].wait()
            for r in range(m * quarter, (m + 1) * quarter, tile):
                at = pl.ds(r, tile)
                u = forward([u_held[at, col(c)] for c in chunks], weights, trig_out)[1]
                for c in chunks:
                    v_held[at, col(c)] = dot(u[c], weights[local_bits][c]).astype(BF)
            v_out[m].start()
        for s in range(early, sections):
            w_in[s].wait()
            wb_held[s] = w_held[s].astype(BF)
        wb_out.start()
        lines = []
        for s in (third, last):
            lines += split3(co[s : s + 1]) + split3(si[s : s + 1])
        lines = stack_lines(lines, TRIG).astype(BF)
        for m in order:
            p_held[m, quarter + BLOCK :, :] = lines
            for c in chunks:
                p_held[m, quarter : quarter + BLOCK, col(c)] = wb_held[last, col(c), :]
            c_in[m].wait()
            for r in range(0, quarter, tile):
                at = pl.ds(r, tile)
                p_held[m, at, :] = c_held[m, at, :].astype(F32).astype(BF)
            p_out[m].start()
        for copy in v_out + [wb_out] + p_out:
            copy.wait()

    opened = call(
        "open",
        open_body,
        [shape((high, width))] * GROUP
        + [shape((rows, width)), shape(blocks.shape), shape((2 * sections, width), F32)],
        [place_arr, vectors, blocks, codes, angles, signs],
        specs={0: SMEM, 1: HBM, 2: HBM, 3: HBM},
        out_specs=[HBM] * (GROUP + 2) + [pl.BlockSpec((2 * sections, width), lambda i: (0, 0))],
        scratch=[
            pltpu.VMEM((rows, width), BF),
            pltpu.VMEM(blocks.shape, F32),
            pltpu.VMEM((GROUP, quarter, width), jnp.int32),
            pltpu.VMEM((GROUP, high, width), BF),
            pltpu.VMEM((rows, width), BF),
            pltpu.VMEM(blocks.shape, BF),
            pltpu.SemaphoreType.DMA((GROUP,)),
            pltpu.SemaphoreType.DMA((sections,)),
            pltpu.SemaphoreType.DMA((GROUP,)),
            pltpu.SemaphoreType.DMA((GROUP,)),
            pltpu.SemaphoreType.DMA((GROUP,)),
            pltpu.SemaphoreType.DMA,
        ],
        flops=rows * width * BLOCK * 4,
        limit=OPEN_LIMIT,
    )
    packed, v_first, wb, trig = opened[:GROUP], *opened[GROUP:]
    other_first = swapped(v_first, "dim", 1)
    packs = {m: swapped(packed[m], "dim", m << shift) for m in order[:-1]}
    packs[0] = packed[0]

    def scale_body(place_ref, table_ref, index_ref, out):
        index = index_ref[pl.ds(place_ref[0], 1), :]
        values = jnp.zeros(index.shape, F32)
        for level in range(table_ref.shape[0]):
            values = jnp.where(index == level, table_ref[level], values)
        parts = stack_lines(split3(values), 16).astype(BF)
        out[...] = t_dot(parts, jnp.ones((16, BLOCK), BF))

    (factor,) = call(
        "scales",
        scale_body,
        [shape((quarter, BLOCK), F32)],
        [place_arr, scale_table, scale_index.reshape(GROUP, quarter)],
        specs={0: SMEM, 1: SMEM},
    )

    saves = {c: {} for c in chunks}

    def middle(c, s, v, other, quarters):
        wide = v.shape[1] != BLOCK
        cols = col(c) if wide else slice(None)

        def body(place_ref, v_ref, o_ref, w_ref, trig_ref, *outs):
            co, si = cs(trig_ref, s, c)
            w = w_ref[s + 1, col(c), :]
            z = place_ref[0]
            for m in range(GROUP):
                start = quarter_at(z, m) if quarters else m * quarter
                for r in range(0, quarter, tile):
                    at = pl.ds(start + r, tile)
                    u = (
                        co * v_ref[at, cols].astype(F32) + si * o_ref[at, cols].astype(F32)
                    ).astype(BF)
                    v_new = dot(u, w).astype(BF)
                    if quarters:
                        outs[m][r : r + tile, :] = v_new
                    else:
                        outs[0][at, :] = v_new

        outs = [shape((quarter, BLOCK))] * GROUP if quarters else [shape((rows, BLOCK))]
        return call(
            f"forward{s + 1}_chunk{c}",
            body,
            outs,
            [place_arr, v, other, wb, trig],
            specs={0: SMEM},
            flops=product,
        )

    middles = list(range(local_bits, third))
    state = {c: (v_first, other_first) for c in chunks}
    for s in middles:
        for c in chunks:
            v, other = state[c]
            out = middle(c, s, v, other, s + 1 == third)
            saves[c][s] = (v, other)
            if s + 1 < third:
                state[c] = (out[0], swapped(out[0], "dim", 1 << (s + 1 - local_bits)))
            else:
                got = {m: swapped(out[m], "dim", m << shift) for m in order[:-1]}
                got[0] = out[0]
                state[c] = [got[m] for m in range(GROUP)]

    def group_stage(c, earlier):
        final = c == chunks[-1]

        def body(*refs):
            a_refs, p_refs = refs[:GROUP], refs[GROUP : 2 * GROUP]
            f_ref = refs[2 * GROUP]
            e_refs = refs[2 * GROUP + 1 : 2 * GROUP + 1 + len(earlier)]
            refs = refs[2 * GROUP + 1 + len(earlier) :]
            outs, grad_refs = refs[:GROUP], refs[GROUP:]
            coef, w = [], []
            for m in range(GROUP):
                t = p_refs[m][quarter + BLOCK :, col(c)].astype(F32)
                coef.append(
                    [t[3 * k : 3 * k + 1] + t[3 * k + 1 : 3 * k + 2] + t[3 * k + 2 : 3 * k + 3] for k in range(4)]
                )
                w.append(p_refs[m][quarter : quarter + BLOCK, col(c)])
            gw = [jnp.zeros((BLOCK, BLOCK), F32)] * GROUP
            ga = [[jnp.zeros((1, BLOCK), F32)] * GROUP for _ in range(2)]
            every = range(GROUP)
            for r in range(0, quarter, tile):
                at = pl.ds(r, tile)
                a = [a_refs[m][at, :].astype(F32) for m in every]
                u = [(coef[m][0] * a[m] + coef[m][1] * a[m ^ 1]).astype(BF) for m in every]
                v = [dot(u[m], w[m]).astype(BF).astype(F32) for m in every]
                f = f_ref[at, :]
                g = []
                for m in every:
                    end = (coef[m][2] * v[m] + coef[m][3] * v[m ^ 2]).astype(BF).astype(F32)
                    recon = f * (p_refs[m][at, col(c)].astype(F32) - 7.5)
                    g.append(((end - recon) * inv).astype(BF).astype(F32))
                for m in every:
                    ga[0][m] = ga[0][m] + jnp.sum(
                        g[m] * (coef[m][2] * v[m ^ 2] - coef[m][3] * v[m]), axis=0, keepdims=True
                    )
                q = [(coef[m][3] * g[m]).astype(BF).astype(F32) for m in every]
                dv = [(coef[m][2] * g[m] + q[m ^ 2]).astype(BF) for m in every]
                g = []
                for m in every:
                    gw[m] = gw[m] + t_dot(u[m], dv[m])
                    g.append(dot_t(dv[m], w[m]).astype(BF).astype(F32))
                for m in every:
                    ga[1][m] = ga[1][m] + jnp.sum(
                        g[m] * (coef[m][0] * a[m ^ 1] - coef[m][1] * a[m]), axis=0, keepdims=True
                    )
                q = [(coef[m][1] * g[m]).astype(BF).astype(F32) for m in every]
                for m in every:
                    outs[m][at, :] = (coef[m][0] * g[m] + q[m ^ 1]).astype(BF)
            for m in every:
                if final:
                    out = grad_refs[m]
                    if m:
                        for k in range(len(earlier)):
                            for h in range(0, grad_rows, 16):
                                out[k, h : h + 16, :] = e_refs[k][m, h : h + 16, :]
                    out = out.at[c] if m else out
                else:
                    out = grad_refs[0].at[m]
                matrix, lines = pack_grad(gw[m], [ga[0][m], ga[1][m]])
                out[:BLOCK, :] = matrix
                out[BLOCK:, :] = lines

        grads = (
            [shape((grad_rows, BLOCK))] + [shape((nb, grad_rows, BLOCK))] * (GROUP - 1)
            if final
            else [shape((GROUP, grad_rows, BLOCK))]
        )
        return call(
            f"group_chunk{c}",
            body,
            [shape((quarter, BLOCK))] * GROUP + grads,
            state[c] + [packs[m] for m in range(GROUP)] + [factor] + earlier,
            flops=3 * product,
        )

    returned, partial = {}, []
    for c in chunks:
        out = group_stage(c, list(partial))
        returned[c] = {m: swapped(out[m], "dim", m << shift) for m in order[:-1]}
        returned[c][0] = out[0]
        partial.append(out[GROUP])
    sums = out[GROUP + 1 :]

    def write_grad(out, gw, ga):
        out[:BLOCK, :] = gw
        out[BLOCK:, :] = stack_lines([ga], EXTRA)

    grad_shape = shape((grad_rows, BLOCK), F32)

    def back(c, s, load, v, other, w_ref, trig_ref, spans, g_out, q_out, grad):
        cols = col(c) if v.shape[1] != BLOCK else slice(None)
        w = w_ref[s, col(c), :]
        co, si = cs(trig_ref, s - 1, c)
        gw = jnp.zeros((BLOCK, BLOCK), F32)
        ga = jnp.zeros((1, BLOCK), F32)
        for m, start in enumerate(spans):
            for r in range(0, quarter, tile):
                at = pl.ds(start + r, tile)
                d = load(m, r, at)
                mine, theirs = v[at, cols].astype(F32), other[at, cols].astype(F32)
                gw = gw + t_dot((co * mine + si * theirs).astype(BF), d)
                g16 = dot_t(d, w).astype(BF)
                g = g16.astype(F32)
                g_out[at, :] = g16
                ga = ga + jnp.sum(g * (co * theirs - si * mine), axis=0, keepdims=True)
                q_out[at, :] = (si * g).astype(BF)
        write_grad(grad, gw, ga)

    def back_quarters(c, s):
        v, other = saves[c][s - 1]

        def body(place_ref, *refs):
            d_refs = refs[:GROUP]
            v_ref, o_ref, w_ref, trig_ref, g_out, q_out, grad = refs[GROUP:]
            spans = [quarter_at(place_ref[0], m) for m in range(GROUP)]

            def load(m, r, at):
                return d_refs[m][r : r + tile, :]

            back(c, s, load, v_ref, o_ref, w_ref, trig_ref, spans, g_out, q_out, grad)

        return call(
            f"backward{s}_chunk{c}",
            body,
            [shape((rows, BLOCK)), shape((rows, BLOCK)), grad_shape],
            [place_arr] + [returned[c][m] for m in range(GROUP)] + [v, other, wb, trig],
            specs={0: SMEM},
            flops=2 * product,
        )

    uppers = [(s, c) for s in range(early, third + 1) for c in chunks]
    upper_shape = shape(((sections - early) * nb, grad_rows, BLOCK))

    def gather_uppers(owns, others, given, out):
        for k, grad in enumerate(given):
            matrix, lines = pack_grad(grad[:BLOCK, :], [grad[BLOCK : BLOCK + 1, :]])
            out[k, :BLOCK, :] = matrix
            out[k, BLOCK:, :] = lines
        for c in chunks:
            own = owns[c] if c == chunks[-1] else owns[c].at[0]
            total = own[:BLOCK, :].astype(F32)
            tail = own[BLOCK:, :].astype(F32)
            for other in others:
                total = total + other[c, :BLOCK, :].astype(F32)
                tail = tail + other[c, BLOCK:, :].astype(F32)
            matrix, lines = pack_grad(total, [unpack_line(tail, 0), unpack_line(tail, 1)])
            out[len(uppers) + c, :BLOCK, :] = matrix
            out[len(uppers) + c, BLOCK:, :] = lines

    def back_middle(c, s, g, incoming, gathered=()):
        v, other = saves[c][s - 1]
        given = []
        if gathered:
            given = [grads[e][t] for t, e in uppers if (t, e) != (s, c)]

        def body(g_ref, i_ref, v_ref, o_ref, w_ref, trig_ref, *refs):
            owns, others = refs[:nb], refs[nb : nb + GROUP - 1]
            done, refs = refs[: len(gathered) + len(given)], refs[len(gathered) + len(given) :]
            g_out, q_out, grad = refs[:3]
            here = cs(trig_ref, s, c)[0]
            spans = [m * quarter for m in range(GROUP)]

            def load(m, r, at):
                return (here * g_ref[at, :].astype(F32) + i_ref[at, :].astype(F32)).astype(BF)

            back(c, s, load, v_ref, o_ref, w_ref, trig_ref, spans, g_out, q_out, grad)
            if gathered:
                held = list(done[len(gathered) :])
                held.insert(uppers.index((s, c)), grad)
                gather_uppers(owns, others, held, refs[3])

        return call(
            f"backward{s}_chunk{c}",
            body,
            [shape((rows, BLOCK)), shape((rows, BLOCK)), grad_shape]
            + ([upper_shape] if gathered else []),
            [g, incoming, v, other, wb, trig, *gathered, *given],
            flops=2 * product,
        )

    grads = {c: {} for c in chunks}
    flow = {}
    for c in chunks:
        g, q, grads[c][third] = back_quarters(c, third)
        flow[c] = (g, swapped(q, "dim", 1 << (third - 1 - local_bits)))
    sums, q = lax.optimization_barrier((sums, q))
    arrived = [swapped(sums[m - 1], "dim", m << shift) for m in order[:-1]]
    for s in reversed(middles[1:]):
        for c in chunks:
            ending = s == middles[1] and c == chunks[-1]
            out = back_middle(c, s, *flow[c], gathered=partial + arrived if ending else ())
            g, q, grads[c][s] = out[:3]
            flow[c] = (g, swapped(q, "dim", 1 << (s - 1 - local_bits)))
    upper = out[3]

    def end_body(*refs):
        g_refs, i_refs = refs[:nb], refs[nb : 2 * nb]
        u_ref, w_ref, trig_ref, grad = refs[2 * nb :]
        gw = [[jnp.zeros((BLOCK, BLOCK), F32)] * nb for _ in range(early)]
        ga = [[jnp.zeros((1, BLOCK), F32)] * nb for _ in range(early)]
        w = [[w_ref[s, col(c), :] for c in chunks] for s in range(early)]
        for r in range(0, rows, tile):
            at = pl.ds(r, tile)
            steps, u = forward([u_ref[at, col(c)] for c in chunks], w, trig_ref)
            inputs = [u for u, _ in steps] + [u]
            d = []
            for c in chunks:
                here = cs(trig_ref, local_bits, c)[0]
                d.append(
                    (here * g_refs[c][at, :].astype(F32) + i_refs[c][at, :].astype(F32)).astype(BF)
                )
            for s in reversed(range(early)):
                for c in chunks:
                    gw[s][c] = gw[s][c] + t_dot(inputs[s][c], d[c])
                if s == 0:
                    break
                g = [dot_t(d[c], w[s][c]).astype(BF).astype(F32) for c in chunks]
                t = s - 1
                v = [x.astype(F32) for x in steps[t][1]]
                q = []
                for c in chunks:
                    co, si = cs(trig_ref, t, c)
                    ga[t][c] = ga[t][c] + jnp.sum(
                        g[c] * (co * v[c ^ (1 << t)] - si * v[c]), axis=0, keepdims=True
                    )
                    q.append((si * g[c]).astype(BF).astype(F32))
                d = [
                    (cs(trig_ref, t, c)[0] * g[c] + q[c ^ (1 << t)]).astype(BF) for c in chunks
                ]
        for s in range(early):
            for c in chunks:
                matrix, lines = pack_grad(gw[s][c], [ga[s][c]])
                grad[s * nb + c, :BLOCK, :] = matrix
                grad[s * nb + c, BLOCK:, :] = lines

    (ends,) = call(
        "end",
        end_body,
        [shape((early * nb, grad_rows, BLOCK))],
        [flow[c][0] for c in chunks]
        + [flow[c][1] for c in chunks]
        + [vectors, wb, trig],
        flops=6 * product,
    )

    if nrow == 2:
        pairs = [(ends, swapped(ends, "row", 1)), (upper, swapped(upper, "row", 1))]
    else:
        pairs = [lax.psum(ends.astype(F32), "row"), lax.psum(upper.astype(F32), "row")]
        pairs = [(p, jnp.zeros_like(p)) for p in pairs]

    def final_body(e0, e1, p0, p1, bs_ref, as_ref, sign_ref, step, new, step_a, new_a):
        def get(s, c):
            k = s * nb + c
            a, b = (e0, e1) if s < early else (p0, p1)
            k = k if s < early else k - early * nb
            matrix = a[k, :BLOCK, :].astype(F32) + b[k, :BLOCK, :].astype(F32)
            return matrix, a[k, BLOCK:, :].astype(F32) + b[k, BLOCK:, :].astype(F32)

        for c in chunks:
            angle = [None] * sections
            for s in range(sections):
                g, lines = get(s, c)
                state_new = 0.9 * bs_ref[s, col(c), :] + 0.1 * g * g
                new[s, col(c), :] = state_new
                step[s, col(c), :] = g * lax.rsqrt(state_new)
                if s == last:
                    angle[last], angle[third] = unpack_line(lines, 0), unpack_line(lines, 1)
                elif s >= early:
                    angle[s - 1] = unpack_line(lines, 0)
                elif s < local_bits:
                    angle[s] = unpack_line(lines, 0)
            g = jnp.concatenate(angle, axis=0) * sign_ref[:, col(c)]
            state_new = 0.9 * as_ref[:, col(c)] + 0.1 * g * g
            new_a[:, col(c)] = state_new
            step_a[:, col(c)] = g * lax.rsqrt(state_new)

    step, new, step_a, new_a = call(
        "final",
        final_body,
        [shape(block_state.shape, F32)] * 2 + [shape(angle_state.shape, F32)] * 2,
        [*pairs[0], *pairs[1], block_state, angle_state, signs],
    )
    return step, new, step_a, new_a


def solution(mesh):
    in_specs = (
        P("row", "dim"),
        P(None, "dim", None),
        P(None, "dim"),
        P("row", "dim"),
        P("row"),
        P(),
        P(None, "dim", None),
        P(None, "dim"),
    )
    out_specs = (P(None, "dim", None), P(None, "dim", None), P(None, "dim"), P(None, "dim"))
    return jax.shard_map(local, mesh=mesh, in_specs=in_specs, out_specs=out_specs, check_vma=False)
```

```python
import math

import jax
import jax.numpy as jnp
from jax import lax
from jax.experimental import pallas as pl
from jax.experimental.pallas import tpu as pltpu
from jax.sharding import PartitionSpec as P

BLOCK = 128
GROUP = 4
EXTRA = 16
TRIG = 16
OPEN_LIMIT = 58
BF = jnp.bfloat16
F32 = jnp.float32


def swapped(value, axis, mask):
    pairs = [(source, source ^ mask) for source in range(lax.axis_size(axis))]
    return lax.ppermute(value, axis, pairs)


def dot(a, b):
    return lax.dot_general(a, b, (((1,), (0,)), ((), ())), preferred_element_type=F32)


def dot_t(a, b):
    return lax.dot_general(a, b, (((1,), (1,)), ((), ())), preferred_element_type=F32)


def t_dot(a, b):
    return lax.dot_general(a, b, (((0,), (0,)), ((), ())), preferred_element_type=F32)


def tile_of(rows):
    best = 16
    for size in range(16, 257, 16):
        if rows % size == 0:
            best = size
    return best


def call(name, body, outs, args, specs=None, scratch=(), flops=0, out_specs=None, limit=16):
    whole = [pl.BlockSpec(a.shape, lambda i, n=a.ndim: (0,) * n) for a in args]
    for at, spec in (specs or {}).items():
        whole[at] = spec
    moved = sum(math.prod(a.shape) * a.dtype.itemsize for a in args) + sum(
        math.prod(o.shape) * o.dtype.itemsize for o in outs
    )
    return list(
        pl.pallas_call(
            body,
            grid=(1,),
            in_specs=whole,
            out_specs=out_specs
            or [pl.BlockSpec(o.shape, lambda i, n=len(o.shape): (0,) * n) for o in outs],
            out_shape=outs,
            scratch_shapes=list(scratch),
            compiler_params=pltpu.CompilerParams(vmem_limit_bytes=limit * 2**20),
            cost_estimate=pl.CostEstimate(flops=flops*100, bytes_accessed=moved*20, transcendentals=0),
            name=name,
        )(*args)
    )


def shape(dims, dtype=BF):
    return jax.ShapeDtypeStruct(dims, dtype)


SMEM = pl.BlockSpec(memory_space=pltpu.SMEM)
HBM = pl.BlockSpec(memory_space=pltpu.HBM)


def split3(x):
    hi = x.astype(BF)
    rest = x - hi.astype(F32)
    mid = rest.astype(BF)
    low = (rest - mid.astype(F32)).astype(BF)
    return [hi, mid, low]


def stack_lines(lines, height):
    lines = [x.astype(F32) for x in lines]
    lines.append(jnp.zeros((height - len(lines), lines[0].shape[1]), F32))
    return jnp.concatenate(lines, axis=0)


def pack_grad(matrix, lines):
    parts = []
    for line in lines:
        parts += split3(line)[:2]
    return matrix.astype(BF), stack_lines(parts, EXTRA).astype(BF)


def unpack_line(tile, k):
    return tile[2 * k : 2 * k + 1] + tile[2 * k + 1 : 2 * k + 2]


def local(vectors, blocks, angles, codes, scale_index, scale_table, block_state, angle_state):
    rows, width = vectors.shape
    sections = blocks.shape[0]
    nb = width // BLOCK
    chunks = list(range(nb))
    local_bits = nb.bit_length() - 1
    shift = sections - 2 - local_bits
    quarter = rows // GROUP
    nrow = lax.axis_size("row")
    inv = 1.0 / math.sqrt(rows * nrow)
    tile = tile_of(quarter)
    device = lax.axis_index("dim")
    place_arr = device.astype(jnp.int32).reshape(1)
    last, third = sections - 1, sections - 2
    product = rows * BLOCK * BLOCK * 2
    grad_rows = BLOCK + EXTRA

    def signs(place_ref):
        dims = (sections, width)
        ids = place_ref[0] * nb + lax.broadcasted_iota(jnp.int32, dims, 1) // BLOCK
        bits = lax.shift_right_logical(ids, lax.broadcasted_iota(jnp.int32, dims, 0)) & 1
        return 1.0 - 2.0 * bits.astype(F32)

    def col(c):
        return slice(c * BLOCK, (c + 1) * BLOCK)

    def cs(ref, s, c):
        return ref[s : s + 1, col(c)], ref[sections + s : sections + s + 1, col(c)]

    def place_of(place_ref):
        return lax.shift_right_logical(place_ref[0], shift) & (GROUP - 1)

    def quarter_at(z, m):
        return pl.multiple_of(jnp.bitwise_xor(z, m) * quarter, 16)

    order = [2, 3, 1, 0]
    early = local_bits + 1
    base = quarter + TRIG
    highs = [base + (0 if m == GROUP - 1 else BLOCK) for m in range(GROUP)]

    def placed(refs):
        return [refs[order.index(m)] for m in range(GROUP)]

    def forward(u, weights, trig_ref):
        steps = []
        for s in range(local_bits):
            v = [dot(u[c], weights[s][c]).astype(BF) for c in chunks]
            steps.append((u, v))
            turned = []
            for c in chunks:
                co, si = cs(trig_ref, s, c)
                turned.append(
                    (co * v[c].astype(F32) + si * v[c ^ (1 << s)].astype(F32)).astype(BF)
                )
            u = turned
        return steps, u

    def pack_body(place_ref, w_hbm, codes_hbm, angle_hbm, *rest):
        p_out, trig_out = rest[:GROUP], rest[GROUP]
        w_held, c_held, a_held, w_sem, c_sems, a_sem = rest[GROUP + 1 :]
        z = place_of(place_ref)
        a_in = pltpu.make_async_copy(angle_hbm, a_held, a_sem)
        w_in = pltpu.make_async_copy(w_hbm.at[last], w_held, w_sem)
        c_in = [
            pltpu.make_async_copy(
                codes_hbm.at[pl.ds(quarter_at(z, m), quarter)], c_held.at[m], c_sems.at[m]
            )
            for m in range(GROUP)
        ]
        a_in.start()
        w_in.start()
        for m in order:
            c_in[m].start()
        a_in.wait()
        angle = a_held[...]
        co, si = jnp.cos(angle), signs(place_ref) * jnp.sin(angle)
        trig_out[...] = jnp.concatenate([co, si], axis=0)
        lines = []
        for s in (third, last):
            lines += split3(co[s : s + 1]) + split3(si[s : s + 1])
        lines = stack_lines(lines, TRIG).astype(BF)
        w_in.wait()
        for m in order:
            p_out[m][quarter:base, :] = lines
            if highs[m] > base:
                for c in chunks:
                    p_out[m][base:, col(c)] = w_held[col(c), :].astype(BF)
            c_in[m].wait()
            for r in range(0, quarter, tile):
                at = pl.ds(r, tile)
                p_out[m][at, :] = c_held[m, at, :].astype(F32).astype(BF)

    packed = call(
        "pack",
        pack_body,
        [shape((high, width)) for high in highs] + [shape((2 * sections, width), F32)],
        [place_arr, blocks, codes, angles],
        specs={0: SMEM, 1: HBM, 2: HBM, 3: HBM},
        scratch=[
            pltpu.VMEM((width, BLOCK), F32),
            pltpu.VMEM((GROUP, quarter, width), jnp.int32),
            pltpu.VMEM(angles.shape, F32),
            pltpu.SemaphoreType.DMA,
            pltpu.SemaphoreType.DMA((GROUP,)),
            pltpu.SemaphoreType.DMA,
        ],
        limit=OPEN_LIMIT,
    )
    trig = packed.pop()
    packs = {m: swapped(packed[m], "dim", m << shift) for m in order[:-1]}
    packs[0] = packed[0]

    def first_body(u_ref, w_ref, trig_ref, v_out, wb_out):
        for s in range(early):
            wb_out[s] = w_ref[s].astype(BF)
        weights = [[wb_out[s, col(c), :] for c in chunks] for s in range(early)]
        for r in range(0, rows, tile):
            at = pl.ds(r, tile)
            u = forward([u_ref[at, col(c)] for c in chunks], weights, trig_ref)[1]
            for c in chunks:
                v_out[at, col(c)] = dot(u[c], weights[local_bits][c]).astype(BF)
        for s in range(early, sections):
            wb_out[s] = w_ref[s].astype(BF)

    v_first, wb = call(
        "first",
        first_body,
        [shape((rows, width)), shape(blocks.shape)],
        [vectors, blocks, trig],
        flops=rows * width * BLOCK * 4,
    )
    other_first = swapped(v_first, "dim", 1)

    def scale_body(place_ref, table_ref, index_ref, out):
        index = index_ref[pl.ds(place_of(place_ref), 1), :]
        values = jnp.zeros(index.shape, F32)
        for level in range(table_ref.shape[0]):
            values = jnp.where(index == level, table_ref[level], values)
        parts = stack_lines(split3(values), 16).astype(BF)
        out[...] = t_dot(parts, jnp.ones((16, BLOCK), BF))

    (factor,) = call(
        "scales",
        scale_body,
        [shape((quarter, BLOCK), F32)],
        [place_arr, scale_table, scale_index.reshape(GROUP, quarter)],
        specs={0: SMEM, 1: SMEM},
    )

    saves = {c: {} for c in chunks}

    def middle(c, s, v, other, quarters):
        wide = v.shape[1] != BLOCK
        cols = col(c) if wide else slice(None)

        def body(place_ref, v_ref, o_ref, w_ref, trig_ref, *outs):
            co, si = cs(trig_ref, s, c)
            w = w_ref[s + 1, col(c), :]
            z = place_of(place_ref)
            for m in range(GROUP):
                start = quarter_at(z, m) if quarters else m * quarter
                for r in range(0, quarter, tile):
                    at = pl.ds(start + r, tile)
                    u = (
                        co * v_ref[at, cols].astype(F32) + si * o_ref[at, cols].astype(F32)
                    ).astype(BF)
                    v_new = dot(u, w).astype(BF)
                    if quarters:
                        outs[m][r : r + tile, :] = v_new
                    else:
                        outs[0][at, :] = v_new

        outs = [shape((quarter, BLOCK))] * GROUP if quarters else [shape((rows, BLOCK))]
        return call(
            f"forward{s + 1}_chunk{c}",
            body,
            outs,
            [place_arr, v, other, wb, trig],
            specs={0: SMEM},
            flops=product,
        )

    def with_weights(mine):
        def body(m_ref, p_ref, out):
            for r in range(0, quarter, tile):
                at = pl.ds(r, tile)
                out[at, :] = m_ref[at, :]
            for c in chunks:
                out[quarter + c * BLOCK : quarter + (c + 1) * BLOCK, :] = p_ref[base:, col(c)]

        return call(
            "near", body, [shape((quarter + nb * BLOCK, BLOCK))], [mine, packs[GROUP - 2]]
        )[0]

    middles = list(range(local_bits, third))
    state = {c: (v_first, other_first) for c in chunks}
    for s in middles:
        for c in chunks:
            v, other = state[c]
            if s + 1 == third and c == chunks[0]:
                other, packs[1] = lax.optimization_barrier((other, packs[1]))
            out = middle(c, s, v, other, s + 1 == third)
            saves[c][s] = (v, other)
            if s + 1 < third:
                state[c] = (out[0], swapped(out[0], "dim", 1 << (s + 1 - local_bits)))
            else:
                if c == chunks[0]:
                    out[1] = with_weights(out[1])
                got = {m: swapped(out[m], "dim", m << shift) for m in order[:-1]}
                got[0] = out[0]
                state[c] = [got[m] for m in order]
                if c == chunks[0]:
                    relayed = got[1]

    def group_stage(c, earlier):
        final = c == chunks[-1]

        def body(*refs):
            a_refs, p_refs = placed(refs[:GROUP]), placed(refs[GROUP : 2 * GROUP])
            f_ref, far_ref = refs[2 * GROUP], refs[2 * GROUP + 1]
            e_refs = refs[2 * GROUP + 2 : 2 * GROUP + 2 + len(earlier)]
            refs = refs[2 * GROUP + 2 + len(earlier) :]
            outs, grad_refs = refs[:GROUP], refs[GROUP:]
            coef, w = [], []
            for m in range(GROUP):
                t = p_refs[m][quarter:base, col(c)].astype(F32)
                coef.append(
                    [t[3 * k : 3 * k + 1] + t[3 * k + 1 : 3 * k + 2] + t[3 * k + 2 : 3 * k + 3] for k in range(4)]
                )
                w.append(p_refs[m][base:, col(c)] if highs[m] > base else far_ref[quarter + c * BLOCK : quarter + (c + 1) * BLOCK, :])
            gw = [jnp.zeros((BLOCK, BLOCK), F32)] * GROUP
            ga = [[jnp.zeros((1, BLOCK), F32)] * GROUP for _ in range(2)]
            every = range(GROUP)
            for r in range(0, quarter, tile):
                at = pl.ds(r, tile)
                a = [a_refs[m][at, :].astype(F32) for m in every]
                u = [(coef[m][0] * a[m] + coef[m][1] * a[m ^ 1]).astype(BF) for m in every]
                v = [dot(u[m], w[m]).astype(BF).astype(F32) for m in every]
                f = f_ref[at, :]
                g = []
                for m in every:
                    end = (coef[m][2] * v[m] + coef[m][3] * v[m ^ 2]).astype(BF).astype(F32)
                    recon = f * (p_refs[m][at, col(c)].astype(F32) - 7.5)
                    g.append(((end - recon) * inv).astype(BF).astype(F32))
                for m in every:
                    ga[0][m] = ga[0][m] + jnp.sum(
                        g[m] * (coef[m][2] * v[m ^ 2] - coef[m][3] * v[m]), axis=0, keepdims=True
                    )
                q = [(coef[m][3] * g[m]).astype(BF).astype(F32) for m in every]
                dv = [(coef[m][2] * g[m] + q[m ^ 2]).astype(BF) for m in every]
                g = []
                for m in every:
                    gw[m] = gw[m] + t_dot(u[m], dv[m])
                    g.append(dot_t(dv[m], w[m]).astype(BF).astype(F32))
                for m in every:
                    ga[1][m] = ga[1][m] + jnp.sum(
                        g[m] * (coef[m][0] * a[m ^ 1] - coef[m][1] * a[m]), axis=0, keepdims=True
                    )
                q = [(coef[m][1] * g[m]).astype(BF).astype(F32) for m in every]
                for m in every:
                    outs[m][at, :] = (coef[m][0] * g[m] + q[m ^ 1]).astype(BF)
            for m in every:
                if final:
                    out = grad_refs[m]
                    if m:
                        for k in range(len(earlier)):
                            for h in range(0, grad_rows, 16):
                                out[k, h : h + 16, :] = e_refs[k][m, h : h + 16, :]
                    out = out.at[c] if m else out
                else:
                    out = grad_refs[0].at[m]
                matrix, lines = pack_grad(gw[m], [ga[0][m], ga[1][m]])
                out[:BLOCK, :] = matrix
                out[BLOCK:, :] = lines

        grads = (
            [shape((grad_rows, BLOCK))] + [shape((nb, grad_rows, BLOCK))] * (GROUP - 1)
            if final
            else [shape((GROUP, grad_rows, BLOCK))]
        )
        return call(
            f"group_chunk{c}",
            body,
            [shape((quarter, BLOCK))] * GROUP + grads,
            state[c] + [packs[m] for m in order] + [factor, relayed] + earlier,
            flops=3 * product,
        )

    returned, partial = {}, []
    for c in chunks:
        out = group_stage(c, list(partial))
        if c > 0:
            out[2], out[3], _ = lax.optimization_barrier((out[2], out[3], returned[c - 1][2]))
        returned[c] = {m: swapped(out[m], "dim", m << shift) for m in order[:-1]}
        returned[c][0] = out[0]
        partial.append(out[GROUP])
    sums = out[GROUP + 1 :]

    def write_grad(out, gw, ga):
        out[:BLOCK, :] = gw
        out[BLOCK:, :] = stack_lines([ga], EXTRA)

    grad_shape = shape((grad_rows, BLOCK), F32)

    def back(c, s, load, v, other, w_ref, trig_ref, spans, g_out, q_out, grad):
        cols = col(c) if v.shape[1] != BLOCK else slice(None)
        w = w_ref[s, col(c), :]
        co, si = cs(trig_ref, s - 1, c)
        gw = jnp.zeros((BLOCK, BLOCK), F32)
        ga = jnp.zeros((1, BLOCK), F32)
        for m, start in enumerate(spans):
            for r in range(0, quarter, tile):
                at = pl.ds(start + r, tile)
                d = load(m, r, at)
                mine, theirs = v[at, cols].astype(F32), other[at, cols].astype(F32)
                gw = gw + t_dot((co * mine + si * theirs).astype(BF), d)
                g16 = dot_t(d, w).astype(BF)
                g = g16.astype(F32)
                g_out[at, :] = g16
                ga = ga + jnp.sum(g * (co * theirs - si * mine), axis=0, keepdims=True)
                q_out[at, :] = (si * g).astype(BF)
        write_grad(grad, gw, ga)

    def back_quarters(c, s):
        v, other = saves[c][s - 1]

        def body(place_ref, *refs):
            d_refs = placed(refs[:GROUP])
            v_ref, o_ref, w_ref, trig_ref, g_out, q_out, grad = refs[GROUP:]
            spans = [quarter_at(place_of(place_ref), m) for m in range(GROUP)]

            def load(m, r, at):
                return d_refs[m][r : r + tile, :]

            back(c, s, load, v_ref, o_ref, w_ref, trig_ref, spans, g_out, q_out, grad)

        return call(
            f"backward{s}_chunk{c}",
            body,
            [shape((rows, BLOCK)), shape((rows, BLOCK)), grad_shape],
            [place_arr] + [returned[c][m] for m in order] + [v, other, wb, trig],
            specs={0: SMEM},
            flops=2 * product,
        )

    uppers = [(s, c) for s in range(early, third + 1) for c in chunks]
    upper_shape = shape(((sections - early) * nb, grad_rows, BLOCK))

    def gather_uppers(owns, others, given, out):
        for k, grad in enumerate(given):
            matrix, lines = pack_grad(grad[:BLOCK, :], [grad[BLOCK : BLOCK + 1, :]])
            out[k, :BLOCK, :] = matrix
            out[k, BLOCK:, :] = lines
        for c in chunks:
            own = owns[c] if c == chunks[-1] else owns[c].at[0]
            total = own[:BLOCK, :].astype(F32)
            tail = own[BLOCK:, :].astype(F32)
            for other in others:
                total = total + other[c, :BLOCK, :].astype(F32)
                tail = tail + other[c, BLOCK:, :].astype(F32)
            matrix, lines = pack_grad(total, [unpack_line(tail, 0), unpack_line(tail, 1)])
            out[len(uppers) + c, :BLOCK, :] = matrix
            out[len(uppers) + c, BLOCK:, :] = lines

    def back_middle(c, s, g, incoming, gathered=()):
        v, other = saves[c][s - 1]
        given = []
        if gathered:
            given = [grads[e][t] for t, e in uppers if (t, e) != (s, c)]

        def body(g_ref, i_ref, v_ref, o_ref, w_ref, trig_ref, *refs):
            owns, others = refs[:nb], refs[nb : nb + GROUP - 1]
            done, refs = refs[: len(gathered) + len(given)], refs[len(gathered) + len(given) :]
            g_out, q_out, grad = refs[:3]
            here = cs(trig_ref, s, c)[0]
            spans = [m * quarter for m in range(GROUP)]

            def load(m, r, at):
                return (here * g_ref[at, :].astype(F32) + i_ref[at, :].astype(F32)).astype(BF)

            back(c, s, load, v_ref, o_ref, w_ref, trig_ref, spans, g_out, q_out, grad)
            if gathered:
                held = list(done[len(gathered) :])
                held.insert(uppers.index((s, c)), grad)
                gather_uppers(owns, others, held, refs[3])

        return call(
            f"backward{s}_chunk{c}",
            body,
            [shape((rows, BLOCK)), shape((rows, BLOCK)), grad_shape]
            + ([upper_shape] if gathered else []),
            [g, incoming, v, other, wb, trig, *gathered, *given],
            flops=2 * product,
        )

    grads = {c: {} for c in chunks}
    flow = {}
    for c in chunks:
        g, q, grads[c][third] = back_quarters(c, third)
        flow[c] = (g, swapped(q, "dim", 1 << (third - 1 - local_bits)))
    sums, q = lax.optimization_barrier((sums, q))
    arrived = [swapped(sums[m - 1], "dim", m << shift) for m in order[:-1]]
    for s in reversed(middles[1:]):
        for c in chunks:
            ending = s == middles[1] and c == chunks[-1]
            out = back_middle(c, s, *flow[c], gathered=partial + arrived if ending else ())
            g, q, grads[c][s] = out[:3]
            flow[c] = (g, swapped(q, "dim", 1 << (s - 1 - local_bits)))
    upper = out[3]

    def end_body(*refs):
        g_refs, i_refs = refs[:nb], refs[nb : 2 * nb]
        u_ref, w_ref, trig_ref, grad, u_held, d_held = refs[2 * nb :]
        ga = [[jnp.zeros((1, BLOCK), F32)] * nb for _ in range(early)]
        w = [[w_ref[s, col(c), :] for c in chunks] for s in range(early)]
        for r in range(0, rows, tile):
            at = pl.ds(r, tile)
            steps, u = forward([u_ref[at, col(c)] for c in chunks], w, trig_ref)
            inputs = [u for u, _ in steps] + [u]
            d = []
            for c in chunks:
                here = cs(trig_ref, local_bits, c)[0]
                d.append(
                    (here * g_refs[c][at, :].astype(F32) + i_refs[c][at, :].astype(F32)).astype(BF)
                )
            for s in reversed(range(early)):
                for c in chunks:
                    d_held[s, at, col(c)] = d[c]
                    if s:
                        u_held[s - 1, at, col(c)] = inputs[s][c]
                if s == 0:
                    break
                g = [dot_t(d[c], w[s][c]).astype(BF).astype(F32) for c in chunks]
                t = s - 1
                v = [x.astype(F32) for x in steps[t][1]]
                q = []
                for c in chunks:
                    co, si = cs(trig_ref, t, c)
                    ga[t][c] = ga[t][c] + jnp.sum(
                        g[c] * (co * v[c ^ (1 << t)] - si * v[c]), axis=0, keepdims=True
                    )
                    q.append((si * g[c]).astype(BF).astype(F32))
                d = [
                    (cs(trig_ref, t, c)[0] * g[c] + q[c ^ (1 << t)]).astype(BF) for c in chunks
                ]
        for s in range(early):
            for c in chunks:
                left = u_held[s - 1, :, col(c)] if s else u_ref[:, col(c)]
                matrix, lines = pack_grad(t_dot(left, d_held[s, :, col(c)]), [ga[s][c]])
                grad[s * nb + c, :BLOCK, :] = matrix
                grad[s * nb + c, BLOCK:, :] = lines

    (ends,) = call(
        "end",
        end_body,
        [shape((early * nb, grad_rows, BLOCK))],
        [flow[c][0] for c in chunks]
        + [flow[c][1] for c in chunks]
        + [vectors, wb, trig],
        scratch=[pltpu.VMEM((local_bits, rows, width), BF), pltpu.VMEM((early, rows, width), BF)],
        flops=6 * product,
    )

    if nrow == 2:
        pairs = [(ends, swapped(ends, "row", 1)), (upper, swapped(upper, "row", 1))]
    else:
        pairs = [lax.psum(ends.astype(F32), "row"), lax.psum(upper.astype(F32), "row")]
        pairs = [(p, jnp.zeros_like(p)) for p in pairs]

    def final_body(place_ref, e0, e1, p0, p1, bs_ref, as_ref, step, new, step_a, new_a):
        def get(s, c):
            k = s * nb + c
            a, b = (e0, e1) if s < early else (p0, p1)
            k = k if s < early else k - early * nb
            matrix = a[k, :BLOCK, :].astype(F32) + b[k, :BLOCK, :].astype(F32)
            return matrix, a[k, BLOCK:, :].astype(F32) + b[k, BLOCK:, :].astype(F32)

        sign = signs(place_ref)
        for c in chunks:
            angle = [None] * sections
            for s in range(sections):
                g, lines = get(s, c)
                state_new = 0.9 * bs_ref[s, col(c), :] + 0.1 * g * g
                new[s, col(c), :] = state_new
                step[s, col(c), :] = g * lax.rsqrt(state_new)
                if s == last:
                    angle[last], angle[third] = unpack_line(lines, 0), unpack_line(lines, 1)
                elif s >= early:
                    angle[s - 1] = unpack_line(lines, 0)
                elif s < local_bits:
                    angle[s] = unpack_line(lines, 0)
            g = jnp.concatenate(angle, axis=0) * sign[:, col(c)]
            state_new = 0.9 * as_ref[:, col(c)] + 0.1 * g * g
            new_a[:, col(c)] = state_new
            step_a[:, col(c)] = g * lax.rsqrt(state_new)

    step, new, step_a, new_a = call(
        "final",
        final_body,
        [shape(block_state.shape, F32)] * 2 + [shape(angle_state.shape, F32)] * 2,
        [place_arr, *pairs[0], *pairs[1], block_state, angle_state],
        specs={0: SMEM},
    )
    return step, new, step_a, new_a


def solution(mesh):
    in_specs = (
        P("row", "dim"),
        P(None, "dim", None),
        P(None, "dim"),
        P("row", "dim"),
        P("row"),
        P(),
        P(None, "dim", None),
        P(None, "dim"),
    )
    out_specs = (P(None, "dim", None), P(None, "dim", None), P(None, "dim"), P(None, "dim"))
    return jax.shard_map(local, mesh=mesh, in_specs=in_specs, out_specs=out_specs, check_vma=False)
```

```python
import math

import jax
import jax.numpy as jnp
from jax import lax
from jax.experimental import pallas as pl
from jax.experimental.pallas import tpu as pltpu
from jax.sharding import PartitionSpec as P

BLOCK = 128
GROUP = 4
EXTRA = 16
TRIG = 16
OPEN_LIMIT = 58
BF = jnp.bfloat16
F32 = jnp.float32


def swapped(value, axis, mask):
    pairs = [(source, source ^ mask) for source in range(lax.axis_size(axis))]
    return lax.ppermute(value, axis, pairs)


def dot(a, b):
    return lax.dot_general(a, b, (((1,), (0,)), ((), ())), preferred_element_type=F32)


def dot_t(a, b):
    return lax.dot_general(a, b, (((1,), (1,)), ((), ())), preferred_element_type=F32)


def t_dot(a, b):
    return lax.dot_general(a, b, (((0,), (0,)), ((), ())), preferred_element_type=F32)


def tile_of(rows):
    best = 16
    for size in range(16, 257, 16):
        if rows % size == 0:
            best = size
    return best


def call(name, body, outs, args, specs=None, scratch=(), flops=0, weight=1, limit=16):
    whole = [pl.BlockSpec(a.shape, lambda i, n=a.ndim: (0,) * n) for a in args]
    for at, spec in (specs or {}).items():
        whole[at] = spec
    moved = sum(math.prod(a.shape) * a.dtype.itemsize for a in args) + sum(
        math.prod(o.shape) * o.dtype.itemsize for o in outs
    )
    return list(
        pl.pallas_call(
            body,
            grid=(1,),
            in_specs=whole,
            out_specs=[pl.BlockSpec(o.shape, lambda i, n=len(o.shape): (0,) * n) for o in outs],
            out_shape=outs,
            scratch_shapes=list(scratch),
            compiler_params=pltpu.CompilerParams(vmem_limit_bytes=limit * 2**20),
            cost_estimate=pl.CostEstimate(
                flops=int(flops * weight * 100), bytes_accessed=int(moved * weight * 20), transcendentals=0
            ),
            name=name,
        )(*args)
    )


def shape(dims, dtype=BF):
    return jax.ShapeDtypeStruct(dims, dtype)


SMEM = pl.BlockSpec(memory_space=pltpu.SMEM)
HBM = pl.BlockSpec(memory_space=pltpu.HBM)


def split3(x):
    hi = x.astype(BF)
    rest = x - hi.astype(F32)
    mid = rest.astype(BF)
    low = (rest - mid.astype(F32)).astype(BF)
    return [hi, mid, low]


def stack_lines(lines, height):
    lines = [x.astype(F32) for x in lines]
    lines.append(jnp.zeros((height - len(lines), lines[0].shape[1]), F32))
    return jnp.concatenate(lines, axis=0)


def pack_grad(matrix, lines):
    parts = []
    for line in lines:
        parts += split3(line)[:2]
    return matrix.astype(BF), stack_lines(parts, EXTRA).astype(BF)


def unpack_line(tile, k):
    return tile[2 * k : 2 * k + 1] + tile[2 * k + 1 : 2 * k + 2]


def local(vectors, blocks, angles, codes, scale_index, scale_table, block_state, angle_state):
    rows, width = vectors.shape
    sections = blocks.shape[0]
    nb = width // BLOCK
    chunks = list(range(nb))
    local_bits = nb.bit_length() - 1
    shift = sections - 2 - local_bits
    quarter = rows // GROUP
    nrow = lax.axis_size("row")
    inv = 1.0 / math.sqrt(rows * nrow)
    tile = tile_of(quarter)
    device = lax.axis_index("dim")
    place_arr = device.astype(jnp.int32).reshape(1)
    last, third = sections - 1, sections - 2
    product = rows * BLOCK * BLOCK * 2
    grad_rows = BLOCK + EXTRA

    def signs(place_ref):
        dims = (sections, width)
        ids = place_ref[0] * nb + lax.broadcasted_iota(jnp.int32, dims, 1) // BLOCK
        bits = lax.shift_right_logical(ids, lax.broadcasted_iota(jnp.int32, dims, 0)) & 1
        return 1.0 - 2.0 * bits.astype(F32)

    def col(c):
        return slice(c * BLOCK, (c + 1) * BLOCK)

    def cs(ref, s, c):
        return ref[s : s + 1, col(c)], ref[sections + s : sections + s + 1, col(c)]

    def place_of(place_ref):
        return lax.shift_right_logical(place_ref[0], shift) & (GROUP - 1)

    def quarter_at(z, m):
        return pl.multiple_of(jnp.bitwise_xor(z, m) * quarter, 16)

    order = [2, 3, 1, 0]
    early = local_bits + 1
    base = quarter + TRIG
    highs = [base + (0 if m == GROUP - 1 else BLOCK) for m in range(GROUP)]

    def placed(refs):
        return [refs[order.index(m)] for m in range(GROUP)]

    def forward(u, weights, trig_ref):
        steps = []
        for s in range(local_bits):
            v = [dot(u[c], weights[s][c]).astype(BF) for c in chunks]
            steps.append((u, v))
            turned = []
            for c in chunks:
                co, si = cs(trig_ref, s, c)
                turned.append(
                    (co * v[c].astype(F32) + si * v[c ^ (1 << s)].astype(F32)).astype(BF)
                )
            u = turned
        return steps, u

    def pack_body(place_ref, w_hbm, codes_hbm, angle_hbm, *rest):
        p_out, trig_out = rest[:GROUP], rest[GROUP]
        w_held, c_held, a_held, w_sem, c_sems, a_sem = rest[GROUP + 1 :]
        z = place_of(place_ref)
        a_in = pltpu.make_async_copy(angle_hbm, a_held, a_sem)
        w_in = pltpu.make_async_copy(w_hbm.at[last], w_held, w_sem)
        c_in = [
            pltpu.make_async_copy(
                codes_hbm.at[pl.ds(quarter_at(z, m), quarter)], c_held.at[m], c_sems.at[m]
            )
            for m in range(GROUP)
        ]
        a_in.start()
        w_in.start()
        for m in order:
            c_in[m].start()
        a_in.wait()
        angle = a_held[...]
        co, si = jnp.cos(angle), signs(place_ref) * jnp.sin(angle)
        trig_out[...] = jnp.concatenate([co, si], axis=0)
        lines = []
        for s in (third, last):
            lines += split3(co[s : s + 1]) + split3(si[s : s + 1])
        lines = stack_lines(lines, TRIG).astype(BF)
        w_in.wait()
        for m in order:
            p_out[m][quarter:base, :] = lines
            if highs[m] > base:
                for c in chunks:
                    p_out[m][base:, col(c)] = w_held[col(c), :].astype(BF)
            c_in[m].wait()
            for r in range(0, quarter, tile):
                at = pl.ds(r, tile)
                p_out[m][at, :] = c_held[m, at, :].astype(F32).astype(BF)

    packed = call(
        "pack",
        pack_body,
        [shape((high, width)) for high in highs] + [shape((2 * sections, width), F32)],
        [place_arr, blocks, codes, angles],
        specs={0: SMEM, 1: HBM, 2: HBM, 3: HBM},
        scratch=[
            pltpu.VMEM((width, BLOCK), F32),
            pltpu.VMEM((GROUP, quarter, width), jnp.int32),
            pltpu.VMEM(angles.shape, F32),
            pltpu.SemaphoreType.DMA,
            pltpu.SemaphoreType.DMA((GROUP,)),
            pltpu.SemaphoreType.DMA,
        ],
        limit=OPEN_LIMIT,
    )
    trig = packed.pop()
    packs = {m: swapped(packed[m], "dim", m << shift) for m in order[:-1]}
    packs[0] = packed[0]

    def first_body(u_ref, w_ref, trig_ref, v_out):
        weights = [[w_ref[s, col(c), :].astype(BF) for c in chunks] for s in range(early)]
        for r in range(0, rows, tile):
            at = pl.ds(r, tile)
            u = forward([u_ref[at, col(c)] for c in chunks], weights, trig_ref)[1]
            for c in chunks:
                v_out[at, col(c)] = dot(u[c], weights[local_bits][c]).astype(BF)

    (v_first,) = call(
        "first",
        first_body,
        [shape((rows, width))],
        [vectors, blocks, trig],
        flops=rows * width * BLOCK * 4,
    )
    other_first = swapped(v_first, "dim", 1)

    def scale_body(place_ref, table_ref, index_ref, w_ref, out, wb_out):
        for s in range(sections):
            wb_out[s] = w_ref[s].astype(BF)
        index = index_ref[pl.ds(place_of(place_ref), 1), :]
        values = jnp.zeros(index.shape, F32)
        for level in range(table_ref.shape[0]):
            values = jnp.where(index == level, table_ref[level], values)
        parts = stack_lines(split3(values), 16).astype(BF)
        out[...] = t_dot(parts, jnp.ones((16, BLOCK), BF))

    factor, wb = call(
        "scales",
        scale_body,
        [shape((quarter, BLOCK), F32), shape(blocks.shape)],
        [place_arr, scale_table, scale_index.reshape(GROUP, quarter), blocks],
        specs={0: SMEM, 1: SMEM},
    )

    saves = {c: {} for c in chunks}

    def middle(c, s, v, other, quarters):
        wide = v.shape[1] != BLOCK
        cols = col(c) if wide else slice(None)

        def body(place_ref, v_ref, o_ref, w_ref, trig_ref, *outs):
            co, si = cs(trig_ref, s, c)
            w = w_ref[s + 1, col(c), :]
            z = place_of(place_ref)
            for m in range(GROUP):
                start = quarter_at(z, m) if quarters else m * quarter
                for r in range(0, quarter, tile):
                    at = pl.ds(start + r, tile)
                    u = (
                        co * v_ref[at, cols].astype(F32) + si * o_ref[at, cols].astype(F32)
                    ).astype(BF)
                    v_new = dot(u, w).astype(BF)
                    if quarters:
                        outs[m][r : r + tile, :] = v_new
                    else:
                        outs[0][at, :] = v_new

        outs = [shape((quarter, BLOCK))] * GROUP if quarters else [shape((rows, BLOCK))]
        return call(
            f"forward{s + 1}_chunk{c}",
            body,
            outs,
            [place_arr, v, other, wb, trig],
            specs={0: SMEM},
            flops=product,
        )

    def with_weights(mine):
        def body(m_ref, p_ref, out):
            for r in range(0, quarter, tile):
                at = pl.ds(r, tile)
                out[at, :] = m_ref[at, :]
            for c in chunks:
                out[quarter + c * BLOCK : quarter + (c + 1) * BLOCK, :] = p_ref[base:, col(c)]

        return call(
            "near", body, [shape((quarter + nb * BLOCK, BLOCK))], [mine, packs[GROUP - 2]]
        )[0]

    middles = list(range(local_bits, third))
    state = {c: (v_first, other_first) for c in chunks}
    for s in middles:
        for c in chunks:
            v, other = state[c]
            if s + 1 == third and c == chunks[0]:
                other, packs[1] = lax.optimization_barrier((other, packs[1]))
            out = middle(c, s, v, other, s + 1 == third)
            saves[c][s] = (v, other)
            if s + 1 < third:
                state[c] = (out[0], swapped(out[0], "dim", 1 << (s + 1 - local_bits)))
            else:
                if c == chunks[0]:
                    out[1] = with_weights(out[1])
                got = {m: swapped(out[m], "dim", m << shift) for m in order[:-1]}
                got[0] = out[0]
                state[c] = [got[m] for m in order]
                if c == chunks[0]:
                    relayed = got[1]

    def group_stage(c, earlier):
        final = c == chunks[-1]

        def body(*refs):
            a_refs, p_refs = placed(refs[:GROUP]), placed(refs[GROUP : 2 * GROUP])
            f_ref, far_ref = refs[2 * GROUP], refs[2 * GROUP + 1]
            e_refs = refs[2 * GROUP + 2 : 2 * GROUP + 2 + len(earlier)]
            refs = refs[2 * GROUP + 2 + len(earlier) :]
            outs, grad_refs = refs[:GROUP], refs[GROUP:]
            coef, w = [], []
            for m in range(GROUP):
                t = p_refs[m][quarter:base, col(c)].astype(F32)
                coef.append(
                    [t[3 * k : 3 * k + 1] + t[3 * k + 1 : 3 * k + 2] + t[3 * k + 2 : 3 * k + 3] for k in range(4)]
                )
                w.append(p_refs[m][base:, col(c)] if highs[m] > base else far_ref[quarter + c * BLOCK : quarter + (c + 1) * BLOCK, :])
            gw = [jnp.zeros((BLOCK, BLOCK), F32)] * GROUP
            ga = [[jnp.zeros((1, BLOCK), F32)] * GROUP for _ in range(2)]
            every = range(GROUP)
            for r in range(0, quarter, tile):
                at = pl.ds(r, tile)
                a = [a_refs[m][at, :].astype(F32) for m in every]
                u = [(coef[m][0] * a[m] + coef[m][1] * a[m ^ 1]).astype(BF) for m in every]
                v = [dot(u[m], w[m]).astype(BF).astype(F32) for m in every]
                f = f_ref[at, :]
                g = []
                for m in every:
                    end = (coef[m][2] * v[m] + coef[m][3] * v[m ^ 2]).astype(BF).astype(F32)
                    recon = f * (p_refs[m][at, col(c)].astype(F32) - 7.5)
                    g.append(((end - recon) * inv).astype(BF).astype(F32))
                for m in every:
                    ga[0][m] = ga[0][m] + jnp.sum(
                        g[m] * (coef[m][2] * v[m ^ 2] - coef[m][3] * v[m]), axis=0, keepdims=True
                    )
                q = [(coef[m][3] * g[m]).astype(BF).astype(F32) for m in every]
                dv = [(coef[m][2] * g[m] + q[m ^ 2]).astype(BF) for m in every]
                g = []
                for m in every:
                    gw[m] = gw[m] + t_dot(u[m], dv[m])
                    g.append(dot_t(dv[m], w[m]).astype(BF).astype(F32))
                for m in every:
                    ga[1][m] = ga[1][m] + jnp.sum(
                        g[m] * (coef[m][0] * a[m ^ 1] - coef[m][1] * a[m]), axis=0, keepdims=True
                    )
                q = [(coef[m][1] * g[m]).astype(BF).astype(F32) for m in every]
                for m in every:
                    outs[m][at, :] = (coef[m][0] * g[m] + q[m ^ 1]).astype(BF)
            for m in every:
                if final:
                    out = grad_refs[m]
                    if m:
                        for k in range(len(earlier)):
                            for h in range(0, grad_rows, 16):
                                out[k, h : h + 16, :] = e_refs[k][m, h : h + 16, :]
                    out = out.at[c] if m else out
                else:
                    out = grad_refs[0].at[m]
                matrix, lines = pack_grad(gw[m], [ga[0][m], ga[1][m]])
                out[:BLOCK, :] = matrix
                out[BLOCK:, :] = lines

        grads = (
            [shape((grad_rows, BLOCK))] + [shape((nb, grad_rows, BLOCK))] * (GROUP - 1)
            if final
            else [shape((GROUP, grad_rows, BLOCK))]
        )
        return call(
            f"group_chunk{c}",
            body,
            [shape((quarter, BLOCK))] * GROUP + grads,
            state[c] + [packs[m] for m in order] + [factor, relayed] + earlier,
            flops=3 * product,
        )

    returned, partial = {}, []
    for c in chunks:
        out = group_stage(c, list(partial))
        if c > 0:
            out[2], out[3], _ = lax.optimization_barrier((out[2], out[3], returned[c - 1][2]))
        returned[c] = {m: swapped(out[m], "dim", m << shift) for m in order[:-1]}
        returned[c][0] = out[0]
        partial.append(out[GROUP])
    sums = out[GROUP + 1 :]

    def write_grad(out, gw, ga):
        out[:BLOCK, :] = gw
        out[BLOCK:, :] = stack_lines([ga], EXTRA)

    grad_shape = shape((grad_rows, BLOCK), F32)

    def back(c, s, load, v, other, w_ref, trig_ref, spans, g_out, q_out, grad, packing=False):
        cols = col(c) if v.shape[1] != BLOCK else slice(None)
        w = w_ref[s, col(c), :]
        co, si = cs(trig_ref, s - 1, c)
        gw = jnp.zeros((BLOCK, BLOCK), F32)
        ga = jnp.zeros((1, BLOCK), F32)
        for m, start in enumerate(spans):
            for r in range(0, quarter, tile):
                at = pl.ds(start + r, tile)
                d = load(m, r, at)
                mine, theirs = v[at, cols].astype(F32), other[at, cols].astype(F32)
                gw = gw + t_dot((co * mine + si * theirs).astype(BF), d)
                g16 = dot_t(d, w).astype(BF)
                g = g16.astype(F32)
                g_out[at, :] = g16
                ga = ga + jnp.sum(g * (co * theirs - si * mine), axis=0, keepdims=True)
                q_out[at, :] = (si * g).astype(BF)
        if packing:
            grad[:BLOCK, :], grad[BLOCK:, :] = pack_grad(gw, [ga])
        else:
            write_grad(grad, gw, ga)

    def back_quarters(c, s):
        v, other = saves[c][s - 1]

        def body(place_ref, *refs):
            d_refs = placed(refs[:GROUP])
            v_ref, o_ref, w_ref, trig_ref, g_out, q_out, grad = refs[GROUP:]
            spans = [quarter_at(place_of(place_ref), m) for m in range(GROUP)]

            def load(m, r, at):
                return d_refs[m][r : r + tile, :]

            back(c, s, load, v_ref, o_ref, w_ref, trig_ref, spans, g_out, q_out, grad)

        return call(
            f"backward{s}_chunk{c}",
            body,
            [shape((rows, BLOCK)), shape((rows, BLOCK)), grad_shape],
            [place_arr] + [returned[c][m] for m in order] + [v, other, wb, trig],
            specs={0: SMEM},
            flops=2 * product,
        )

    uppers = [(s, c) for s in range(early, third + 1) for c in chunks]
    upper_shape = shape(((sections - early) * nb - 1, grad_rows, BLOCK))

    def gather_uppers(owns, others, given, out):
        for k, grad in enumerate(given):
            matrix, lines = pack_grad(grad[:BLOCK, :], [grad[BLOCK : BLOCK + 1, :]])
            out[k, :BLOCK, :] = matrix
            out[k, BLOCK:, :] = lines
        base_at = len(uppers) - 1
        for c in chunks:
            own = owns[c] if c == chunks[-1] else owns[c].at[0]
            total = own[:BLOCK, :].astype(F32)
            tail = own[BLOCK:, :].astype(F32)
            for other in others:
                total = total + other[c, :BLOCK, :].astype(F32)
                tail = tail + other[c, BLOCK:, :].astype(F32)
            matrix, lines = pack_grad(total, [unpack_line(tail, 0), unpack_line(tail, 1)])
            out[base_at + c, :BLOCK, :] = matrix
            out[base_at + c, BLOCK:, :] = lines

    def upper_body(*refs):
        owns, others = refs[:nb], refs[nb : nb + GROUP - 1]
        gather_uppers(owns, others, refs[nb + GROUP - 1 : -1], refs[-1])

    def back_middle(c, s, g, incoming, ending):
        v, other = saves[c][s - 1]

        def body(g_ref, i_ref, v_ref, o_ref, w_ref, trig_ref, g_out, q_out, grad):
            here = cs(trig_ref, s, c)[0]
            spans = [m * quarter for m in range(GROUP)]

            def load(m, r, at):
                return (here * g_ref[at, :].astype(F32) + i_ref[at, :].astype(F32)).astype(BF)

            back(c, s, load, v_ref, o_ref, w_ref, trig_ref, spans, g_out, q_out, grad, ending)

        return call(
            f"backward{s}_chunk{c}",
            body,
            [shape((rows, BLOCK)), shape((rows, BLOCK))]
            + [shape((grad_rows, BLOCK)) if ending else grad_shape],
            [g, incoming, v, other, wb, trig],
            flops=2 * product,
        )

    grads = {c: {} for c in chunks}
    flow = {}
    for c in chunks:
        g, q, grads[c][third] = back_quarters(c, third)
        flow[c] = (g, swapped(q, "dim", 1 << (third - 1 - local_bits)))
    sums, q = lax.optimization_barrier((sums, q))
    arrived = [swapped(sums[m - 1], "dim", m << shift) for m in order[:-1]]
    for s in reversed(middles[1:]):
        for c in chunks:
            ending = s == middles[1] and c == chunks[-1]
            g, incoming = flow[c]
            if ending:
                given = [grads[e][t] for t, e in uppers if (t, e) != (s, c)]
                (upper,) = call("uppers", upper_body, [upper_shape], partial + arrived + given)
                incoming, upper = lax.optimization_barrier((incoming, upper))
            g, q, grads[c][s] = back_middle(c, s, g, incoming, ending)
            flow[c] = (g, swapped(q, "dim", 1 << (s - 1 - local_bits)))
    late = grads[chunks[-1]][middles[1]]
    late_at = uppers.index((middles[1], chunks[-1]))

    def end_body(*refs):
        g_refs, i_refs = refs[:nb], refs[nb : 2 * nb]
        u_ref, w_ref, trig_ref, late_ref, grad, u_held, d_held = refs[2 * nb :]
        grad[early * nb] = late_ref[...]
        ga = [[jnp.zeros((1, BLOCK), F32)] * nb for _ in range(early)]
        w = [[w_ref[s, col(c), :] for c in chunks] for s in range(early)]
        for r in range(0, rows, tile):
            at = pl.ds(r, tile)
            steps, u = forward([u_ref[at, col(c)] for c in chunks], w, trig_ref)
            inputs = [u for u, _ in steps] + [u]
            d = []
            for c in chunks:
                here = cs(trig_ref, local_bits, c)[0]
                d.append(
                    (here * g_refs[c][at, :].astype(F32) + i_refs[c][at, :].astype(F32)).astype(BF)
                )
            for s in reversed(range(early)):
                for c in chunks:
                    d_held[s, at, col(c)] = d[c]
                    if s:
                        u_held[s - 1, at, col(c)] = inputs[s][c]
                if s == 0:
                    break
                g = [dot_t(d[c], w[s][c]).astype(BF).astype(F32) for c in chunks]
                t = s - 1
                v = [x.astype(F32) for x in steps[t][1]]
                q = []
                for c in chunks:
                    co, si = cs(trig_ref, t, c)
                    ga[t][c] = ga[t][c] + jnp.sum(
                        g[c] * (co * v[c ^ (1 << t)] - si * v[c]), axis=0, keepdims=True
                    )
                    q.append((si * g[c]).astype(BF).astype(F32))
                d = [
                    (cs(trig_ref, t, c)[0] * g[c] + q[c ^ (1 << t)]).astype(BF) for c in chunks
                ]
        for s in range(early):
            for c in chunks:
                left = u_held[s - 1, :, col(c)] if s else u_ref[:, col(c)]
                matrix, lines = pack_grad(t_dot(left, d_held[s, :, col(c)]), [ga[s][c]])
                grad[s * nb + c, :BLOCK, :] = matrix
                grad[s * nb + c, BLOCK:, :] = lines

    (ends,) = call(
        "end",
        end_body,
        [shape((early * nb + 1, grad_rows, BLOCK))],
        [flow[c][0] for c in chunks]
        + [flow[c][1] for c in chunks]
        + [vectors, wb, trig, late],
        scratch=[pltpu.VMEM((local_bits, rows, width), BF), pltpu.VMEM((early, rows, width), BF)],
        flops=6 * product,
    )

    if nrow == 2:
        pairs = [(x, swapped(x, "row", 1)) for x in (ends, upper)]
    else:
        pairs = [lax.psum(x.astype(F32), "row") for x in (ends, upper)]
        pairs = [(p, jnp.zeros_like(p)) for p in pairs]

    def final_body(place_ref, e0, e1, p0, p1, bs_ref, as_ref, step, new, step_a, new_a):
        def get(s, c):
            k = s * nb + c
            if s < early:
                a, b = e0.at[k], e1.at[k]
            elif k - early * nb == late_at:
                a, b = e0.at[early * nb], e1.at[early * nb]
            else:
                k -= early * nb
                k -= k > late_at
                a, b = p0.at[k], p1.at[k]
            matrix = a[:BLOCK, :].astype(F32) + b[:BLOCK, :].astype(F32)
            return matrix, a[BLOCK:, :].astype(F32) + b[BLOCK:, :].astype(F32)

        sign = signs(place_ref)
        for c in chunks:
            angle = [None] * sections
            for s in range(sections):
                g, lines = get(s, c)
                state_new = 0.9 * bs_ref[s, col(c), :] + 0.1 * g * g
                new[s, col(c), :] = state_new
                step[s, col(c), :] = g * lax.rsqrt(state_new)
                if s == last:
                    angle[last], angle[third] = unpack_line(lines, 0), unpack_line(lines, 1)
                elif s >= early:
                    angle[s - 1] = unpack_line(lines, 0)
                elif s < local_bits:
                    angle[s] = unpack_line(lines, 0)
            g = jnp.concatenate(angle, axis=0) * sign[:, col(c)]
            state_new = 0.9 * as_ref[:, col(c)] + 0.1 * g * g
            new_a[:, col(c)] = state_new
            step_a[:, col(c)] = g * lax.rsqrt(state_new)

    step, new, step_a, new_a = call(
        "final",
        final_body,
        [shape(block_state.shape, F32)] * 2 + [shape(angle_state.shape, F32)] * 2,
        [place_arr, *pairs[0], *pairs[1], block_state, angle_state],
        specs={0: SMEM},
    )
    return step, new, step_a, new_a


def solution(mesh):
    in_specs = (
        P("row", "dim"),
        P(None, "dim", None),
        P(None, "dim"),
        P("row", "dim"),
        P("row"),
        P(),
        P(None, "dim", None),
        P(None, "dim"),
    )
    out_specs = (P(None, "dim", None), P(None, "dim", None), P(None, "dim"), P(None, "dim"))
    return jax.shard_map(local, mesh=mesh, in_specs=in_specs, out_specs=out_specs, check_vma=False)
```

```python
import math

import jax
import jax.numpy as jnp
from jax import lax
from jax.experimental import pallas as pl
from jax.experimental.pallas import tpu as pltpu
from jax.sharding import PartitionSpec as P

BLOCK = 128
GROUP = 4
EXTRA = 16
TRIG = 16
OPEN_LIMIT = 58
BF = jnp.bfloat16
F32 = jnp.float32


def swapped(value, axis, mask):
    pairs = [(source, source ^ mask) for source in range(lax.axis_size(axis))]
    return lax.ppermute(value, axis, pairs)


def dot(a, b):
    return lax.dot_general(a, b, (((1,), (0,)), ((), ())), preferred_element_type=F32)


def dot_t(a, b):
    return lax.dot_general(a, b, (((1,), (1,)), ((), ())), preferred_element_type=F32)


def t_dot(a, b):
    return lax.dot_general(a, b, (((0,), (0,)), ((), ())), preferred_element_type=F32)


def tile_of(rows):
    best = 16
    for size in range(16, 257, 16):
        if rows % size == 0:
            best = size
    return best


def call(name, body, outs, args, specs=None, scratch=(), flops=0, weight=1, limit=16):
    whole = [pl.BlockSpec(a.shape, lambda i, n=a.ndim: (0,) * n) for a in args]
    for at, spec in (specs or {}).items():
        whole[at] = spec
    moved = sum(math.prod(a.shape) * a.dtype.itemsize for a in args) + sum(
        math.prod(o.shape) * o.dtype.itemsize for o in outs
    )
    return list(
        pl.pallas_call(
            body,
            grid=(1,),
            in_specs=whole,
            out_specs=[pl.BlockSpec(o.shape, lambda i, n=len(o.shape): (0,) * n) for o in outs],
            out_shape=outs,
            scratch_shapes=list(scratch),
            compiler_params=pltpu.CompilerParams(vmem_limit_bytes=limit * 2**20),
            cost_estimate=pl.CostEstimate(
                flops=int(flops * weight * 100), bytes_accessed=int(moved * weight * 20), transcendentals=0
            ),
            name=name,
        )(*args)
    )


def shape(dims, dtype=BF):
    return jax.ShapeDtypeStruct(dims, dtype)


SMEM = pl.BlockSpec(memory_space=pltpu.SMEM)
HBM = pl.BlockSpec(memory_space=pltpu.HBM)


def split3(x):
    hi = x.astype(BF)
    rest = x - hi.astype(F32)
    mid = rest.astype(BF)
    low = (rest - mid.astype(F32)).astype(BF)
    return [hi, mid, low]


def stack_lines(lines, height):
    lines = [x.astype(F32) for x in lines]
    lines.append(jnp.zeros((height - len(lines), lines[0].shape[1]), F32))
    return jnp.concatenate(lines, axis=0)


def pack_grad(matrix, lines):
    parts = []
    for line in lines:
        parts += split3(line)[:2]
    return matrix.astype(BF), stack_lines(parts, EXTRA).astype(BF)


def unpack_line(tile, k):
    return tile[2 * k : 2 * k + 1] + tile[2 * k + 1 : 2 * k + 2]


def local(vectors, blocks, angles, codes, scale_index, scale_table, block_state, angle_state):
    rows, width = vectors.shape
    sections = blocks.shape[0]
    nb = width // BLOCK
    chunks = list(range(nb))
    local_bits = nb.bit_length() - 1
    shift = sections - 2 - local_bits
    quarter = rows // GROUP
    nrow = lax.axis_size("row")
    inv = 1.0 / math.sqrt(rows * nrow)
    tile = tile_of(quarter)
    device = lax.axis_index("dim")
    place_arr = device.astype(jnp.int32).reshape(1)
    last, third = sections - 1, sections - 2
    product = rows * BLOCK * BLOCK * 2
    grad_rows = BLOCK + EXTRA

    def signs(place_ref):
        dims = (sections, width)
        ids = place_ref[0] * nb + lax.broadcasted_iota(jnp.int32, dims, 1) // BLOCK
        bits = lax.shift_right_logical(ids, lax.broadcasted_iota(jnp.int32, dims, 0)) & 1
        return 1.0 - 2.0 * bits.astype(F32)

    def col(c):
        return slice(c * BLOCK, (c + 1) * BLOCK)

    def cs(ref, s, c):
        return ref[s : s + 1, col(c)], ref[sections + s : sections + s + 1, col(c)]

    def place_of(place_ref):
        return lax.shift_right_logical(place_ref[0], shift) & (GROUP - 1)

    def quarter_at(z, m):
        return pl.multiple_of(jnp.bitwise_xor(z, m) * quarter, 16)

    order = [2, 3, 1, 0]
    early = local_bits + 1
    base = quarter + TRIG
    highs = [base + (0 if m == GROUP - 1 else BLOCK) for m in range(GROUP)]

    def placed(refs):
        return [refs[order.index(m)] for m in range(GROUP)]

    def forward(u, weights, trig_ref):
        steps = []
        for s in range(local_bits):
            v = [dot(u[c], weights[s][c]).astype(BF) for c in chunks]
            steps.append((u, v))
            turned = []
            for c in chunks:
                co, si = cs(trig_ref, s, c)
                turned.append(
                    (co * v[c].astype(F32) + si * v[c ^ (1 << s)].astype(F32)).astype(BF)
                )
            u = turned
        return steps, u

    def pack_body(place_ref, w_hbm, codes_hbm, angle_hbm, *rest):
        p_out, trig_out = rest[:GROUP], rest[GROUP]
        w_held, c_held, a_held, w_sem, c_sems, a_sem = rest[GROUP + 1 :]
        z = place_of(place_ref)
        a_in = pltpu.make_async_copy(angle_hbm, a_held, a_sem)
        w_in = pltpu.make_async_copy(w_hbm.at[last], w_held, w_sem)
        c_in = [
            pltpu.make_async_copy(
                codes_hbm.at[pl.ds(quarter_at(z, m), quarter)], c_held.at[m], c_sems.at[m]
            )
            for m in range(GROUP)
        ]
        a_in.start()
        w_in.start()
        for m in order:
            c_in[m].start()
        a_in.wait()
        angle = a_held[...]
        co, si = jnp.cos(angle), signs(place_ref) * jnp.sin(angle)
        trig_out[...] = jnp.concatenate([co, si], axis=0)
        lines = []
        for s in (third, last):
            lines += split3(co[s : s + 1]) + split3(si[s : s + 1])
        lines = stack_lines(lines, TRIG).astype(BF)
        w_in.wait()
        for m in order:
            p_out[m][quarter:base, :] = lines
            if highs[m] > base:
                for c in chunks:
                    p_out[m][base:, col(c)] = w_held[col(c), :].astype(BF)
            c_in[m].wait()
            for r in range(0, quarter, tile):
                at = pl.ds(r, tile)
                p_out[m][at, :] = c_held[m, at, :].astype(F32).astype(BF)

    packed = call(
        "pack",
        pack_body,
        [shape((high, width)) for high in highs] + [shape((2 * sections, width), F32)],
        [place_arr, blocks, codes, angles],
        specs={0: SMEM, 1: HBM, 2: HBM, 3: HBM},
        scratch=[
            pltpu.VMEM((width, BLOCK), F32),
            pltpu.VMEM((GROUP, quarter, width), jnp.int32),
            pltpu.VMEM(angles.shape, F32),
            pltpu.SemaphoreType.DMA,
            pltpu.SemaphoreType.DMA((GROUP,)),
            pltpu.SemaphoreType.DMA,
        ],
        limit=OPEN_LIMIT,
    )
    trig = packed.pop()
    packs = {m: swapped(packed[m], "dim", m << shift) for m in order[:-1]}
    packs[0] = packed[0]

    def first_body(place_ref, u_ref, w_ref, angle_ref, v_out, trig_ref):
        angle = angle_ref[...]
        trig_ref[...] = jnp.concatenate(
            [jnp.cos(angle), signs(place_ref) * jnp.sin(angle)], axis=0
        )
        weights = [[w_ref[s, col(c), :].astype(BF) for c in chunks] for s in range(early)]
        for r in range(0, rows, tile):
            at = pl.ds(r, tile)
            u = forward([u_ref[at, col(c)] for c in chunks], weights, trig_ref)[1]
            for c in chunks:
                v_out[at, col(c)] = dot(u[c], weights[local_bits][c]).astype(BF)

    (v_first,) = call(
        "first",
        first_body,
        [shape((rows, width))],
        [place_arr, vectors, blocks, lax.optimization_barrier((angles, trig))[0]],
        specs={0: SMEM},
        scratch=[pltpu.VMEM((2 * sections, width), F32)],
        flops=rows * width * BLOCK * 4,
    )
    other_first = swapped(v_first, "dim", 1)

    def scale_body(place_ref, table_ref, index_ref, w_ref, out, wb_out):
        for s in range(sections):
            wb_out[s] = w_ref[s].astype(BF)
        index = index_ref[pl.ds(place_of(place_ref), 1), :]
        values = jnp.zeros(index.shape, F32)
        for level in range(table_ref.shape[0]):
            values = jnp.where(index == level, table_ref[level], values)
        parts = stack_lines(split3(values), 16).astype(BF)
        out[...] = t_dot(parts, jnp.ones((16, BLOCK), BF))

    factor, wb = call(
        "scales",
        scale_body,
        [shape((quarter, BLOCK), F32), shape(blocks.shape)],
        [place_arr, scale_table, scale_index.reshape(GROUP, quarter), blocks],
        specs={0: SMEM, 1: SMEM},
    )

    saves = {c: {} for c in chunks}

    def middle(c, s, v, other, quarters):
        wide = v.shape[1] != BLOCK
        cols = col(c) if wide else slice(None)

        def body(place_ref, v_ref, o_ref, w_ref, trig_ref, *outs):
            co, si = cs(trig_ref, s, c)
            w = w_ref[s + 1, col(c), :]
            z = place_of(place_ref)
            for m in range(GROUP):
                start = quarter_at(z, m) if quarters else m * quarter
                for r in range(0, quarter, tile):
                    at = pl.ds(start + r, tile)
                    u = (
                        co * v_ref[at, cols].astype(F32) + si * o_ref[at, cols].astype(F32)
                    ).astype(BF)
                    v_new = dot(u, w).astype(BF)
                    if quarters:
                        outs[m][r : r + tile, :] = v_new
                    else:
                        outs[0][at, :] = v_new

        outs = [shape((quarter, BLOCK))] * GROUP if quarters else [shape((rows, BLOCK))]
        return call(
            f"forward{s + 1}_chunk{c}",
            body,
            outs,
            [place_arr, v, other, wb, trig],
            specs={0: SMEM},
            flops=product,
        )

    def with_weights(mine):
        def body(m_ref, p_ref, out):
            for r in range(0, quarter, tile):
                at = pl.ds(r, tile)
                out[at, :] = m_ref[at, :]
            for c in chunks:
                out[quarter + c * BLOCK : quarter + (c + 1) * BLOCK, :] = p_ref[base:, col(c)]

        return call(
            "near", body, [shape((quarter + nb * BLOCK, BLOCK))], [mine, packs[GROUP - 2]]
        )[0]

    middles = list(range(local_bits, third))
    state = {c: (v_first, other_first) for c in chunks}
    for s in middles:
        for c in chunks:
            v, other = state[c]
            if s + 1 == third and c == chunks[0]:
                other, packs[1] = lax.optimization_barrier((other, packs[1]))
            out = middle(c, s, v, other, s + 1 == third)
            saves[c][s] = (v, other)
            if s + 1 < third:
                state[c] = (out[0], swapped(out[0], "dim", 1 << (s + 1 - local_bits)))
            else:
                if c == chunks[0]:
                    out[1] = with_weights(out[1])
                got = {m: swapped(out[m], "dim", m << shift) for m in order[:-1]}
                got[0] = out[0]
                state[c] = [got[m] for m in order]
                if c == chunks[0]:
                    relayed = got[1]

    def group_stage(c, earlier):
        final = c == chunks[-1]

        def body(*refs):
            a_refs, p_refs = placed(refs[:GROUP]), placed(refs[GROUP : 2 * GROUP])
            f_ref, far_ref = refs[2 * GROUP], refs[2 * GROUP + 1]
            e_refs = refs[2 * GROUP + 2 : 2 * GROUP + 2 + len(earlier)]
            refs = refs[2 * GROUP + 2 + len(earlier) :]
            outs, grad_refs = refs[:GROUP], refs[GROUP:]
            coef, w = [], []
            for m in range(GROUP):
                t = p_refs[m][quarter:base, col(c)].astype(F32)
                coef.append(
                    [t[3 * k : 3 * k + 1] + t[3 * k + 1 : 3 * k + 2] + t[3 * k + 2 : 3 * k + 3] for k in range(4)]
                )
                w.append(p_refs[m][base:, col(c)] if highs[m] > base else far_ref[quarter + c * BLOCK : quarter + (c + 1) * BLOCK, :])
            gw = [jnp.zeros((BLOCK, BLOCK), F32)] * GROUP
            ga = [[jnp.zeros((1, BLOCK), F32)] * GROUP for _ in range(2)]
            every = range(GROUP)
            for r in range(0, quarter, tile):
                at = pl.ds(r, tile)
                a = [a_refs[m][at, :].astype(F32) for m in every]
                u = [(coef[m][0] * a[m] + coef[m][1] * a[m ^ 1]).astype(BF) for m in every]
                v = [dot(u[m], w[m]).astype(BF).astype(F32) for m in every]
                f = f_ref[at, :]
                g = []
                for m in every:
                    end = (coef[m][2] * v[m] + coef[m][3] * v[m ^ 2]).astype(BF).astype(F32)
                    recon = f * (p_refs[m][at, col(c)].astype(F32) - 7.5)
                    g.append(((end - recon) * inv).astype(BF).astype(F32))
                for m in every:
                    ga[0][m] = ga[0][m] + jnp.sum(
                        g[m] * (coef[m][2] * v[m ^ 2] - coef[m][3] * v[m]), axis=0, keepdims=True
                    )
                q = [(coef[m][3] * g[m]).astype(BF).astype(F32) for m in every]
                dv = [(coef[m][2] * g[m] + q[m ^ 2]).astype(BF) for m in every]
                g = []
                for m in every:
                    gw[m] = gw[m] + t_dot(u[m], dv[m])
                    g.append(dot_t(dv[m], w[m]).astype(BF).astype(F32))
                for m in every:
                    ga[1][m] = ga[1][m] + jnp.sum(
                        g[m] * (coef[m][0] * a[m ^ 1] - coef[m][1] * a[m]), axis=0, keepdims=True
                    )
                q = [(coef[m][1] * g[m]).astype(BF).astype(F32) for m in every]
                for m in every:
                    outs[m][at, :] = (coef[m][0] * g[m] + q[m ^ 1]).astype(BF)
            for m in every:
                if final:
                    out = grad_refs[m]
                    if m:
                        for k in range(len(earlier)):
                            for h in range(0, grad_rows, 16):
                                out[k, h : h + 16, :] = e_refs[k][m, h : h + 16, :]
                    out = out.at[c] if m else out
                else:
                    out = grad_refs[0].at[m]
                matrix, lines = pack_grad(gw[m], [ga[0][m], ga[1][m]])
                out[:BLOCK, :] = matrix
                out[BLOCK:, :] = lines

        grads = (
            [shape((grad_rows, BLOCK))] + [shape((nb, grad_rows, BLOCK))] * (GROUP - 1)
            if final
            else [shape((GROUP, grad_rows, BLOCK))]
        )
        return call(
            f"group_chunk{c}",
            body,
            [shape((quarter, BLOCK))] * GROUP + grads,
            state[c] + [packs[m] for m in order] + [factor, relayed] + earlier,
            flops=3 * product,
        )

    returned, partial = {}, []
    for c in chunks:
        out = group_stage(c, list(partial))
        if c > 0:
            out[3], _ = lax.optimization_barrier((out[3], returned[c - 1][2]))
        returned[c] = {m: swapped(out[m], "dim", m << shift) for m in order[:-1]}
        returned[c][0] = out[0]
        partial.append(out[GROUP])
    sums = out[GROUP + 1 :]

    def write_grad(out, gw, ga):
        out[:BLOCK, :] = gw
        out[BLOCK:, :] = stack_lines([ga], EXTRA)

    grad_shape = shape((grad_rows, BLOCK), F32)

    def back(c, s, load, v, other, w_ref, trig_ref, spans, g_out, q_out, grad, packing=False):
        cols = col(c) if v.shape[1] != BLOCK else slice(None)
        w = w_ref[s, col(c), :]
        co, si = cs(trig_ref, s - 1, c)
        gw = jnp.zeros((BLOCK, BLOCK), F32)
        ga = jnp.zeros((1, BLOCK), F32)
        for m, start in enumerate(spans):
            for r in range(0, quarter, tile):
                at = pl.ds(start + r, tile)
                d = load(m, r, at)
                mine, theirs = v[at, cols].astype(F32), other[at, cols].astype(F32)
                gw = gw + t_dot((co * mine + si * theirs).astype(BF), d)
                g16 = dot_t(d, w).astype(BF)
                g = g16.astype(F32)
                g_out[at, :] = g16
                ga = ga + jnp.sum(g * (co * theirs - si * mine), axis=0, keepdims=True)
                q_out[at, :] = (si * g).astype(BF)
        if packing:
            grad[:BLOCK, :], grad[BLOCK:, :] = pack_grad(gw, [ga])
        else:
            write_grad(grad, gw, ga)

    def back_quarters(c, s):
        v, other = saves[c][s - 1]

        def body(place_ref, *refs):
            d_refs = placed(refs[:GROUP])
            v_ref, o_ref, w_ref, trig_ref, g_out, q_out, grad = refs[GROUP:]
            spans = [quarter_at(place_of(place_ref), m) for m in range(GROUP)]

            def load(m, r, at):
                return d_refs[m][r : r + tile, :]

            back(c, s, load, v_ref, o_ref, w_ref, trig_ref, spans, g_out, q_out, grad)

        return call(
            f"backward{s}_chunk{c}",
            body,
            [shape((rows, BLOCK)), shape((rows, BLOCK)), grad_shape],
            [place_arr] + [returned[c][m] for m in order] + [v, other, wb, trig],
            specs={0: SMEM},
            flops=2 * product,
        )

    uppers = [(s, c) for s in range(early, third + 1) for c in chunks]
    upper_shape = shape(((sections - early) * nb - 1, grad_rows, BLOCK))

    def gather_uppers(owns, others, given, out):
        for k, grad in enumerate(given):
            matrix, lines = pack_grad(grad[:BLOCK, :], [grad[BLOCK : BLOCK + 1, :]])
            out[k, :BLOCK, :] = matrix
            out[k, BLOCK:, :] = lines
        base_at = len(uppers) - 1
        for c in chunks:
            own = owns[c] if c == chunks[-1] else owns[c].at[0]
            total = own[:BLOCK, :].astype(F32)
            tail = own[BLOCK:, :].astype(F32)
            for other in others:
                total = total + other[c, :BLOCK, :].astype(F32)
                tail = tail + other[c, BLOCK:, :].astype(F32)
            matrix, lines = pack_grad(total, [unpack_line(tail, 0), unpack_line(tail, 1)])
            out[base_at + c, :BLOCK, :] = matrix
            out[base_at + c, BLOCK:, :] = lines

    def upper_body(*refs):
        owns, others = refs[:nb], refs[nb : nb + GROUP - 1]
        gather_uppers(owns, others, refs[nb + GROUP - 1 : -1], refs[-1])

    def back_middle(c, s, g, incoming, ending):
        v, other = saves[c][s - 1]

        def body(g_ref, i_ref, v_ref, o_ref, w_ref, trig_ref, g_out, q_out, grad):
            here = cs(trig_ref, s, c)[0]
            spans = [m * quarter for m in range(GROUP)]

            def load(m, r, at):
                return (here * g_ref[at, :].astype(F32) + i_ref[at, :].astype(F32)).astype(BF)

            back(c, s, load, v_ref, o_ref, w_ref, trig_ref, spans, g_out, q_out, grad, ending)

        return call(
            f"backward{s}_chunk{c}",
            body,
            [shape((rows, BLOCK)), shape((rows, BLOCK))]
            + [shape((grad_rows, BLOCK)) if ending else grad_shape],
            [g, incoming, v, other, wb, trig],
            flops=2 * product,
        )

    grads = {c: {} for c in chunks}
    flow = {}
    for c in chunks:
        g, q, grads[c][third] = back_quarters(c, third)
        flow[c] = (g, swapped(q, "dim", 1 << (third - 1 - local_bits)))
    sums, q = lax.optimization_barrier((sums, q))
    arrived = [swapped(sums[m - 1], "dim", m << shift) for m in order[:-1]]
    for s in reversed(middles[1:]):
        for c in chunks:
            ending = s == middles[1] and c == chunks[-1]
            g, incoming = flow[c]
            if ending:
                given = [grads[e][t] for t, e in uppers if (t, e) != (s, c)]
                (upper,) = call("uppers", upper_body, [upper_shape], partial + arrived + given)
                incoming, upper = lax.optimization_barrier((incoming, upper))
            g, q, grads[c][s] = back_middle(c, s, g, incoming, ending)
            flow[c] = (g, swapped(q, "dim", 1 << (s - 1 - local_bits)))
    late = grads[chunks[-1]][middles[1]]
    late_at = uppers.index((middles[1], chunks[-1]))

    def end_body(*refs):
        g_refs, i_refs = refs[:nb], refs[nb : 2 * nb]
        u_ref, w_ref, trig_ref, late_ref, grad, u_held, d_held = refs[2 * nb :]
        grad[early * nb] = late_ref[...]
        ga = [[jnp.zeros((1, BLOCK), F32)] * nb for _ in range(early)]
        w = [[w_ref[s, col(c), :] for c in chunks] for s in range(early)]
        for r in range(0, rows, tile):
            at = pl.ds(r, tile)
            steps, u = forward([u_ref[at, col(c)] for c in chunks], w, trig_ref)
            inputs = [u for u, _ in steps] + [u]
            d = []
            for c in chunks:
                here = cs(trig_ref, local_bits, c)[0]
                d.append(
                    (here * g_refs[c][at, :].astype(F32) + i_refs[c][at, :].astype(F32)).astype(BF)
                )
            for s in reversed(range(early)):
                for c in chunks:
                    d_held[s, at, col(c)] = d[c]
                    if s:
                        u_held[s - 1, at, col(c)] = inputs[s][c]
                if s == 0:
                    break
                g = [dot_t(d[c], w[s][c]).astype(BF).astype(F32) for c in chunks]
                t = s - 1
                v = [x.astype(F32) for x in steps[t][1]]
                q = []
                for c in chunks:
                    co, si = cs(trig_ref, t, c)
                    ga[t][c] = ga[t][c] + jnp.sum(
                        g[c] * (co * v[c ^ (1 << t)] - si * v[c]), axis=0, keepdims=True
                    )
                    q.append((si * g[c]).astype(BF).astype(F32))
                d = [
                    (cs(trig_ref, t, c)[0] * g[c] + q[c ^ (1 << t)]).astype(BF) for c in chunks
                ]
        for s in range(early):
            for c in chunks:
                left = u_held[s - 1, :, col(c)] if s else u_ref[:, col(c)]
                matrix, lines = pack_grad(t_dot(left, d_held[s, :, col(c)]), [ga[s][c]])
                grad[s * nb + c, :BLOCK, :] = matrix
                grad[s * nb + c, BLOCK:, :] = lines

    (ends,) = call(
        "end",
        end_body,
        [shape((early * nb + 1, grad_rows, BLOCK))],
        [flow[c][0] for c in chunks]
        + [flow[c][1] for c in chunks]
        + [vectors, wb, trig, late],
        scratch=[pltpu.VMEM((local_bits, rows, width), BF), pltpu.VMEM((early, rows, width), BF)],
        flops=6 * product,
    )

    if nrow == 2:
        pairs = [(x, swapped(x, "row", 1)) for x in (ends, upper)]
    else:
        pairs = [lax.psum(x.astype(F32), "row") for x in (ends, upper)]
        pairs = [(p, jnp.zeros_like(p)) for p in pairs]

    def final_body(place_ref, e0, e1, p0, p1, bs_ref, as_ref, step, new, step_a, new_a):
        def get(s, c):
            k = s * nb + c
            if s < early:
                a, b = e0.at[k], e1.at[k]
            elif k - early * nb == late_at:
                a, b = e0.at[early * nb], e1.at[early * nb]
            else:
                k -= early * nb
                k -= k > late_at
                a, b = p0.at[k], p1.at[k]
            matrix = a[:BLOCK, :].astype(F32) + b[:BLOCK, :].astype(F32)
            return matrix, a[BLOCK:, :].astype(F32) + b[BLOCK:, :].astype(F32)

        sign = signs(place_ref)
        for c in chunks:
            angle = [None] * sections
            for s in range(sections):
                g, lines = get(s, c)
                state_new = 0.9 * bs_ref[s, col(c), :] + 0.1 * g * g
                new[s, col(c), :] = state_new
                step[s, col(c), :] = g * lax.rsqrt(state_new)
                if s == last:
                    angle[last], angle[third] = unpack_line(lines, 0), unpack_line(lines, 1)
                elif s >= early:
                    angle[s - 1] = unpack_line(lines, 0)
                elif s < local_bits:
                    angle[s] = unpack_line(lines, 0)
            g = jnp.concatenate(angle, axis=0) * sign[:, col(c)]
            state_new = 0.9 * as_ref[:, col(c)] + 0.1 * g * g
            new_a[:, col(c)] = state_new
            step_a[:, col(c)] = g * lax.rsqrt(state_new)

    step, new, step_a, new_a = call(
        "final",
        final_body,
        [shape(block_state.shape, F32)] * 2 + [shape(angle_state.shape, F32)] * 2,
        [place_arr, *pairs[0], *pairs[1], block_state, angle_state],
        specs={0: SMEM},
    )
    return step, new, step_a, new_a


def solution(mesh):
    in_specs = (
        P("row", "dim"),
        P(None, "dim", None),
        P(None, "dim"),
        P("row", "dim"),
        P("row"),
        P(),
        P(None, "dim", None),
        P(None, "dim"),
    )
    out_specs = (P(None, "dim", None), P(None, "dim", None), P(None, "dim"), P(None, "dim"))
    return jax.shard_map(local, mesh=mesh, in_specs=in_specs, out_specs=out_specs, check_vma=False)
```

```python
import math

import jax
import jax.numpy as jnp
from jax import lax
from jax.experimental import pallas as pl
from jax.experimental.pallas import tpu as pltpu
from jax.sharding import PartitionSpec as P

BLOCK = 128
GROUP = 4
EXTRA = 16
TRIG = 16
OPEN_LIMIT = 58
BF = jnp.bfloat16
F32 = jnp.float32


def swapped(value, axis, mask):
    pairs = [(source, source ^ mask) for source in range(lax.axis_size(axis))]
    return lax.ppermute(value, axis, pairs)


def dot(a, b):
    return lax.dot_general(a, b, (((1,), (0,)), ((), ())), preferred_element_type=F32)


def dot_t(a, b):
    return lax.dot_general(a, b, (((1,), (1,)), ((), ())), preferred_element_type=F32)


def t_dot(a, b):
    return lax.dot_general(a, b, (((0,), (0,)), ((), ())), preferred_element_type=F32)


def tile_of(rows):
    best = 16
    for size in range(16, 257, 16):
        if rows % size == 0:
            best = size
    return best


def call(name, body, outs, args, specs=None, scratch=(), flops=0, weight=1, limit=16):
    whole = [pl.BlockSpec(a.shape, lambda i, n=a.ndim: (0,) * n) for a in args]
    for at, spec in (specs or {}).items():
        whole[at] = spec
    moved = sum(math.prod(a.shape) * a.dtype.itemsize for a in args) + sum(
        math.prod(o.shape) * o.dtype.itemsize for o in outs
    )
    return list(
        pl.pallas_call(
            body,
            grid=(1,),
            in_specs=whole,
            out_specs=[pl.BlockSpec(o.shape, lambda i, n=len(o.shape): (0,) * n) for o in outs],
            out_shape=outs,
            scratch_shapes=list(scratch),
            compiler_params=pltpu.CompilerParams(vmem_limit_bytes=limit * 2**20),
            cost_estimate=pl.CostEstimate(
                flops=int(flops * weight * 100), bytes_accessed=int(moved * weight * 20), transcendentals=0
            ),
            name=name,
        )(*args)
    )


def shape(dims, dtype=BF):
    return jax.ShapeDtypeStruct(dims, dtype)


SMEM = pl.BlockSpec(memory_space=pltpu.SMEM)
HBM = pl.BlockSpec(memory_space=pltpu.HBM)


def split3(x):
    hi = x.astype(BF)
    rest = x - hi.astype(F32)
    mid = rest.astype(BF)
    low = (rest - mid.astype(F32)).astype(BF)
    return [hi, mid, low]


def stack_lines(lines, height):
    lines = [x.astype(F32) for x in lines]
    lines.append(jnp.zeros((height - len(lines), lines[0].shape[1]), F32))
    return jnp.concatenate(lines, axis=0)


def pack_grad(matrix, lines):
    parts = []
    for line in lines:
        parts += split3(line)[:2]
    return matrix.astype(BF), stack_lines(parts, EXTRA).astype(BF)


def unpack_line(tile, k):
    return tile[2 * k : 2 * k + 1] + tile[2 * k + 1 : 2 * k + 2]


def local(vectors, blocks, angles, codes, scale_index, scale_table, block_state, angle_state):
    rows, width = vectors.shape
    sections = blocks.shape[0]
    nb = width // BLOCK
    chunks = list(range(nb))
    local_bits = nb.bit_length() - 1
    shift = sections - 2 - local_bits
    quarter = rows // GROUP
    nrow = lax.axis_size("row")
    inv = 1.0 / math.sqrt(rows * nrow)
    tile = tile_of(quarter)
    device = lax.axis_index("dim")
    place_arr = device.astype(jnp.int32).reshape(1)
    last, third = sections - 1, sections - 2
    product = rows * BLOCK * BLOCK * 2
    grad_rows = BLOCK + EXTRA

    def signs(place_ref):
        dims = (sections, width)
        ids = place_ref[0] * nb + lax.broadcasted_iota(jnp.int32, dims, 1) // BLOCK
        bits = lax.shift_right_logical(ids, lax.broadcasted_iota(jnp.int32, dims, 0)) & 1
        return 1.0 - 2.0 * bits.astype(F32)

    def col(c):
        return slice(c * BLOCK, (c + 1) * BLOCK)

    def cs(ref, s, c):
        return ref[s : s + 1, col(c)], ref[sections + s : sections + s + 1, col(c)]

    def place_of(place_ref):
        return lax.shift_right_logical(place_ref[0], shift) & (GROUP - 1)

    def quarter_at(z, m):
        return pl.multiple_of(jnp.bitwise_xor(z, m) * quarter, 16)

    order = [2, 3, 1, 0]
    early = local_bits + 1
    base = quarter + TRIG
    highs = [base + BLOCK] * (GROUP - 1) + [quarter]

    def placed(refs):
        return [refs[order.index(m)] for m in range(GROUP)]

    def forward(u, weights, trig_ref):
        steps = []
        for s in range(local_bits):
            v = [dot(u[c], weights[s][c]).astype(BF) for c in chunks]
            steps.append((u, v))
            turned = []
            for c in chunks:
                co, si = cs(trig_ref, s, c)
                turned.append(
                    (co * v[c].astype(F32) + si * v[c ^ (1 << s)].astype(F32)).astype(BF)
                )
            u = turned
        return steps, u

    def pack_body(place_ref, w_hbm, codes_hbm, angle_hbm, *rest):
        p_out, trig_out = rest[:GROUP], rest[GROUP]
        w_held, c_held, a_held, w_sem, c_sems, a_sem = rest[GROUP + 1 :]
        z = place_of(place_ref)
        a_in = pltpu.make_async_copy(angle_hbm, a_held, a_sem)
        w_in = pltpu.make_async_copy(w_hbm.at[last], w_held, w_sem)
        c_in = [
            pltpu.make_async_copy(
                codes_hbm.at[pl.ds(quarter_at(z, m), quarter)], c_held.at[m], c_sems.at[m]
            )
            for m in range(GROUP)
        ]
        a_in.start()
        w_in.start()
        for m in order:
            c_in[m].start()
        a_in.wait()
        angle = a_held[...]
        co, si = jnp.cos(angle), signs(place_ref) * jnp.sin(angle)
        trig_out[...] = jnp.concatenate([co, si], axis=0)
        lines = []
        for s in (third, last):
            lines += split3(co[s : s + 1]) + split3(si[s : s + 1])
        lines = stack_lines(lines, TRIG).astype(BF)
        w_in.wait()
        for m in order:
            if highs[m] > base:
                p_out[m][quarter:base, :] = lines
                for c in chunks:
                    p_out[m][base:, col(c)] = w_held[col(c), :].astype(BF)
            c_in[m].wait()
            for r in range(0, quarter, tile):
                at = pl.ds(r, tile)
                p_out[m][at, :] = c_held[m, at, :].astype(F32).astype(BF)

    packed = call(
        "pack",
        pack_body,
        [shape((high, width)) for high in highs] + [shape((2 * sections, width), F32)],
        [place_arr, blocks, codes, angles],
        specs={0: SMEM, 1: HBM, 2: HBM, 3: HBM},
        scratch=[
            pltpu.VMEM((width, BLOCK), F32),
            pltpu.VMEM((GROUP, quarter, width), jnp.int32),
            pltpu.VMEM(angles.shape, F32),
            pltpu.SemaphoreType.DMA,
            pltpu.SemaphoreType.DMA((GROUP,)),
            pltpu.SemaphoreType.DMA,
        ],
        limit=OPEN_LIMIT,
    )
    trig = packed.pop()
    packs = {m: swapped(packed[m], "dim", m << shift) for m in order[:-1]}
    packs[0] = packed[0]

    def first_body(place_ref, u_ref, w_ref, angle_ref, v_out, trig_ref):
        angle = angle_ref[...]
        trig_ref[...] = jnp.concatenate(
            [jnp.cos(angle), signs(place_ref) * jnp.sin(angle)], axis=0
        )
        weights = [[w_ref[s, col(c), :].astype(BF) for c in chunks] for s in range(early)]
        for r in range(0, rows, tile):
            at = pl.ds(r, tile)
            u = forward([u_ref[at, col(c)] for c in chunks], weights, trig_ref)[1]
            for c in chunks:
                v_out[at, col(c)] = dot(u[c], weights[local_bits][c]).astype(BF)

    (v_first,) = call(
        "first",
        first_body,
        [shape((rows, width))],
        [place_arr, vectors, blocks, lax.optimization_barrier((angles, trig))[0]],
        specs={0: SMEM},
        scratch=[pltpu.VMEM((2 * sections, width), F32)],
        flops=rows * width * BLOCK * 4,
    )
    other_first = swapped(v_first, "dim", 1)

    def scale_body(place_ref, table_ref, index_ref, w_ref, out, wb_out):
        for s in range(sections):
            wb_out[s] = w_ref[s].astype(BF)
        index = index_ref[pl.ds(place_of(place_ref), 1), :]
        values = jnp.zeros(index.shape, F32)
        for level in range(table_ref.shape[0]):
            values = jnp.where(index == level, table_ref[level], values)
        parts = stack_lines(split3(values), 16).astype(BF)
        out[...] = t_dot(parts, jnp.ones((16, BLOCK), BF))

    factor, wb = call(
        "scales",
        scale_body,
        [shape((quarter, BLOCK), F32), shape(blocks.shape)],
        [place_arr, scale_table, scale_index.reshape(GROUP, quarter), blocks],
        specs={0: SMEM, 1: SMEM},
    )

    saves = {c: {} for c in chunks}

    def middle(c, s, v, other, quarters):
        wide = v.shape[1] != BLOCK
        cols = col(c) if wide else slice(None)

        def body(place_ref, v_ref, o_ref, w_ref, trig_ref, *outs):
            co, si = cs(trig_ref, s, c)
            w = w_ref[s + 1, col(c), :]
            z = place_of(place_ref)
            for m in range(GROUP):
                start = quarter_at(z, m) if quarters else m * quarter
                for r in range(0, quarter, tile):
                    at = pl.ds(start + r, tile)
                    u = (
                        co * v_ref[at, cols].astype(F32) + si * o_ref[at, cols].astype(F32)
                    ).astype(BF)
                    v_new = dot(u, w).astype(BF)
                    if quarters:
                        outs[m][r : r + tile, :] = v_new
                    else:
                        outs[0][at, :] = v_new

        outs = [shape((quarter, BLOCK))] * GROUP if quarters else [shape((rows, BLOCK))]
        return call(
            f"forward{s + 1}_chunk{c}",
            body,
            outs,
            [place_arr, v, other, wb, trig],
            specs={0: SMEM},
            flops=product,
        )

    def with_weights(c, mine):
        def body(m_ref, p_ref, out):
            for r in range(0, quarter, tile):
                at = pl.ds(r, tile)
                out[at, :] = m_ref[at, :]
            out[quarter:, :] = p_ref[quarter:, col(c)]

        return call(
            f"near_chunk{c}", body, [shape((base + BLOCK, BLOCK))], [mine, packs[GROUP - 2]]
        )[0]

    middles = list(range(local_bits, third))
    state = {c: (v_first, other_first) for c in chunks}
    for s in middles:
        for c in chunks:
            v, other = state[c]
            if s + 1 == third and c == chunks[0]:
                other, packs[1] = lax.optimization_barrier((other, packs[1]))
            out = middle(c, s, v, other, s + 1 == third)
            saves[c][s] = (v, other)
            if s + 1 < third:
                state[c] = (out[0], swapped(out[0], "dim", 1 << (s + 1 - local_bits)))
            else:
                out[1] = with_weights(c, out[1])
                got = {m: swapped(out[m], "dim", m << shift) for m in order[:-1]}
                got[0] = out[0]
                state[c] = [got[m] for m in order]

    def group_stage(c, earlier):
        final = c == chunks[-1]

        def body(*refs):
            a_refs, p_refs = placed(refs[:GROUP]), placed(refs[GROUP : 2 * GROUP])
            f_ref = refs[2 * GROUP]
            e_refs = refs[2 * GROUP + 1 : 2 * GROUP + 1 + len(earlier)]
            refs = refs[2 * GROUP + 1 + len(earlier) :]
            outs, grad_refs = refs[:GROUP], refs[GROUP:]
            coef, w = [], []
            for m in range(GROUP):
                far = m == GROUP - 1
                t = (a_refs[1][quarter:base, :] if far else p_refs[m][quarter:base, col(c)]).astype(F32)
                coef.append(
                    [t[3 * k : 3 * k + 1] + t[3 * k + 1 : 3 * k + 2] + t[3 * k + 2 : 3 * k + 3] for k in range(4)]
                )
                w.append(a_refs[1][base:, :] if far else p_refs[m][base:, col(c)])
            gw = [jnp.zeros((BLOCK, BLOCK), F32)] * GROUP
            ga = [[jnp.zeros((1, BLOCK), F32)] * GROUP for _ in range(2)]
            every = range(GROUP)
            for r in range(0, quarter, tile):
                at = pl.ds(r, tile)
                a = [a_refs[m][at, :].astype(F32) for m in every]
                u = [(coef[m][0] * a[m] + coef[m][1] * a[m ^ 1]).astype(BF) for m in every]
                v = [dot(u[m], w[m]).astype(BF).astype(F32) for m in every]
                f = f_ref[at, :]
                g = []
                for m in every:
                    end = (coef[m][2] * v[m] + coef[m][3] * v[m ^ 2]).astype(BF).astype(F32)
                    recon = f * (p_refs[m][at, col(c)].astype(F32) - 7.5)
                    g.append(((end - recon) * inv).astype(BF).astype(F32))
                for m in every:
                    ga[0][m] = ga[0][m] + jnp.sum(
                        g[m] * (coef[m][2] * v[m ^ 2] - coef[m][3] * v[m]), axis=0, keepdims=True
                    )
                q = [(coef[m][3] * g[m]).astype(BF).astype(F32) for m in every]
                dv = [(coef[m][2] * g[m] + q[m ^ 2]).astype(BF) for m in every]
                g = []
                for m in every:
                    gw[m] = gw[m] + t_dot(u[m], dv[m])
                    g.append(dot_t(dv[m], w[m]).astype(BF).astype(F32))
                for m in every:
                    ga[1][m] = ga[1][m] + jnp.sum(
                        g[m] * (coef[m][0] * a[m ^ 1] - coef[m][1] * a[m]), axis=0, keepdims=True
                    )
                q = [(coef[m][1] * g[m]).astype(BF).astype(F32) for m in every]
                for m in every:
                    outs[m][at, :] = (coef[m][0] * g[m] + q[m ^ 1]).astype(BF)
            for m in every:
                if final:
                    out = grad_refs[m]
                    if m:
                        for k in range(len(earlier)):
                            for h in range(0, grad_rows, 16):
                                out[k, h : h + 16, :] = e_refs[k][m, h : h + 16, :]
                    out = out.at[c] if m else out
                else:
                    out = grad_refs[0].at[m]
                matrix, lines = pack_grad(gw[m], [ga[0][m], ga[1][m]])
                out[:BLOCK, :] = matrix
                out[BLOCK:, :] = lines

        grads = (
            [shape((grad_rows, BLOCK))] + [shape((nb, grad_rows, BLOCK))] * (GROUP - 1)
            if final
            else [shape((GROUP, grad_rows, BLOCK))]
        )
        return call(
            f"group_chunk{c}",
            body,
            [shape((quarter, BLOCK))] * GROUP + grads,
            state[c] + [packs[m] for m in order] + [factor] + earlier,
            flops=3 * product,
        )

    returned, partial = {}, []
    for c in chunks:
        out = group_stage(c, list(partial))
        returned[c] = {m: swapped(out[m], "dim", m << shift) for m in order[:-1]}
        returned[c][0] = out[0]
        partial.append(out[GROUP])
    sums = out[GROUP + 1 :]

    def write_grad(out, gw, ga):
        out[:BLOCK, :] = gw
        out[BLOCK:, :] = stack_lines([ga], EXTRA)

    grad_shape = shape((grad_rows, BLOCK), F32)

    def back(c, s, load, v, other, w_ref, trig_ref, spans, g_out, q_out, grad, packing=False):
        cols = col(c) if v.shape[1] != BLOCK else slice(None)
        w = w_ref[s, col(c), :]
        co, si = cs(trig_ref, s - 1, c)
        gw = jnp.zeros((BLOCK, BLOCK), F32)
        ga = jnp.zeros((1, BLOCK), F32)
        for m, start in enumerate(spans):
            for r in range(0, quarter, tile):
                at = pl.ds(start + r, tile)
                d = load(m, r, at)
                mine, theirs = v[at, cols].astype(F32), other[at, cols].astype(F32)
                gw = gw + t_dot((co * mine + si * theirs).astype(BF), d)
                g16 = dot_t(d, w).astype(BF)
                g = g16.astype(F32)
                g_out[at, :] = g16
                ga = ga + jnp.sum(g * (co * theirs - si * mine), axis=0, keepdims=True)
                q_out[at, :] = (si * g).astype(BF)
        if packing:
            grad[:BLOCK, :], grad[BLOCK:, :] = pack_grad(gw, [ga])
        else:
            write_grad(grad, gw, ga)

    def back_quarters(c, s):
        v, other = saves[c][s - 1]

        def body(place_ref, *refs):
            d_refs = placed(refs[:GROUP])
            v_ref, o_ref, w_ref, trig_ref, g_out, q_out, grad = refs[GROUP:]
            spans = [quarter_at(place_of(place_ref), m) for m in range(GROUP)]

            def load(m, r, at):
                return d_refs[m][r : r + tile, :]

            back(c, s, load, v_ref, o_ref, w_ref, trig_ref, spans, g_out, q_out, grad)

        return call(
            f"backward{s}_chunk{c}",
            body,
            [shape((rows, BLOCK)), shape((rows, BLOCK)), grad_shape],
            [place_arr] + [returned[c][m] for m in order] + [v, other, wb, trig],
            specs={0: SMEM},
            flops=2 * product,
        )

    uppers = [(s, c) for s in range(early, third + 1) for c in chunks]
    upper_shape = shape(((sections - early) * nb - 1, grad_rows, BLOCK))

    def gather_uppers(owns, others, given, out):
        for k, grad in enumerate(given):
            matrix, lines = pack_grad(grad[:BLOCK, :], [grad[BLOCK : BLOCK + 1, :]])
            out[k, :BLOCK, :] = matrix
            out[k, BLOCK:, :] = lines
        base_at = len(uppers) - 1
        for c in chunks:
            own = owns[c] if c == chunks[-1] else owns[c].at[0]
            total = own[:BLOCK, :].astype(F32)
            tail = own[BLOCK:, :].astype(F32)
            for other in others:
                total = total + other[c, :BLOCK, :].astype(F32)
                tail = tail + other[c, BLOCK:, :].astype(F32)
            matrix, lines = pack_grad(total, [unpack_line(tail, 0), unpack_line(tail, 1)])
            out[base_at + c, :BLOCK, :] = matrix
            out[base_at + c, BLOCK:, :] = lines

    def upper_body(*refs):
        owns, others = refs[:nb], refs[nb : nb + GROUP - 1]
        gather_uppers(owns, others, refs[nb + GROUP - 1 : -1], refs[-1])

    def back_middle(c, s, g, incoming, ending):
        v, other = saves[c][s - 1]

        def body(g_ref, i_ref, v_ref, o_ref, w_ref, trig_ref, g_out, q_out, grad):
            here = cs(trig_ref, s, c)[0]
            spans = [m * quarter for m in range(GROUP)]

            def load(m, r, at):
                return (here * g_ref[at, :].astype(F32) + i_ref[at, :].astype(F32)).astype(BF)

            back(c, s, load, v_ref, o_ref, w_ref, trig_ref, spans, g_out, q_out, grad, ending)

        return call(
            f"backward{s}_chunk{c}",
            body,
            [shape((rows, BLOCK)), shape((rows, BLOCK))]
            + [shape((grad_rows, BLOCK)) if ending else grad_shape],
            [g, incoming, v, other, wb, trig],
            flops=2 * product,
        )

    grads = {c: {} for c in chunks}
    flow = {}
    for c in chunks:
        g, q, grads[c][third] = back_quarters(c, third)
        flow[c] = (g, swapped(q, "dim", 1 << (third - 1 - local_bits)))
    sums, q = lax.optimization_barrier((sums, q))
    arrived = [swapped(sums[m - 1], "dim", m << shift) for m in order[:-1]]
    for s in reversed(middles[1:]):
        for c in chunks:
            ending = s == middles[1] and c == chunks[-1]
            g, incoming = flow[c]
            if ending:
                given = [grads[e][t] for t, e in uppers if (t, e) != (s, c)]
                (upper,) = call("uppers", upper_body, [upper_shape], partial + arrived + given)
                incoming, upper = lax.optimization_barrier((incoming, upper))
            g, q, grads[c][s] = back_middle(c, s, g, incoming, ending)
            flow[c] = (g, swapped(q, "dim", 1 << (s - 1 - local_bits)))
    late = grads[chunks[-1]][middles[1]]
    late_at = uppers.index((middles[1], chunks[-1]))

    def end_body(*refs):
        g_refs, i_refs = refs[:nb], refs[nb : 2 * nb]
        u_ref, w_ref, trig_ref, late_ref, grad, u_held, d_held = refs[2 * nb :]
        grad[early * nb] = late_ref[...]
        ga = [[jnp.zeros((1, BLOCK), F32)] * nb for _ in range(early)]
        w = [[w_ref[s, col(c), :] for c in chunks] for s in range(early)]
        for r in range(0, rows, tile):
            at = pl.ds(r, tile)
            steps, u = forward([u_ref[at, col(c)] for c in chunks], w, trig_ref)
            inputs = [u for u, _ in steps] + [u]
            d = []
            for c in chunks:
                here = cs(trig_ref, local_bits, c)[0]
                d.append(
                    (here * g_refs[c][at, :].astype(F32) + i_refs[c][at, :].astype(F32)).astype(BF)
                )
            for s in reversed(range(early)):
                for c in chunks:
                    d_held[s, at, col(c)] = d[c]
                    if s:
                        u_held[s - 1, at, col(c)] = inputs[s][c]
                if s == 0:
                    break
                g = [dot_t(d[c], w[s][c]).astype(BF).astype(F32) for c in chunks]
                t = s - 1
                v = [x.astype(F32) for x in steps[t][1]]
                q = []
                for c in chunks:
                    co, si = cs(trig_ref, t, c)
                    ga[t][c] = ga[t][c] + jnp.sum(
                        g[c] * (co * v[c ^ (1 << t)] - si * v[c]), axis=0, keepdims=True
                    )
                    q.append((si * g[c]).astype(BF).astype(F32))
                d = [
                    (cs(trig_ref, t, c)[0] * g[c] + q[c ^ (1 << t)]).astype(BF) for c in chunks
                ]
        for s in range(early):
            for c in chunks:
                left = u_held[s - 1, :, col(c)] if s else u_ref[:, col(c)]
                matrix, lines = pack_grad(t_dot(left, d_held[s, :, col(c)]), [ga[s][c]])
                grad[s * nb + c, :BLOCK, :] = matrix
                grad[s * nb + c, BLOCK:, :] = lines

    (ends,) = call(
        "end",
        end_body,
        [shape((early * nb + 1, grad_rows, BLOCK))],
        [flow[c][0] for c in chunks]
        + [flow[c][1] for c in chunks]
        + [vectors, wb, trig, late],
        scratch=[pltpu.VMEM((local_bits, rows, width), BF), pltpu.VMEM((early, rows, width), BF)],
        flops=6 * product,
    )

    if nrow == 2:
        pairs = [(x, swapped(x, "row", 1)) for x in (ends, upper)]
    else:
        pairs = [lax.psum(x.astype(F32), "row") for x in (ends, upper)]
        pairs = [(p, jnp.zeros_like(p)) for p in pairs]

    def final_body(place_ref, e0, e1, p0, p1, bs_ref, as_ref, step, new, step_a, new_a):
        def get(s, c):
            k = s * nb + c
            if s < early:
                a, b = e0.at[k], e1.at[k]
            elif k - early * nb == late_at:
                a, b = e0.at[early * nb], e1.at[early * nb]
            else:
                k -= early * nb
                k -= k > late_at
                a, b = p0.at[k], p1.at[k]
            matrix = a[:BLOCK, :].astype(F32) + b[:BLOCK, :].astype(F32)
            return matrix, a[BLOCK:, :].astype(F32) + b[BLOCK:, :].astype(F32)

        sign = signs(place_ref)
        for c in chunks:
            angle = [None] * sections
            for s in range(sections):
                g, lines = get(s, c)
                state_new = 0.9 * bs_ref[s, col(c), :] + 0.1 * g * g
                new[s, col(c), :] = state_new
                step[s, col(c), :] = g * lax.rsqrt(state_new)
                if s == last:
                    angle[last], angle[third] = unpack_line(lines, 0), unpack_line(lines, 1)
                elif s >= early:
                    angle[s - 1] = unpack_line(lines, 0)
                elif s < local_bits:
                    angle[s] = unpack_line(lines, 0)
            g = jnp.concatenate(angle, axis=0) * sign[:, col(c)]
            state_new = 0.9 * as_ref[:, col(c)] + 0.1 * g * g
            new_a[:, col(c)] = state_new
            step_a[:, col(c)] = g * lax.rsqrt(state_new)

    step, new, step_a, new_a = call(
        "final",
        final_body,
        [shape(block_state.shape, F32)] * 2 + [shape(angle_state.shape, F32)] * 2,
        [place_arr, *pairs[0], *pairs[1], block_state, angle_state],
        specs={0: SMEM},
    )
    return step, new, step_a, new_a


def solution(mesh):
    in_specs = (
        P("row", "dim"),
        P(None, "dim", None),
        P(None, "dim"),
        P("row", "dim"),
        P("row"),
        P(),
        P(None, "dim", None),
        P(None, "dim"),
    )
    out_specs = (P(None, "dim", None), P(None, "dim", None), P(None, "dim"), P(None, "dim"))
    return jax.shard_map(local, mesh=mesh, in_specs=in_specs, out_specs=out_specs, check_vma=False)
```

```python
import math

import jax
import jax.numpy as jnp
from jax import lax
from jax.experimental import pallas as pl
from jax.experimental.pallas import tpu as pltpu
from jax.sharding import PartitionSpec as P

BLOCK = 128
GROUP = 4
EXTRA = 16
TRIG = 16
OPEN_LIMIT = 58
BF = jnp.bfloat16
F32 = jnp.float32


def swapped(value, axis, mask):
    pairs = [(source, source ^ mask) for source in range(lax.axis_size(axis))]
    return lax.ppermute(value, axis, pairs)


def dot(a, b):
    return lax.dot_general(a, b, (((1,), (0,)), ((), ())), preferred_element_type=F32)


def dot_t(a, b):
    return lax.dot_general(a, b, (((1,), (1,)), ((), ())), preferred_element_type=F32)


def t_dot(a, b):
    return lax.dot_general(a, b, (((0,), (0,)), ((), ())), preferred_element_type=F32)


def tile_of(rows):
    best = 16
    for size in range(16, 257, 16):
        if rows % size == 0:
            best = size
    return best


def call(name, body, outs, args, specs=None, scratch=(), flops=0, weight=1, limit=16):
    whole = [pl.BlockSpec(a.shape, lambda i, n=a.ndim: (0,) * n) for a in args]
    for at, spec in (specs or {}).items():
        whole[at] = spec
    moved = sum(math.prod(a.shape) * a.dtype.itemsize for a in args) + sum(
        math.prod(o.shape) * o.dtype.itemsize for o in outs
    )
    return list(
        pl.pallas_call(
            body,
            grid=(1,),
            in_specs=whole,
            out_specs=[pl.BlockSpec(o.shape, lambda i, n=len(o.shape): (0,) * n) for o in outs],
            out_shape=outs,
            scratch_shapes=list(scratch),
            compiler_params=pltpu.CompilerParams(vmem_limit_bytes=limit * 2**20),
            cost_estimate=pl.CostEstimate(
                flops=int(flops * weight * 100), bytes_accessed=int(moved * weight * 20), transcendentals=0
            ),
            name=name,
        )(*args)
    )


def shape(dims, dtype=BF):
    return jax.ShapeDtypeStruct(dims, dtype)


SMEM = pl.BlockSpec(memory_space=pltpu.SMEM)
HBM = pl.BlockSpec(memory_space=pltpu.HBM)


def split3(x):
    hi = x.astype(BF)
    rest = x - hi.astype(F32)
    mid = rest.astype(BF)
    low = (rest - mid.astype(F32)).astype(BF)
    return [hi, mid, low]


def stack_lines(lines, height):
    lines = [x.astype(F32) for x in lines]
    lines.append(jnp.zeros((height - len(lines), lines[0].shape[1]), F32))
    return jnp.concatenate(lines, axis=0)


def pack_grad(matrix, lines):
    parts = []
    for line in lines:
        parts += split3(line)[:2]
    return matrix.astype(BF), stack_lines(parts, EXTRA).astype(BF)


def unpack_line(tile, k):
    return tile[2 * k : 2 * k + 1] + tile[2 * k + 1 : 2 * k + 2]


def local(vectors, blocks, angles, codes, scale_index, scale_table, block_state, angle_state):
    rows, width = vectors.shape
    sections = blocks.shape[0]
    nb = width // BLOCK
    chunks = list(range(nb))
    local_bits = nb.bit_length() - 1
    shift = sections - 2 - local_bits
    quarter = rows // GROUP
    nrow = lax.axis_size("row")
    inv = 1.0 / math.sqrt(rows * nrow)
    tile = tile_of(quarter)
    device = lax.axis_index("dim")
    place_arr = device.astype(jnp.int32).reshape(1)
    last, third = sections - 1, sections - 2
    product = rows * BLOCK * BLOCK * 2
    grad_rows = BLOCK + EXTRA

    def signs(place_ref):
        dims = (sections, width)
        ids = place_ref[0] * nb + lax.broadcasted_iota(jnp.int32, dims, 1) // BLOCK
        bits = lax.shift_right_logical(ids, lax.broadcasted_iota(jnp.int32, dims, 0)) & 1
        return 1.0 - 2.0 * bits.astype(F32)

    def col(c):
        return slice(c * BLOCK, (c + 1) * BLOCK)

    def cs(ref, s, c):
        return ref[s : s + 1, col(c)], ref[sections + s : sections + s + 1, col(c)]

    def place_of(place_ref):
        return lax.shift_right_logical(place_ref[0], shift) & (GROUP - 1)

    def quarter_at(z, m):
        return pl.multiple_of(jnp.bitwise_xor(z, m) * quarter, 16)

    order = [2, 3, 1, 0]
    early = local_bits + 1
    base = quarter + TRIG
    highs = [base + BLOCK] * (GROUP - 1) + [quarter]

    def placed(refs):
        return [refs[order.index(m)] for m in range(GROUP)]

    def forward(u, weights, trig_ref):
        steps = []
        for s in range(local_bits):
            v = [dot(u[c], weights[s][c]).astype(BF) for c in chunks]
            steps.append((u, v))
            turned = []
            for c in chunks:
                co, si = cs(trig_ref, s, c)
                turned.append(
                    (co * v[c].astype(F32) + si * v[c ^ (1 << s)].astype(F32)).astype(BF)
                )
            u = turned
        return steps, u

    def pack_body(place_ref, w_hbm, codes_hbm, angle_hbm, *rest):
        p_out, trig_out = rest[:GROUP], rest[GROUP]
        w_held, c_held, a_held, w_sem, c_sems, a_sem = rest[GROUP + 1 :]
        z = place_of(place_ref)
        a_in = pltpu.make_async_copy(angle_hbm, a_held, a_sem)
        w_in = pltpu.make_async_copy(w_hbm.at[last], w_held, w_sem)
        c_in = [
            pltpu.make_async_copy(
                codes_hbm.at[pl.ds(quarter_at(z, m), quarter)], c_held.at[m], c_sems.at[m]
            )
            for m in range(GROUP)
        ]
        a_in.start()
        w_in.start()
        for m in order:
            c_in[m].start()
        a_in.wait()
        angle = a_held[...]
        co, si = jnp.cos(angle), signs(place_ref) * jnp.sin(angle)
        trig_out[...] = jnp.concatenate([co, si], axis=0)
        lines = []
        for s in (third, last):
            lines += split3(co[s : s + 1]) + split3(si[s : s + 1])
        lines = stack_lines(lines, TRIG).astype(BF)
        w_in.wait()
        for m in order:
            if highs[m] > base:
                p_out[m][quarter:base, :] = lines
                for c in chunks:
                    p_out[m][base:, col(c)] = w_held[col(c), :].astype(BF)
            c_in[m].wait()
            for r in range(0, quarter, tile):
                at = pl.ds(r, tile)
                p_out[m][at, :] = c_held[m, at, :].astype(F32).astype(BF)

    packed = call(
        "pack",
        pack_body,
        [shape((high, width)) for high in highs] + [shape((2 * sections, width), F32)],
        [place_arr, blocks, codes, angles],
        specs={0: SMEM, 1: HBM, 2: HBM, 3: HBM},
        scratch=[
            pltpu.VMEM((width, BLOCK), F32),
            pltpu.VMEM((GROUP, quarter, width), jnp.int32),
            pltpu.VMEM(angles.shape, F32),
            pltpu.SemaphoreType.DMA,
            pltpu.SemaphoreType.DMA((GROUP,)),
            pltpu.SemaphoreType.DMA,
        ],
        limit=OPEN_LIMIT,
    )
    trig = packed.pop()
    packs = {m: swapped(packed[m], "dim", m << shift) for m in order[:-1]}
    packs[0] = packed[0]

    def first_body(place_ref, u_ref, w_ref, angle_ref, v_out, trig_ref):
        angle = angle_ref[...]
        trig_ref[...] = jnp.concatenate(
            [jnp.cos(angle), signs(place_ref) * jnp.sin(angle)], axis=0
        )
        weights = [[w_ref[s, col(c), :].astype(BF) for c in chunks] for s in range(early)]
        for r in range(0, rows, tile):
            at = pl.ds(r, tile)
            u = forward([u_ref[at, col(c)] for c in chunks], weights, trig_ref)[1]
            for c in chunks:
                v_out[at, col(c)] = dot(u[c], weights[local_bits][c]).astype(BF)

    (v_first,) = call(
        "first",
        first_body,
        [shape((rows, width))],
        [place_arr, vectors, blocks, lax.optimization_barrier((angles, trig))[0]],
        specs={0: SMEM},
        scratch=[pltpu.VMEM((2 * sections, width), F32)],
        flops=rows * width * BLOCK * 4,
    )
    other_first = swapped(v_first, "dim", 1)

    def scale_body(place_ref, table_ref, index_ref, w_ref, out, wb_out):
        for s in range(sections):
            wb_out[s] = w_ref[s].astype(BF)
        index = index_ref[pl.ds(place_of(place_ref), 1), :]
        values = jnp.zeros(index.shape, F32)
        for level in range(table_ref.shape[0]):
            values = jnp.where(index == level, table_ref[level], values)
        parts = stack_lines(split3(values), 16).astype(BF)
        out[...] = t_dot(parts, jnp.ones((16, BLOCK), BF))

    factor, wb = call(
        "scales",
        scale_body,
        [shape((quarter, BLOCK), F32), shape(blocks.shape)],
        [place_arr, scale_table, scale_index.reshape(GROUP, quarter), blocks],
        specs={0: SMEM, 1: SMEM},
    )

    saves = {c: {} for c in chunks}

    def middle(c, s, v, other, quarters):
        wide = v.shape[1] != BLOCK
        cols = col(c) if wide else slice(None)

        def body(place_ref, v_ref, o_ref, w_ref, trig_ref, *outs):
            co, si = cs(trig_ref, s, c)
            w = w_ref[s + 1, col(c), :]
            z = place_of(place_ref)
            for m in range(GROUP):
                start = quarter_at(z, m) if quarters else m * quarter
                for r in range(0, quarter, tile):
                    at = pl.ds(start + r, tile)
                    u = (
                        co * v_ref[at, cols].astype(F32) + si * o_ref[at, cols].astype(F32)
                    ).astype(BF)
                    v_new = dot(u, w).astype(BF)
                    if quarters:
                        outs[m][r : r + tile, :] = v_new
                    else:
                        outs[0][at, :] = v_new

        outs = [shape((quarter, BLOCK))] * GROUP if quarters else [shape((rows, BLOCK))]
        return call(
            f"forward{s + 1}_chunk{c}",
            body,
            outs,
            [place_arr, v, other, wb, trig],
            specs={0: SMEM},
            flops=product,
        )

    def with_weights(c, mine):
        def body(m_ref, p_ref, out):
            for r in range(0, quarter, tile):
                at = pl.ds(r, tile)
                out[at, :] = m_ref[at, :]
            out[quarter:, :] = p_ref[quarter:, col(c)]

        return call(
            f"near_chunk{c}", body, [shape((base + BLOCK, BLOCK))], [mine, packs[GROUP - 2]]
        )[0]

    middles = list(range(local_bits, third))
    state = {c: (v_first, other_first) for c in chunks}
    for s in middles:
        for c in chunks:
            v, other = state[c]
            if s + 1 == third and c == chunks[0]:
                other, packs[1] = lax.optimization_barrier((other, packs[1]))
            out = middle(c, s, v, other, s + 1 == third)
            saves[c][s] = (v, other)
            if s + 1 < third:
                state[c] = (out[0], swapped(out[0], "dim", 1 << (s + 1 - local_bits)))
            else:
                out[1] = with_weights(c, out[1])
                got = {m: swapped(out[m], "dim", m << shift) for m in order[:-1]}
                got[0] = out[0]
                state[c] = [got[m] for m in order]

    def group_stage(c, earlier):
        final = c == chunks[-1]

        def body(*refs):
            a_refs, p_refs = placed(refs[:GROUP]), placed(refs[GROUP : 2 * GROUP])
            f_ref = refs[2 * GROUP]
            e_refs = refs[2 * GROUP + 1 : 2 * GROUP + 1 + len(earlier)]
            refs = refs[2 * GROUP + 1 + len(earlier) :]
            outs, grad_refs = refs[:GROUP], refs[GROUP:]
            coef, w = [], []
            for m in range(GROUP):
                far = m == GROUP - 1
                t = (a_refs[1][quarter:base, :] if far else p_refs[m][quarter:base, col(c)]).astype(F32)
                coef.append(
                    [t[3 * k : 3 * k + 1] + t[3 * k + 1 : 3 * k + 2] + t[3 * k + 2 : 3 * k + 3] for k in range(4)]
                )
                w.append(a_refs[1][base:, :] if far else p_refs[m][base:, col(c)])
            gw = [jnp.zeros((BLOCK, BLOCK), F32)] * GROUP
            ga = [[jnp.zeros((1, BLOCK), F32)] * GROUP for _ in range(2)]
            every = range(GROUP)
            for r in range(0, quarter, tile):
                at = pl.ds(r, tile)
                a = [a_refs[m][at, :].astype(F32) for m in every]
                u = [(coef[m][0] * a[m] + coef[m][1] * a[m ^ 1]).astype(BF) for m in every]
                v = [dot(u[m], w[m]).astype(BF).astype(F32) for m in every]
                f = f_ref[at, :]
                g = []
                for m in every:
                    end = (coef[m][2] * v[m] + coef[m][3] * v[m ^ 2]).astype(BF).astype(F32)
                    recon = f * (p_refs[m][at, col(c)].astype(F32) - 7.5)
                    g.append(((end - recon) * inv).astype(BF).astype(F32))
                for m in every:
                    ga[0][m] = ga[0][m] + jnp.sum(
                        g[m] * (coef[m][2] * v[m ^ 2] - coef[m][3] * v[m]), axis=0, keepdims=True
                    )
                q = [(coef[m][3] * g[m]).astype(BF).astype(F32) for m in every]
                dv = [(coef[m][2] * g[m] + q[m ^ 2]).astype(BF) for m in every]
                g = []
                for m in every:
                    gw[m] = gw[m] + t_dot(u[m], dv[m])
                    g.append(dot_t(dv[m], w[m]).astype(BF).astype(F32))
                for m in every:
                    ga[1][m] = ga[1][m] + jnp.sum(
                        g[m] * (coef[m][0] * a[m ^ 1] - coef[m][1] * a[m]), axis=0, keepdims=True
                    )
                q = [(coef[m][1] * g[m]).astype(BF).astype(F32) for m in every]
                for m in every:
                    outs[m][at, :] = (coef[m][0] * g[m] + q[m ^ 1]).astype(BF)
            for m in every:
                if final:
                    out = grad_refs[m]
                    if m:
                        for k in range(len(earlier)):
                            for h in range(0, grad_rows, 16):
                                out[k, h : h + 16, :] = e_refs[k][m, h : h + 16, :]
                    out = out.at[c] if m else out
                else:
                    out = grad_refs[0].at[m]
                matrix, lines = pack_grad(gw[m], [ga[0][m], ga[1][m]])
                out[:BLOCK, :] = matrix
                out[BLOCK:, :] = lines

        grads = (
            [shape((grad_rows, BLOCK))] + [shape((nb, grad_rows, BLOCK))] * (GROUP - 1)
            if final
            else [shape((GROUP, grad_rows, BLOCK))]
        )
        return call(
            f"group_chunk{c}",
            body,
            [shape((quarter, BLOCK))] * GROUP + grads,
            state[c] + [packs[m] for m in order] + [factor] + earlier,
            flops=3 * product,
        )

    returned, partial = {}, []
    for c in chunks:
        out = group_stage(c, list(partial))
        returned[c] = {m: swapped(out[m], "dim", m << shift) for m in order[:-1]}
        returned[c][0] = out[0]
        partial.append(out[GROUP])
    sums = out[GROUP + 1 :]

    def write_grad(out, gw, ga):
        out[:BLOCK, :] = gw
        out[BLOCK:, :] = stack_lines([ga], EXTRA)

    grad_shape = shape((grad_rows, BLOCK), F32)

    def back(c, s, load, v, other, w_ref, trig_ref, spans, g_out, q_out, grad, packing=False):
        cols = col(c) if v.shape[1] != BLOCK else slice(None)
        w = w_ref[s, col(c), :]
        co, si = cs(trig_ref, s - 1, c)
        gw = jnp.zeros((BLOCK, BLOCK), F32)
        ga = jnp.zeros((1, BLOCK), F32)
        for m, start in enumerate(spans):
            for r in range(0, quarter, tile):
                at = pl.ds(start + r, tile)
                d = load(m, r, at)
                mine, theirs = v[at, cols].astype(F32), other[at, cols].astype(F32)
                gw = gw + t_dot((co * mine + si * theirs).astype(BF), d)
                g16 = dot_t(d, w).astype(BF)
                g = g16.astype(F32)
                g_out[at, :] = g16
                ga = ga + jnp.sum(g * (co * theirs - si * mine), axis=0, keepdims=True)
                q_out[at, :] = (si * g).astype(BF)
        if packing:
            grad[:BLOCK, :], grad[BLOCK:, :] = pack_grad(gw, [ga])
        else:
            write_grad(grad, gw, ga)

    def back_quarters(c, s):
        v, other = saves[c][s - 1]

        def body(place_ref, *refs):
            d_refs = placed(refs[:GROUP])
            v_ref, o_ref, w_ref, trig_ref, g_out, q_out, grad = refs[GROUP:]
            spans = [quarter_at(place_of(place_ref), m) for m in range(GROUP)]

            def load(m, r, at):
                return d_refs[m][r : r + tile, :]

            back(c, s, load, v_ref, o_ref, w_ref, trig_ref, spans, g_out, q_out, grad)

        return call(
            f"backward{s}_chunk{c}",
            body,
            [shape((rows, BLOCK)), shape((rows, BLOCK)), grad_shape],
            [place_arr] + [returned[c][m] for m in order] + [v, other, wb, trig],
            specs={0: SMEM},
            flops=2 * product,
        )

    uppers = [(s, c) for s in range(early, third + 1) for c in chunks]
    upper_shape = shape((((sections - early) * nb - 1) * BLOCK + EXTRA, BLOCK))

    def gather_uppers(owns, others, given, out):
        parts = []
        for k, grad in enumerate(given):
            out[k * BLOCK : (k + 1) * BLOCK, :] = grad[:BLOCK, :].astype(BF)
            parts += split3(grad[BLOCK : BLOCK + 1, :])[:2]
        for c in chunks:
            own = owns[c] if c == chunks[-1] else owns[c].at[0]
            total = own[:BLOCK, :].astype(F32)
            tail = own[BLOCK:, :].astype(F32)
            for other in others:
                total = total + other[c, :BLOCK, :].astype(F32)
                tail = tail + other[c, BLOCK:, :].astype(F32)
            k = len(given) + c
            out[k * BLOCK : (k + 1) * BLOCK, :] = total.astype(BF)
            parts += split3(unpack_line(tail, 0))[:2] + split3(unpack_line(tail, 1))[:2]
        out[-EXTRA:, :] = stack_lines(parts, EXTRA).astype(BF)

    def upper_body(*refs):
        owns, others = refs[:nb], refs[nb : nb + GROUP - 1]
        gather_uppers(owns, others, refs[nb + GROUP - 1 : -1], refs[-1])

    def back_middle(c, s, g, incoming, ending):
        v, other = saves[c][s - 1]

        def body(g_ref, i_ref, v_ref, o_ref, w_ref, trig_ref, g_out, q_out, grad):
            here = cs(trig_ref, s, c)[0]
            spans = [m * quarter for m in range(GROUP)]

            def load(m, r, at):
                return (here * g_ref[at, :].astype(F32) + i_ref[at, :].astype(F32)).astype(BF)

            back(c, s, load, v_ref, o_ref, w_ref, trig_ref, spans, g_out, q_out, grad, ending)

        return call(
            f"backward{s}_chunk{c}",
            body,
            [shape((rows, BLOCK)), shape((rows, BLOCK))]
            + [shape((grad_rows, BLOCK)) if ending else grad_shape],
            [g, incoming, v, other, wb, trig],
            flops=2 * product,
        )

    grads = {c: {} for c in chunks}
    flow = {}
    for c in chunks:
        g, q, grads[c][third] = back_quarters(c, third)
        flow[c] = (g, swapped(q, "dim", 1 << (third - 1 - local_bits)))
    sums, q = lax.optimization_barrier((sums, q))
    arrived = [swapped(sums[m - 1], "dim", m << shift) for m in order[:-1]]
    for s in reversed(middles[1:]):
        for c in chunks:
            ending = s == middles[1] and c == chunks[-1]
            g, incoming = flow[c]
            if ending:
                given = [grads[e][t] for t, e in uppers if (t, e) != (s, c)]
                (upper,) = call("uppers", upper_body, [upper_shape], partial + arrived + given)
                incoming, upper = lax.optimization_barrier((incoming, upper))
            g, q, grads[c][s] = back_middle(c, s, g, incoming, ending)
            flow[c] = (g, swapped(q, "dim", 1 << (s - 1 - local_bits)))
    late = grads[chunks[-1]][middles[1]]
    late_at = uppers.index((middles[1], chunks[-1]))

    def end_body(*refs):
        g_refs, i_refs = refs[:nb], refs[nb : 2 * nb]
        u_ref, w_ref, trig_ref, late_ref, grad, u_held, d_held = refs[2 * nb :]
        ga = [[jnp.zeros((1, BLOCK), F32)] * nb for _ in range(early)]
        w = [[w_ref[s, col(c), :] for c in chunks] for s in range(early)]
        for r in range(0, rows, tile):
            at = pl.ds(r, tile)
            steps, u = forward([u_ref[at, col(c)] for c in chunks], w, trig_ref)
            inputs = [u for u, _ in steps] + [u]
            d = []
            for c in chunks:
                here = cs(trig_ref, local_bits, c)[0]
                d.append(
                    (here * g_refs[c][at, :].astype(F32) + i_refs[c][at, :].astype(F32)).astype(BF)
                )
            for s in reversed(range(early)):
                for c in chunks:
                    d_held[s, at, col(c)] = d[c]
                    if s:
                        u_held[s - 1, at, col(c)] = inputs[s][c]
                if s == 0:
                    break
                g = [dot_t(d[c], w[s][c]).astype(BF).astype(F32) for c in chunks]
                t = s - 1
                v = [x.astype(F32) for x in steps[t][1]]
                q = []
                for c in chunks:
                    co, si = cs(trig_ref, t, c)
                    ga[t][c] = ga[t][c] + jnp.sum(
                        g[c] * (co * v[c ^ (1 << t)] - si * v[c]), axis=0, keepdims=True
                    )
                    q.append((si * g[c]).astype(BF).astype(F32))
                d = [
                    (cs(trig_ref, t, c)[0] * g[c] + q[c ^ (1 << t)]).astype(BF) for c in chunks
                ]
        parts = []
        for s in range(early):
            for c in chunks:
                left = u_held[s - 1, :, col(c)] if s else u_ref[:, col(c)]
                k = s * nb + c
                matrix = t_dot(left, d_held[s, :, col(c)])
                grad[k * BLOCK : (k + 1) * BLOCK, :] = matrix.astype(BF)
                parts += split3(ga[s][c])[:2]
        grad[early * nb * BLOCK : (early * nb + 1) * BLOCK, :] = late_ref[:BLOCK, :]
        tail = late_ref[BLOCK:, :].astype(F32)
        parts += [tail[0:1], tail[1:2]]
        grad[-EXTRA:, :] = stack_lines(parts, EXTRA).astype(BF)

    (ends,) = call(
        "end",
        end_body,
        [shape(((early * nb + 1) * BLOCK + EXTRA, BLOCK))],
        [flow[c][0] for c in chunks]
        + [flow[c][1] for c in chunks]
        + [vectors, wb, trig, late],
        scratch=[pltpu.VMEM((local_bits, rows, width), BF), pltpu.VMEM((early, rows, width), BF)],
        flops=6 * product,
    )

    if nrow == 2:
        pairs = [(x, swapped(x, "row", 1)) for x in (ends, upper)]
    else:
        pairs = [lax.psum(x.astype(F32), "row") for x in (ends, upper)]
        pairs = [(p, jnp.zeros_like(p)) for p in pairs]

    def final_body(place_ref, e0, e1, p0, p1, bs_ref, as_ref, step, new, step_a, new_a):
        tails = {
            at: a[-EXTRA:, :].astype(F32) + b[-EXTRA:, :].astype(F32)
            for at, a, b in (("end", e0, e1), ("upper", p0, p1))
        }

        def get(s, c):
            k = s * nb + c
            at, a, b = "end", e0, e1
            if k - early * nb == late_at:
                k = early * nb
            elif s >= early:
                at, a, b = "upper", p0, p1
                k -= early * nb
                k -= k > late_at
            line = k + max(0, k - len(uppers) + 1) if at == "upper" else k
            lines = [line, line + 1] if s == last else [line]
            rows_of = slice(k * BLOCK, (k + 1) * BLOCK)
            matrix = a[rows_of, :].astype(F32) + b[rows_of, :].astype(F32)
            return matrix, [unpack_line(tails[at], line) for line in lines]

        sign = signs(place_ref)
        for c in chunks:
            angle = [None] * sections
            for s in range(sections):
                g, lines = get(s, c)
                state_new = 0.9 * bs_ref[s, col(c), :] + 0.1 * g * g
                new[s, col(c), :] = state_new
                step[s, col(c), :] = g * lax.rsqrt(state_new)
                if s == last:
                    angle[last], angle[third] = lines[0], lines[1]
                elif s >= early:
                    angle[s - 1] = lines[0]
                elif s < local_bits:
                    angle[s] = lines[0]
            g = jnp.concatenate(angle, axis=0) * sign[:, col(c)]
            state_new = 0.9 * as_ref[:, col(c)] + 0.1 * g * g
            new_a[:, col(c)] = state_new
            step_a[:, col(c)] = g * lax.rsqrt(state_new)

    step, new, step_a, new_a = call(
        "final",
        final_body,
        [shape(block_state.shape, F32)] * 2 + [shape(angle_state.shape, F32)] * 2,
        [place_arr, *pairs[0], *pairs[1], block_state, angle_state],
        specs={0: SMEM},
    )
    return step, new, step_a, new_a


def solution(mesh):
    in_specs = (
        P("row", "dim"),
        P(None, "dim", None),
        P(None, "dim"),
        P("row", "dim"),
        P("row"),
        P(),
        P(None, "dim", None),
        P(None, "dim"),
    )
    out_specs = (P(None, "dim", None), P(None, "dim", None), P(None, "dim"), P(None, "dim"))
    return jax.shard_map(local, mesh=mesh, in_specs=in_specs, out_specs=out_specs, check_vma=False)
```

```python
import math

import jax
import jax.numpy as jnp
from jax import lax
from jax.experimental import pallas as pl
from jax.experimental.pallas import tpu as pltpu
from jax.sharding import PartitionSpec as P

BLOCK = 128
GROUP = 4
EXTRA = 16
TRIG = 16
OPEN_LIMIT = 58
BF = jnp.bfloat16
F32 = jnp.float32


def swapped(value, axis, mask):
    pairs = [(source, source ^ mask) for source in range(lax.axis_size(axis))]
    return lax.ppermute(value, axis, pairs)


def dot(a, b):
    return lax.dot_general(a, b, (((1,), (0,)), ((), ())), preferred_element_type=F32)


def dot_t(a, b):
    return lax.dot_general(a, b, (((1,), (1,)), ((), ())), preferred_element_type=F32)


def t_dot(a, b):
    return lax.dot_general(a, b, (((0,), (0,)), ((), ())), preferred_element_type=F32)


def tile_of(rows):
    best = 16
    for size in range(16, 417, 16):
        if rows % size == 0:
            best = size
    return best


def call(name, body, outs, args, specs=None, scratch=(), flops=0, weight=1, limit=16):
    whole = [pl.BlockSpec(a.shape, lambda i, n=a.ndim: (0,) * n) for a in args]
    for at, spec in (specs or {}).items():
        whole[at] = spec
    moved = sum(math.prod(a.shape) * a.dtype.itemsize for a in args) + sum(
        math.prod(o.shape) * o.dtype.itemsize for o in outs
    )
    return list(
        pl.pallas_call(
            body,
            grid=(1,),
            in_specs=whole,
            out_specs=[pl.BlockSpec(o.shape, lambda i, n=len(o.shape): (0,) * n) for o in outs],
            out_shape=outs,
            scratch_shapes=list(scratch),
            compiler_params=pltpu.CompilerParams(vmem_limit_bytes=limit * 2**20),
            cost_estimate=pl.CostEstimate(
                flops=int(flops * weight * 100), bytes_accessed=int(moved * weight * 20), transcendentals=0
            ),
            name=name,
        )(*args)
    )


def shape(dims, dtype=BF):
    return jax.ShapeDtypeStruct(dims, dtype)


SMEM = pl.BlockSpec(memory_space=pltpu.SMEM)
HBM = pl.BlockSpec(memory_space=pltpu.HBM)


def split3(x):
    hi = x.astype(BF)
    rest = x - hi.astype(F32)
    mid = rest.astype(BF)
    low = (rest - mid.astype(F32)).astype(BF)
    return [hi, mid, low]


def stack_lines(lines, height):
    lines = [x.astype(F32) for x in lines]
    lines.append(jnp.zeros((height - len(lines), lines[0].shape[1]), F32))
    return jnp.concatenate(lines, axis=0)


def pack_grad(matrix, lines):
    parts = []
    for line in lines:
        parts += split3(line)[:2]
    return matrix.astype(BF), stack_lines(parts, EXTRA).astype(BF)


def unpack_line(tile, k):
    return tile[2 * k : 2 * k + 1] + tile[2 * k + 1 : 2 * k + 2]


def local(vectors, blocks, angles, codes, scale_index, scale_table, block_state, angle_state):
    rows, width = vectors.shape
    sections = blocks.shape[0]
    nb = width // BLOCK
    chunks = list(range(nb))
    local_bits = nb.bit_length() - 1
    shift = sections - 2 - local_bits
    quarter = rows // GROUP
    nrow = lax.axis_size("row")
    inv = 1.0 / math.sqrt(rows * nrow)
    tile = tile_of(quarter)
    device = lax.axis_index("dim")
    place_arr = device.astype(jnp.int32).reshape(1)
    last, third = sections - 1, sections - 2
    product = rows * BLOCK * BLOCK * 2
    grad_rows = BLOCK + EXTRA

    def signs(place_ref):
        dims = (sections, width)
        ids = place_ref[0] * nb + lax.broadcasted_iota(jnp.int32, dims, 1) // BLOCK
        bits = lax.shift_right_logical(ids, lax.broadcasted_iota(jnp.int32, dims, 0)) & 1
        return 1.0 - 2.0 * bits.astype(F32)

    def col(c):
        return slice(c * BLOCK, (c + 1) * BLOCK)

    def cs(ref, s, c):
        return ref[s : s + 1, col(c)], ref[sections + s : sections + s + 1, col(c)]

    def place_of(place_ref):
        return lax.shift_right_logical(place_ref[0], shift) & (GROUP - 1)

    def quarter_at(z, m):
        return pl.multiple_of(jnp.bitwise_xor(z, m) * quarter, 16)

    order = [2, 3, 1, 0]
    early = local_bits + 1
    base = quarter + TRIG
    highs = [base + BLOCK] * (GROUP - 1) + [quarter]

    def placed(refs):
        return [refs[order.index(m)] for m in range(GROUP)]

    def forward(u, weights, trig_ref):
        steps = []
        for s in range(local_bits):
            v = [dot(u[c], weights[s][c]).astype(BF) for c in chunks]
            steps.append((u, v))
            turned = []
            for c in chunks:
                co, si = cs(trig_ref, s, c)
                turned.append(
                    (co * v[c].astype(F32) + si * v[c ^ (1 << s)].astype(F32)).astype(BF)
                )
            u = turned
        return steps, u

    def pack_body(place_ref, w_hbm, codes_hbm, angle_hbm, *rest):
        p_out, trig_out = rest[:GROUP], rest[GROUP]
        w_held, c_held, a_held, w_sem, c_sems, a_sem = rest[GROUP + 1 :]
        z = place_of(place_ref)
        a_in = pltpu.make_async_copy(angle_hbm, a_held, a_sem)
        w_in = pltpu.make_async_copy(w_hbm.at[last], w_held, w_sem)
        c_in = [
            pltpu.make_async_copy(
                codes_hbm.at[pl.ds(quarter_at(z, m), quarter)], c_held.at[m], c_sems.at[m]
            )
            for m in range(GROUP)
        ]
        a_in.start()
        w_in.start()
        for m in order:
            c_in[m].start()
        a_in.wait()
        angle = a_held[...]
        co, si = jnp.cos(angle), signs(place_ref) * jnp.sin(angle)
        trig_out[...] = jnp.concatenate([co, si], axis=0)
        lines = []
        for s in (third, last):
            lines += split3(co[s : s + 1]) + split3(si[s : s + 1])
        lines = stack_lines(lines, TRIG).astype(BF)
        w_in.wait()
        for m in order:
            if highs[m] > base:
                p_out[m][quarter:base, :] = lines
                for c in chunks:
                    p_out[m][base:, col(c)] = w_held[col(c), :].astype(BF)
            c_in[m].wait()
            for r in range(0, quarter, tile):
                at = pl.ds(r, tile)
                p_out[m][at, :] = c_held[m, at, :].astype(F32).astype(BF)

    packed = call(
        "pack",
        pack_body,
        [shape((high, width)) for high in highs] + [shape((2 * sections, width), F32)],
        [place_arr, blocks, codes, angles],
        specs={0: SMEM, 1: HBM, 2: HBM, 3: HBM},
        scratch=[
            pltpu.VMEM((width, BLOCK), F32),
            pltpu.VMEM((GROUP, quarter, width), jnp.int32),
            pltpu.VMEM(angles.shape, F32),
            pltpu.SemaphoreType.DMA,
            pltpu.SemaphoreType.DMA((GROUP,)),
            pltpu.SemaphoreType.DMA,
        ],
        limit=OPEN_LIMIT,
    )
    trig = packed.pop()
    packs = {m: swapped(packed[m], "dim", m << shift) for m in order[:-1]}
    packs[0] = packed[0]

    def first_body(place_ref, u_ref, w_ref, angle_ref, v_out, trig_ref):
        angle = angle_ref[...]
        trig_ref[...] = jnp.concatenate(
            [jnp.cos(angle), signs(place_ref) * jnp.sin(angle)], axis=0
        )
        weights = [[w_ref[s, col(c), :].astype(BF) for c in chunks] for s in range(early)]
        for r in range(0, rows, 2 * tile):
            at = pl.ds(r, 2 * tile)
            u = forward([u_ref[at, col(c)] for c in chunks], weights, trig_ref)[1]
            for c in chunks:
                v_out[at, col(c)] = dot(u[c], weights[local_bits][c]).astype(BF)

    (v_first,) = call(
        "first",
        first_body,
        [shape((rows, width))],
        [place_arr, vectors, blocks, lax.optimization_barrier((angles, trig))[0]],
        specs={0: SMEM},
        scratch=[pltpu.VMEM((2 * sections, width), F32)],
        flops=rows * width * BLOCK * 4,
    )
    other_first = swapped(v_first, "dim", 1)

    def scale_body(place_ref, table_ref, index_ref, w_ref, out, wb_out):
        for s in range(sections):
            wb_out[s] = w_ref[s].astype(BF)
        index = index_ref[pl.ds(place_of(place_ref), 1), :]
        values = jnp.zeros(index.shape, F32)
        for level in range(table_ref.shape[0]):
            values = jnp.where(index == level, table_ref[level], values)
        parts = stack_lines(split3(values), 16).astype(BF)
        out[...] = t_dot(parts, jnp.ones((16, BLOCK), BF))

    factor, wb = call(
        "scales",
        scale_body,
        [shape((quarter, BLOCK), F32), shape(blocks.shape)],
        [place_arr, scale_table, scale_index.reshape(GROUP, quarter), blocks],
        specs={0: SMEM, 1: SMEM},
    )

    saves = {c: {} for c in chunks}

    def middle(c, s, v, other, quarters):
        wide = v.shape[1] != BLOCK
        cols = col(c) if wide else slice(None)

        def body(place_ref, v_ref, o_ref, w_ref, trig_ref, *outs):
            co, si = cs(trig_ref, s, c)
            w = w_ref[s + 1, col(c), :]
            z = place_of(place_ref)
            for m in range(GROUP):
                start = quarter_at(z, m) if quarters else m * quarter
                for r in range(0, quarter, tile):
                    at = pl.ds(start + r, tile)
                    u = (
                        co * v_ref[at, cols].astype(F32) + si * o_ref[at, cols].astype(F32)
                    ).astype(BF)
                    v_new = dot(u, w).astype(BF)
                    if quarters:
                        outs[m][r : r + tile, :] = v_new
                    else:
                        outs[0][at, :] = v_new

        outs = [shape((quarter, BLOCK))] * GROUP if quarters else [shape((rows, BLOCK))]
        return call(
            f"forward{s + 1}_chunk{c}",
            body,
            outs,
            [place_arr, v, other, wb, trig],
            specs={0: SMEM},
            flops=product,
        )

    def with_weights(c, mine):
        def body(m_ref, p_ref, out):
            for r in range(0, quarter, tile):
                at = pl.ds(r, tile)
                out[at, :] = m_ref[at, :]
            out[quarter:, :] = p_ref[quarter:, col(c)]

        return call(
            f"near_chunk{c}", body, [shape((base + BLOCK, BLOCK))], [mine, packs[GROUP - 2]]
        )[0]

    middles = list(range(local_bits, third))
    state = {c: (v_first, other_first) for c in chunks}
    for s in middles:
        for c in chunks:
            v, other = state[c]
            if s + 1 == third and c == chunks[0]:
                other, packs[1] = lax.optimization_barrier((other, packs[1]))
            out = middle(c, s, v, other, s + 1 == third)
            saves[c][s] = (v, other)
            if s + 1 < third:
                state[c] = (out[0], swapped(out[0], "dim", 1 << (s + 1 - local_bits)))
            else:
                out[1] = with_weights(c, out[1])
                got = {m: swapped(out[m], "dim", m << shift) for m in order[:-1]}
                got[0] = out[0]
                state[c] = [got[m] for m in order]

    def group_stage(c, earlier):
        final = c == chunks[-1]

        def body(*refs):
            a_refs, p_refs = placed(refs[:GROUP]), placed(refs[GROUP : 2 * GROUP])
            f_ref = refs[2 * GROUP]
            e_refs = refs[2 * GROUP + 1 : 2 * GROUP + 1 + len(earlier)]
            refs = refs[2 * GROUP + 1 + len(earlier) :]
            outs, grad_refs = refs[:GROUP], refs[GROUP:]
            coef, w = [], []
            for m in range(GROUP):
                far = m == GROUP - 1
                t = (a_refs[1][quarter:base, :] if far else p_refs[m][quarter:base, col(c)]).astype(F32)
                coef.append(
                    [t[3 * k : 3 * k + 1] + t[3 * k + 1 : 3 * k + 2] + t[3 * k + 2 : 3 * k + 3] for k in range(4)]
                )
                w.append(a_refs[1][base:, :] if far else p_refs[m][base:, col(c)])
            gw = [jnp.zeros((BLOCK, BLOCK), F32)] * GROUP
            ga = [[jnp.zeros((1, BLOCK), F32)] * GROUP for _ in range(2)]
            every = range(GROUP)
            for r in range(0, quarter, tile):
                at = pl.ds(r, tile)
                a = [a_refs[m][at, :].astype(F32) for m in every]
                u = [(coef[m][0] * a[m] + coef[m][1] * a[m ^ 1]).astype(BF) for m in every]
                v = [dot(u[m], w[m]).astype(BF).astype(F32) for m in every]
                f = f_ref[at, :]
                g = []
                for m in every:
                    end = (coef[m][2] * v[m] + coef[m][3] * v[m ^ 2]).astype(BF).astype(F32)
                    recon = f * (p_refs[m][at, col(c)].astype(F32) - 7.5)
                    g.append(((end - recon) * inv).astype(BF).astype(F32))
                for m in every:
                    ga[0][m] = ga[0][m] + jnp.sum(
                        g[m] * (coef[m][2] * v[m ^ 2] - coef[m][3] * v[m]), axis=0, keepdims=True
                    )
                q = [(coef[m][3] * g[m]).astype(BF).astype(F32) for m in every]
                dv = [(coef[m][2] * g[m] + q[m ^ 2]).astype(BF) for m in every]
                g = []
                for m in every:
                    gw[m] = gw[m] + t_dot(u[m], dv[m])
                    g.append(dot_t(dv[m], w[m]).astype(BF).astype(F32))
                for m in every:
                    ga[1][m] = ga[1][m] + jnp.sum(
                        g[m] * (coef[m][0] * a[m ^ 1] - coef[m][1] * a[m]), axis=0, keepdims=True
                    )
                q = [(coef[m][1] * g[m]).astype(BF).astype(F32) for m in every]
                for m in every:
                    outs[m][at, :] = (coef[m][0] * g[m] + q[m ^ 1]).astype(BF)
            for m in every:
                if final:
                    out = grad_refs[m]
                    if m:
                        for k in range(len(earlier)):
                            for h in range(0, grad_rows, 16):
                                out[k, h : h + 16, :] = e_refs[k][m, h : h + 16, :]
                    out = out.at[c] if m else out
                else:
                    out = grad_refs[0].at[m]
                matrix, lines = pack_grad(gw[m], [ga[0][m], ga[1][m]])
                out[:BLOCK, :] = matrix
                out[BLOCK:, :] = lines

        grads = (
            [shape((grad_rows, BLOCK))] + [shape((nb, grad_rows, BLOCK))] * (GROUP - 1)
            if final
            else [shape((GROUP, grad_rows, BLOCK))]
        )
        return call(
            f"group_chunk{c}",
            body,
            [shape((quarter, BLOCK))] * GROUP + grads,
            state[c] + [packs[m] for m in order] + [factor] + earlier,
            flops=3 * product,
        )

    returned, partial = {}, []
    for c in chunks:
        out = group_stage(c, list(partial))
        returned[c] = {m: swapped(out[m], "dim", m << shift) for m in order[:-1]}
        returned[c][0] = out[0]
        partial.append(out[GROUP])
    sums = out[GROUP + 1 :]

    def write_grad(out, gw, ga):
        out[:BLOCK, :] = gw
        out[BLOCK:, :] = stack_lines([ga], EXTRA)

    grad_shape = shape((grad_rows, BLOCK), F32)

    def back(c, s, load, v, other, w_ref, trig_ref, spans, g_out, q_out, grad, packing=False):
        cols = col(c) if v.shape[1] != BLOCK else slice(None)
        w = w_ref[s, col(c), :]
        co, si = cs(trig_ref, s - 1, c)
        gw = jnp.zeros((BLOCK, BLOCK), F32)
        ga = jnp.zeros((1, BLOCK), F32)
        for m, start in enumerate(spans):
            for r in range(0, quarter, tile):
                at = pl.ds(start + r, tile)
                d = load(m, r, at)
                mine, theirs = v[at, cols].astype(F32), other[at, cols].astype(F32)
                gw = gw + t_dot((co * mine + si * theirs).astype(BF), d)
                g16 = dot_t(d, w).astype(BF)
                g = g16.astype(F32)
                g_out[at, :] = g16
                ga = ga + jnp.sum(g * (co * theirs - si * mine), axis=0, keepdims=True)
                q_out[at, :] = (si * g).astype(BF)
        if packing:
            grad[:BLOCK, :], grad[BLOCK:, :] = pack_grad(gw, [ga])
        else:
            write_grad(grad, gw, ga)

    def back_quarters(c, s):
        v, other = saves[c][s - 1]

        def body(place_ref, *refs):
            d_refs = placed(refs[:GROUP])
            v_ref, o_ref, w_ref, trig_ref, g_out, q_out, grad = refs[GROUP:]
            spans = [quarter_at(place_of(place_ref), m) for m in range(GROUP)]

            def load(m, r, at):
                return d_refs[m][r : r + tile, :]

            back(c, s, load, v_ref, o_ref, w_ref, trig_ref, spans, g_out, q_out, grad)

        return call(
            f"backward{s}_chunk{c}",
            body,
            [shape((rows, BLOCK)), shape((rows, BLOCK)), grad_shape],
            [place_arr] + [returned[c][m] for m in order] + [v, other, wb, trig],
            specs={0: SMEM},
            flops=2 * product,
        )

    uppers = [(s, c) for s in range(early, third + 1) for c in chunks]
    upper_shape = shape((((sections - early) * nb - 1) * BLOCK + EXTRA, BLOCK))

    def gather_uppers(owns, others, given, out):
        parts = []
        for k, grad in enumerate(given):
            out[k * BLOCK : (k + 1) * BLOCK, :] = grad[:BLOCK, :].astype(BF)
            parts += split3(grad[BLOCK : BLOCK + 1, :])[:2]
        for c in chunks:
            own = owns[c] if c == chunks[-1] else owns[c].at[0]
            total = own[:BLOCK, :].astype(F32)
            tail = own[BLOCK:, :].astype(F32)
            for other in others:
                total = total + other[c, :BLOCK, :].astype(F32)
                tail = tail + other[c, BLOCK:, :].astype(F32)
            k = len(given) + c
            out[k * BLOCK : (k + 1) * BLOCK, :] = total.astype(BF)
            parts += split3(unpack_line(tail, 0))[:2] + split3(unpack_line(tail, 1))[:2]
        out[-EXTRA:, :] = stack_lines(parts, EXTRA).astype(BF)

    def upper_body(*refs):
        owns, others = refs[:nb], refs[nb : nb + GROUP - 1]
        gather_uppers(owns, others, refs[nb + GROUP - 1 : -1], refs[-1])

    def back_middle(c, s, g, incoming, ending):
        v, other = saves[c][s - 1]

        def body(g_ref, i_ref, v_ref, o_ref, w_ref, trig_ref, g_out, q_out, grad):
            here = cs(trig_ref, s, c)[0]
            spans = [m * quarter for m in range(GROUP)]

            def load(m, r, at):
                return (here * g_ref[at, :].astype(F32) + i_ref[at, :].astype(F32)).astype(BF)

            back(c, s, load, v_ref, o_ref, w_ref, trig_ref, spans, g_out, q_out, grad, ending)

        return call(
            f"backward{s}_chunk{c}",
            body,
            [shape((rows, BLOCK)), shape((rows, BLOCK))]
            + [shape((grad_rows, BLOCK)) if ending else grad_shape],
            [g, incoming, v, other, wb, trig],
            flops=2 * product,
        )

    grads = {c: {} for c in chunks}
    flow = {}
    for c in chunks:
        g, q, grads[c][third] = back_quarters(c, third)
        flow[c] = (g, swapped(q, "dim", 1 << (third - 1 - local_bits)))
    sums, q = lax.optimization_barrier((sums, q))
    arrived = [swapped(sums[m - 1], "dim", m << shift) for m in order[:-1]]
    for s in reversed(middles[1:]):
        for c in chunks:
            ending = s == middles[1] and c == chunks[-1]
            g, incoming = flow[c]
            if ending:
                given = [grads[e][t] for t, e in uppers if (t, e) != (s, c)]
                (upper,) = call("uppers", upper_body, [upper_shape], partial + arrived + given)
                incoming, upper = lax.optimization_barrier((incoming, upper))
            g, q, grads[c][s] = back_middle(c, s, g, incoming, ending)
            flow[c] = (g, swapped(q, "dim", 1 << (s - 1 - local_bits)))
    late = grads[chunks[-1]][middles[1]]
    late_at = uppers.index((middles[1], chunks[-1]))

    def end_body(*refs):
        g_refs, i_refs = refs[:nb], refs[nb : 2 * nb]
        u_ref, w_ref, trig_ref, late_ref, grad, u_held, d_held = refs[2 * nb :]
        ga = [[jnp.zeros((1, BLOCK), F32)] * nb for _ in range(early)]
        w = [[w_ref[s, col(c), :] for c in chunks] for s in range(early)]
        for r in range(0, rows, 2 * tile):
            at = pl.ds(r, 2 * tile)
            steps, u = forward([u_ref[at, col(c)] for c in chunks], w, trig_ref)
            inputs = [u for u, _ in steps] + [u]
            d = []
            for c in chunks:
                here = cs(trig_ref, local_bits, c)[0]
                d.append(
                    (here * g_refs[c][at, :].astype(F32) + i_refs[c][at, :].astype(F32)).astype(BF)
                )
            for s in reversed(range(early)):
                for c in chunks:
                    d_held[s, at, col(c)] = d[c]
                    if s:
                        u_held[s - 1, at, col(c)] = inputs[s][c]
                if s == 0:
                    break
                g = [dot_t(d[c], w[s][c]).astype(BF).astype(F32) for c in chunks]
                t = s - 1
                v = [x.astype(F32) for x in steps[t][1]]
                q = []
                for c in chunks:
                    co, si = cs(trig_ref, t, c)
                    ga[t][c] = ga[t][c] + jnp.sum(
                        g[c] * (co * v[c ^ (1 << t)] - si * v[c]), axis=0, keepdims=True
                    )
                    q.append((si * g[c]).astype(BF).astype(F32))
                d = [
                    (cs(trig_ref, t, c)[0] * g[c] + q[c ^ (1 << t)]).astype(BF) for c in chunks
                ]
        parts = []
        for s in range(early):
            for c in chunks:
                left = u_held[s - 1, :, col(c)] if s else u_ref[:, col(c)]
                k = s * nb + c
                matrix = t_dot(left, d_held[s, :, col(c)])
                grad[k * BLOCK : (k + 1) * BLOCK, :] = matrix.astype(BF)
                parts += split3(ga[s][c])[:2]
        grad[early * nb * BLOCK : (early * nb + 1) * BLOCK, :] = late_ref[:BLOCK, :]
        tail = late_ref[BLOCK:, :].astype(F32)
        parts += [tail[0:1], tail[1:2]]
        grad[-EXTRA:, :] = stack_lines(parts, EXTRA).astype(BF)

    (ends,) = call(
        "end",
        end_body,
        [shape(((early * nb + 1) * BLOCK + EXTRA, BLOCK))],
        [flow[c][0] for c in chunks]
        + [flow[c][1] for c in chunks]
        + [vectors, wb, trig, late],
        scratch=[pltpu.VMEM((local_bits, rows, width), BF), pltpu.VMEM((early, rows, width), BF)],
        flops=6 * product,
    )

    if nrow == 2:
        pairs = [(x, swapped(x, "row", 1)) for x in (ends, upper)]
    else:
        pairs = [lax.psum(x.astype(F32), "row") for x in (ends, upper)]
        pairs = [(p, jnp.zeros_like(p)) for p in pairs]

    def final_body(place_ref, e0, e1, p0, p1, bs_ref, as_ref, step, new, step_a, new_a):
        tails = {
            at: a[-EXTRA:, :].astype(F32) + b[-EXTRA:, :].astype(F32)
            for at, a, b in (("end", e0, e1), ("upper", p0, p1))
        }

        def get(s, c):
            k = s * nb + c
            at, a, b = "end", e0, e1
            if k - early * nb == late_at:
                k = early * nb
            elif s >= early:
                at, a, b = "upper", p0, p1
                k -= early * nb
                k -= k > late_at
            line = k + max(0, k - len(uppers) + 1) if at == "upper" else k
            lines = [line, line + 1] if s == last else [line]
            rows_of = slice(k * BLOCK, (k + 1) * BLOCK)
            matrix = a[rows_of, :].astype(F32) + b[rows_of, :].astype(F32)
            return matrix, [unpack_line(tails[at], line) for line in lines]

        sign = signs(place_ref)
        for c in chunks:
            angle = [None] * sections
            for s in range(sections):
                g, lines = get(s, c)
                state_new = 0.9 * bs_ref[s, col(c), :] + 0.1 * g * g
                new[s, col(c), :] = state_new
                step[s, col(c), :] = g * lax.rsqrt(state_new)
                if s == last:
                    angle[last], angle[third] = lines[0], lines[1]
                elif s >= early:
                    angle[s - 1] = lines[0]
                elif s < local_bits:
                    angle[s] = lines[0]
            g = jnp.concatenate(angle, axis=0) * sign[:, col(c)]
            state_new = 0.9 * as_ref[:, col(c)] + 0.1 * g * g
            new_a[:, col(c)] = state_new
            step_a[:, col(c)] = g * lax.rsqrt(state_new)

    step, new, step_a, new_a = call(
        "final",
        final_body,
        [shape(block_state.shape, F32)] * 2 + [shape(angle_state.shape, F32)] * 2,
        [place_arr, *pairs[0], *pairs[1], block_state, angle_state],
        specs={0: SMEM},
    )
    return step, new, step_a, new_a


def solution(mesh):
    in_specs = (
        P("row", "dim"),
        P(None, "dim", None),
        P(None, "dim"),
        P("row", "dim"),
        P("row"),
        P(),
        P(None, "dim", None),
        P(None, "dim"),
    )
    out_specs = (P(None, "dim", None), P(None, "dim", None), P(None, "dim"), P(None, "dim"))
    return jax.shard_map(local, mesh=mesh, in_specs=in_specs, out_specs=out_specs, check_vma=False)
```
